32 devices in a mesh: row: 8 (over y, x, core), col: 4 (over z).
Axes of the slice: x: 2, y: 2, z: 4, core: 2. Of those that a mesh axis runs over, the one named last changes fastest.
Arguments:
- objects: float32 [4, 4096, 2048], P(None, 'row', 'col'), may hold values from -1 to 1, as said below
- probe: float32 [2, 256, 256], replicated, may hold values from -6 to 6
- kernel: float32 [2, 256, 256], replicated, may hold values from -1 to 1, as said below
- measured: float32 [8, 4, 9, 256, 256], P('row', 'col'), may hold values from 0.3 to 3
- offsets: int32 [8, 4, 9, 2], P('row', 'col'), may hold values from -64 to 320, as said below
Outputs:
- updated: float32 [4, 4096, 2048], P(None, 'row', 'col')
The draws below stay inside these ranges and needn't reach their ends.
Inputs may be any that keep to these rules, and one draw needn't show every extreme that they name: Every window lies inside the object: tiles in the first row or column have offsets of 0 or more there, tiles in the last have offsets of at most 256 there. `objects`: real and imaginary parts of each slice give a magnitude between 0.6 and 1. `kernel`: each entry has magnitude 1.
All inputs are finite; a program needn't handle non-finite values.
Results may differ from the reference program's by a relative error of at most 0.012.
Values sent between devices are 32-bit elements; how exact they have to be, the bound alone decides.
No kernel may reach another device: no remote copies, remote signals or barrier semaphores. Data moves between devices by JAX's collectives and lax.ppermute only.
A program may use at most 128 MiB of HBM per device.

```python
import math
import jax
import jax.numpy as jnp
from jax import lax

W = 256
TILE = 512
HALO = 64
POS = 9
TILES_R = 8
TILES_C = 4
IMG_Y = 4096
IMG_X = 2048


def draw_objects(key, part):
    key_amp = jax.random.fold_in(key, 101)
    key_phase = jax.random.fold_in(key, 202)
    amplitude = jax.random.uniform(key_amp, (2, IMG_Y, IMG_X), jnp.float32, 0.6, 1.0)
    phase = jax.random.uniform(key_phase, (2, IMG_Y, IMG_X), jnp.float32, -1.5, 1.5)
    return jnp.stack([amplitude[0] * jnp.cos(phase[0]), amplitude[0] * jnp.sin(phase[0]), amplitude[1] * jnp.cos(phase[1]), amplitude[1] * jnp.sin(phase[1])])


def draw_kernel(key, part):
    phase = jax.random.uniform(jax.random.fold_in(key, 303), (W, W), jnp.float32, -3.14159, 3.14159)
    return jnp.stack([jnp.cos(phase), jnp.sin(phase)])


def lattice_offset(level, low, high, jitter, span):
    middle = (TILE - W) // 2 + jitter - span // 2
    first = low + jitter
    last = high - jitter
    return jnp.where(level == 0, first, jnp.where(level == 1, middle, last))


def draw_offsets(key, part):
    rows = jnp.arange(TILES_R, dtype=jnp.int32)[:, None, None]
    cols = jnp.arange(TILES_C, dtype=jnp.int32)[None, :, None]
    which = jnp.arange(POS, dtype=jnp.int32)[None, None, :]
    low_r = jnp.where(rows == 0, 0, -HALO)
    high_r = jnp.where(rows == TILES_R - 1, TILE - W, TILE - W + HALO)
    low_c = jnp.where(cols == 0, 0, -HALO)
    high_c = jnp.where(cols == TILES_C - 1, TILE - W, TILE - W + HALO)
    span = HALO // 2
    jitter_y = jax.random.randint(jax.random.fold_in(key, 404), (TILES_R, TILES_C, POS), 0, span)
    jitter_x = jax.random.randint(jax.random.fold_in(key, 505), (TILES_R, TILES_C, POS), 0, span)
    level_y = which // 3
    level_x = which % 3
    offset_y = lattice_offset(level_y, low_r, high_r, jitter_y, span)
    offset_x = lattice_offset(level_x, low_c, high_c, jitter_x, span)
    return jnp.stack([offset_y, offset_x], -1).astype(jnp.int32)


def block_levels(stream_key, shape, shards, least, largest):
    level, own = 1.0, jax.random.fold_in(stream_key, 6)
    for dim, shards_of in shards:
        heights = jnp.exp(jax.random.uniform(jax.random.fold_in(own, dim), (shards_of,), jnp.float32, least / len(shards), largest / len(shards)))
        level = level * jnp.repeat(heights, shape[dim] // shards_of).reshape([-1 if axis == dim else 1 for axis in range(len(shape))])
    return level


def bell_draw(stream_key, extent, scale, limit, held_as=jnp.bfloat16):
    array = jax.random.normal(stream_key, extent, jnp.float32) * scale
    return jnp.minimum(jnp.maximum(array, -limit), limit).astype(held_as)


def setup_inputs(seed: int = 0) -> dict:
    streams_of = jax.random.split(jax.random.key(seed), 6)
    return {
        "objects": draw_objects(jax.random.fold_in(streams_of[5], 71), 0),
        "probe": bell_draw(streams_of[1], (2, W, W), 1.0, 6.0, jnp.float32),
        "kernel": draw_kernel(jax.random.fold_in(streams_of[5], 71), 0),
        "measured": jnp.clip(jnp.exp(math.log(3.0) - 2.3025851 * jax.random.uniform(streams_of[3], (TILES_R, TILES_C, POS, W, W), jnp.float32) ** block_levels(streams_of[3], (TILES_R, TILES_C, POS, W, W), ((0, 8), (1, 4)), -0.2, 0.2)), 0.3, 3.0),
        "offsets": draw_offsets(jax.random.fold_in(streams_of[5], 71), 0),
    }


RATE = 0.5

def make_tables(width):
    index = jnp.arange(width, dtype=jnp.int32)
    product = index[:, None] * index[None, :] % width
    angle = 2.0 * jnp.pi / width * product.astype(jnp.float32)
    norm = 1.0 / jnp.sqrt(jnp.float32(width))
    cosine = jnp.cos(angle) * norm
    sine = jnp.sin(angle) * norm

    def blocks(real_part, imag_part):
        left = jnp.concatenate([jnp.concatenate([real_part, -imag_part], 1), jnp.concatenate([imag_part, real_part], 1)], 0)
        right = jnp.concatenate([jnp.concatenate([real_part, imag_part], 1), jnp.concatenate([-imag_part, real_part], 1)], 0)
        return (left.astype(jnp.bfloat16), right.astype(jnp.bfloat16))
    return (blocks(cosine, -sine), blocks(cosine, sine))

def transform(real_part, imag_part, table):
    left, right = table
    width = real_part.shape[0]
    stacked = jnp.concatenate([real_part, imag_part], 0).astype(jnp.bfloat16)
    first = jnp.dot(left, stacked, preferred_element_type=jnp.float32)
    middle = jnp.concatenate([first[:width], first[width:]], 1).astype(jnp.bfloat16)
    result = jnp.dot(middle, right, preferred_element_type=jnp.float32)
    return (result[:, :width], result[:, width:])

def position_gradient(window, probe, kernel, amplitude, tables):
    forward, inverse = tables
    o1r, o1i, o2r, o2i = (window[0], window[1], window[2], window[3])
    pr, pim = (probe[0], probe[1])
    kr, kim = (kernel[0], kernel[1])
    ar = pr * o1r - pim * o1i
    ai = pr * o1i + pim * o1r
    fr, fi = transform(ar, ai, forward)
    br = kr * fr - kim * fi
    bi = kr * fi + kim * fr
    sr, si = transform(br, bi, inverse)
    er = sr * o2r - si * o2i
    ei = sr * o2i + si * o2r
    zr, zi = transform(er, ei, forward)
    factor = 1.0 - amplitude / jnp.sqrt(zr * zr + zi * zi + 1.0)
    gr, gi = transform(zr * factor, zi * factor, inverse)
    g2r = sr * gr + si * gi
    g2i = sr * gi - si * gr
    hr = o2r * gr + o2i * gi
    hi = o2r * gi - o2i * gr
    ur, ui = transform(hr, hi, forward)
    vr = kr * ur + kim * ui
    vi = kr * ui - kim * ur
    wr, wi = transform(vr, vi, inverse)
    g1r = pr * wr + pim * wi
    g1i = pr * wi - pim * wr
    return jnp.stack([g1r, g1i, g2r, g2i])

def reference(objects, probe, kernel, measured, offsets):
    tables = make_tables(W)
    count = TILES_R * TILES_C * POS
    items = jnp.arange(count, dtype=jnp.int32)
    tile_row = items // (TILES_C * POS)
    tile_col = items // POS % TILES_C
    flat_offsets = offsets.reshape(count, 2)
    anchor_y = (tile_row * TILE + flat_offsets[:, 0]).astype(jnp.int32)
    anchor_x = (tile_col * TILE + flat_offsets[:, 1]).astype(jnp.int32)
    amplitudes = measured.reshape(count, W, W)
    zero = jnp.zeros((), jnp.int32)

    def step(gradient, item):
        top, left, amplitude = item
        window = lax.dynamic_slice(objects, (zero, top, left), (4, W, W))
        piece = position_gradient(window, probe, kernel, amplitude, tables)
        current = lax.dynamic_slice(gradient, (zero, top, left), (4, W, W))
        gradient = lax.dynamic_update_slice(gradient, current + piece, (zero, top, left))
        return (gradient, None)
    gradient, _ = lax.scan(step, jnp.zeros_like(objects), (anchor_y, anchor_x, amplitudes))
    return objects - RATE * gradient
```

```python
import functools
import jax
import jax.numpy as jnp
import numpy as np
from jax import lax
from jax.experimental import pallas as pl
from jax.experimental.pallas import tpu as pltpu
from jax.sharding import PartitionSpec as P

HALO = 64
RATE = 0.5
LANES = 128
ROWS = 8


def make_tables(width):
    half = width // 2
    index = np.arange(width)
    angle = 2.0 * np.pi / width * (index[:, None] * index[None, :] % width)
    cosine = np.cos(angle) / np.sqrt(width)
    sine = np.sin(angle) / np.sqrt(width)

    def block(parity):
        c, s = cosine[parity::2, :half], sine[parity::2, :half]
        return np.block([[c, s], [-s, c]])

    even, odd = block(0), block(1)
    order = np.zeros((width, width))
    order[index[0::2], np.arange(half)] = 1.0
    order[index[1::2], half + np.arange(half)] = 1.0
    return np.stack([even, odd, even.T, odd.T, order]).astype(jnp.bfloat16)


def dot(a, b):
    return jnp.dot(a, b, preferred_element_type=jnp.float32)


def forward(xr, xi, tables):
    half = xr.shape[0] // 2
    le, lo, re, ro = tables[0], tables[1], tables[2], tables[3]
    u = jnp.concatenate([xr[:half] + xr[half:], xi[:half] + xi[half:]], 0)
    v = jnp.concatenate([xr[:half] - xr[half:], xi[:half] - xi[half:]], 0)
    e = dot(le, u.astype(jnp.bfloat16))
    o = dot(lo, v.astype(jnp.bfloat16))

    def fold(parts):
        fr, fi = parts[:half], parts[half:]
        p = jnp.concatenate([fr[:, :half] + fr[:, half:], fi[:, :half] + fi[:, half:]], 1)
        m = jnp.concatenate([fr[:, :half] - fr[:, half:], fi[:, :half] - fi[:, half:]], 1)
        return p.astype(jnp.bfloat16), m.astype(jnp.bfloat16)

    pe, me = fold(e)
    po, mo = fold(o)
    y = dot(jnp.concatenate([pe, po], 0), re)
    z = dot(jnp.concatenate([me, mo], 0), ro)
    return (
        jnp.concatenate([y[:, :half], z[:, :half]], 1),
        jnp.concatenate([y[:, half:], z[:, half:]], 1),
    )


def inverse(xr, xi, tables):
    half = xr.shape[0] // 2
    le, lo, re, ro = tables[2], tables[3], tables[0], tables[1]
    e = dot(le, jnp.concatenate([xr[:half], xi[:half]], 0).astype(jnp.bfloat16))
    o = dot(lo, jnp.concatenate([xr[half:], xi[half:]], 0).astype(jnp.bfloat16))
    p = (e + o).astype(jnp.bfloat16)
    m = (e - o).astype(jnp.bfloat16)

    def pick(cols):
        return jnp.concatenate(
            [
                jnp.concatenate([p[:half, cols], p[half:, cols]], 1),
                jnp.concatenate([m[:half, cols], m[half:, cols]], 1),
            ],
            0,
        )

    y = dot(pick(slice(0, half)), re)
    z = dot(pick(slice(half, 2 * half)), ro)
    s, d = y + z, y - z
    return (
        jnp.concatenate([s[:, :half], d[:, :half]], 1),
        jnp.concatenate([s[:, half:], d[:, half:]], 1),
    )


def reorder(x, order, stage):
    half = x.shape[0] // 2
    high = x.astype(jnp.bfloat16)
    low = (x - high.astype(jnp.float32)).astype(jnp.bfloat16)
    columns = dot(high, order) + dot(low, order)
    parts = []
    for k in range(2):
        stage[k] = columns[:, k * LANES : (k + 1) * LANES]
        parts.append(
            jnp.concatenate([stage[k, pl.ds(0, half, 2), :], stage[k, pl.ds(1, half, 2), :]], 0)
        )
    return jnp.concatenate(parts, 1)


def rolled(x, down, right):
    return pltpu.roll(pltpu.roll(x, down, 0), right, 1)


def masks(down, right):
    sub = lax.broadcasted_iota(jnp.int32, (ROWS, LANES), 0) >= down
    lane = lax.broadcasted_iota(jnp.int32, (1, LANES), 1) >= right
    return sub, lane


def window(ref, channel, row, tile, down, right, width):
    sub, lane = masks(down, right)
    parts = []
    for k in range(3):
        at = ref[channel, tile + k, pl.ds(row, width), :]
        after = ref[channel, tile + k, pl.ds(row + width, ROWS), :]
        parts.append(jnp.concatenate([jnp.where(sub, at[:ROWS], after), at[ROWS:]], 0))
    return jnp.concatenate([jnp.where(lane, parts[0], parts[2]), parts[1]], 1)


def accumulate(ref, channel, row, tile, down, right, value):
    width = value.shape[0]
    sub, lane = masks(down, right)
    first = value[:, :LANES]
    for k, part in enumerate(
        (jnp.where(lane, first, 0.0), value[:, LANES:], jnp.where(lane, 0.0, first))
    ):
        head = part[:ROWS]
        ref[channel, tile + k, pl.ds(row, ROWS), :] += jnp.where(sub, head, 0.0)
        ref[channel, tile + k, pl.ds(row + ROWS, width - ROWS), :] += part[ROWS:]
        ref[channel, tile + k, pl.ds(row + width, ROWS), :] += jnp.where(sub, 0.0, head)


def body(offsets, padded, probe, kernel, measured, tables, gradient, spectrum, stage):
    width = probe.shape[1]
    position = pl.program_id(0)

    @pl.when(position == 0)
    def _():
        gradient[...] = jnp.zeros_like(gradient)
        for part in range(2):
            spectrum[part] = reorder(kernel[part], tables[4], stage)

    top = offsets[position, 0] + HALO
    left = offsets[position, 1] + LANES
    down, right = top % ROWS, left % LANES
    row, tile = pl.multiple_of(top - down, ROWS), left // LANES
    place = (row, tile, down, right)

    pr, pim = rolled(probe[0], down, right), rolled(probe[1], down, right)
    kr, kim = spectrum[0], spectrum[1]
    o1r = window(padded, 0, *place, width)
    o1i = window(padded, 1, *place, width)
    fr, fi = forward(pr * o1r - pim * o1i, pr * o1i + pim * o1r, tables)
    sr, si = inverse(kr * fr - kim * fi, kr * fi + kim * fr, tables)
    o2r = window(padded, 2, *place, width)
    o2i = window(padded, 3, *place, width)
    zr, zi = forward(sr * o2r - si * o2i, sr * o2i + si * o2r, tables)
    amplitude = reorder(measured[0], tables[4], stage)
    factor = 1.0 - amplitude * lax.rsqrt(zr * zr + zi * zi + 1.0)
    gr, gi = inverse(zr * factor, zi * factor, tables)
    accumulate(gradient, 2, *place, sr * gr + si * gi)
    accumulate(gradient, 3, *place, sr * gi - si * gr)
    ur, ui = forward(o2r * gr + o2i * gi, o2r * gi - o2i * gr, tables)
    wr, wi = inverse(kr * ur + kim * ui, kr * ui - kim * ur, tables)
    accumulate(gradient, 0, *place, pr * wr + pim * wi)
    accumulate(gradient, 1, *place, pr * wi - pim * wr)


def gradients(offsets, padded, probe, kernel, measured, tables):
    count, width = measured.shape[0], measured.shape[1]
    whole = pl.BlockSpec(memory_space=pltpu.VMEM)
    return pl.pallas_call(
        body,
        out_shape=jax.ShapeDtypeStruct(padded.shape, jnp.float32),
        grid_spec=pltpu.PrefetchScalarGridSpec(
            num_scalar_prefetch=1,
            grid=(count,),
            in_specs=[
                whole,
                whole,
                whole,
                pl.BlockSpec((1, width, width), lambda i, _: (i, 0, 0)),
                whole,
            ],
            out_specs=whole,
            scratch_shapes=[
                pltpu.VMEM((2, width, width), jnp.float32),
                pltpu.VMEM((2, width, LANES), jnp.float32),
            ],
        ),
        compiler_params=pltpu.CompilerParams(vmem_limit_bytes=56 * 1024 * 1024),
        name="positions",
    )(offsets, padded, probe, kernel, measured, tables)


def padded_2(x, sides, width):
    for axis, dim in sides:
        devices, length = (lax.axis_size(axis), x.shape[dim])
        up = [(i, (i + 1) % devices) for i in range(devices - 1)]
        down = [(j, i) for i, j in up]
        last = lax.slice_in_dim(x, length - width, length, axis=dim)
        initial = lax.slice_in_dim(x, 0, width, axis=dim)
        before = lax.ppermute(last, axis, up)
        after = lax.ppermute(initial, axis, down)
        x = jnp.concatenate([before, x, after], axis=dim)
    return x


def per_device(objects, probe, kernel, measured, offsets):
    tile = objects.shape[1]
    width = probe.shape[1]
    margin = HALO
    extent = tile + 2 * margin
    tables = jnp.asarray(make_tables(width))
    padded = padded_2(objects, (("row", 1), ("col", 2)), margin)
    padded = jnp.pad(padded, ((0, 0), (0, ROWS), (LANES - margin, LANES - margin)))
    tiles = padded.shape[2] // LANES
    padded = padded.reshape(4, extent + ROWS, tiles, LANES).transpose(0, 2, 1, 3)
    gradient = gradients(offsets[0, 0], padded, probe, kernel, measured[0, 0], tables)
    gradient = gradient.transpose(0, 2, 1, 3).reshape(4, extent + ROWS, tiles * LANES)
    gradient = gradient[:, :extent, LANES - margin : LANES - margin + extent]
    cycle = padded_2(gradient, (("row", 1), ("col", 2)), margin)
    inner = gradient[:, margin : margin + tile, margin : margin + tile]
    gap_rows = jnp.zeros((4, tile - 2 * margin, tile), jnp.float32)
    gap_cols = jnp.zeros((4, tile, tile - 2 * margin), jnp.float32)
    gap_corner = jnp.zeros((4, margin, tile - 2 * margin), jnp.float32)
    top = cycle[:, :margin, 2 * margin : 2 * margin + tile]
    bottom = cycle[:, extent + margin :, 2 * margin : 2 * margin + tile]
    left = cycle[:, 2 * margin : 2 * margin + tile, :margin]
    right = cycle[:, 2 * margin : 2 * margin + tile, extent + margin :]
    corner_top = jnp.concatenate(
        [cycle[:, :margin, :margin], gap_corner, cycle[:, :margin, extent + margin :]], 2
    )
    corner_bottom = jnp.concatenate(
        [
            cycle[:, extent + margin :, :margin],
            gap_corner,
            cycle[:, extent + margin :, extent + margin :],
        ],
        2,
    )
    vertical = jnp.concatenate([top + corner_top, gap_rows, bottom + corner_bottom], 1)
    horizontal = jnp.concatenate([left, gap_cols, right], 2)
    total = inner + vertical + horizontal
    return objects - RATE * total


def solution(mesh):
    return jax.shard_map(
        per_device,
        mesh=mesh,
        in_specs=(
            P(None, "row", "col"),
            P(),
            P(),
            P("row", "col", None, None, None),
            P("row", "col", None, None),
        ),
        out_specs=P(None, "row", "col"),
        check_vma=False,
    )
```

```python
import functools
import jax
import jax.numpy as jnp
import numpy as np
from jax import lax
from jax.experimental import pallas as pl
from jax.experimental.pallas import tpu as pltpu
from jax.sharding import PartitionSpec as P

HALO = 64
RATE = 0.5
LANES = 128
ROWS = 8


def make_tables(width):
    half = width // 2
    index = np.arange(width)
    angle = 2.0 * np.pi / width * (index[:, None] * index[None, :] % width)
    cosine = np.cos(angle) / np.sqrt(width)
    sine = np.sin(angle) / np.sqrt(width)

    def block(parity):
        c, s = cosine[parity::2, :half], sine[parity::2, :half]
        return np.block([[c, s], [-s, c]])

    even, odd = block(0), block(1)
    order = np.zeros((width, width))
    order[index[0::2], np.arange(half)] = 1.0
    order[index[1::2], half + np.arange(half)] = 1.0
    return np.stack([even, odd, even.T, odd.T, order]).astype(jnp.bfloat16)


def dot(a, b):
    return jnp.dot(a, b, preferred_element_type=jnp.float32)


def forward(xr, xi, tables):
    half = xr.shape[0] // 2
    le, lo, re, ro = tables[0], tables[1], tables[2], tables[3]
    u = jnp.concatenate([xr[:half] + xr[half:], xi[:half] + xi[half:]], 0)
    v = jnp.concatenate([xr[:half] - xr[half:], xi[:half] - xi[half:]], 0)
    e = dot(le, u.astype(jnp.bfloat16))
    o = dot(lo, v.astype(jnp.bfloat16))

    def fold(parts):
        fr, fi = parts[:half], parts[half:]
        p = jnp.concatenate([fr[:, :half] + fr[:, half:], fi[:, :half] + fi[:, half:]], 1)
        m = jnp.concatenate([fr[:, :half] - fr[:, half:], fi[:, :half] - fi[:, half:]], 1)
        return p.astype(jnp.bfloat16), m.astype(jnp.bfloat16)

    pe, me = fold(e)
    po, mo = fold(o)
    y = dot(jnp.concatenate([pe, po], 0), re)
    z = dot(jnp.concatenate([me, mo], 0), ro)
    return (
        jnp.concatenate([y[:, :half], z[:, :half]], 1),
        jnp.concatenate([y[:, half:], z[:, half:]], 1),
    )


def inverse(xr, xi, tables):
    half = xr.shape[0] // 2
    le, lo, re, ro = tables[2], tables[3], tables[0], tables[1]
    e = dot(le, jnp.concatenate([xr[:half], xi[:half]], 0).astype(jnp.bfloat16))
    o = dot(lo, jnp.concatenate([xr[half:], xi[half:]], 0).astype(jnp.bfloat16))
    p = (e + o).astype(jnp.bfloat16)
    m = (e - o).astype(jnp.bfloat16)

    def pick(cols):
        return jnp.concatenate(
            [
                jnp.concatenate([p[:half, cols], p[half:, cols]], 1),
                jnp.concatenate([m[:half, cols], m[half:, cols]], 1),
            ],
            0,
        )

    y = dot(pick(slice(0, half)), re)
    z = dot(pick(slice(half, 2 * half)), ro)
    s, d = y + z, y - z
    return (
        jnp.concatenate([s[:, :half], d[:, :half]], 1),
        jnp.concatenate([s[:, half:], d[:, half:]], 1),
    )


def reorder(x, order, stage):
    half = x.shape[0] // 2
    high = x.astype(jnp.bfloat16)
    low = (x - high.astype(jnp.float32)).astype(jnp.bfloat16)
    columns = dot(high, order) + dot(low, order)
    parts = []
    for k in range(2):
        stage[k] = columns[:, k * LANES : (k + 1) * LANES]
        parts.append(
            jnp.concatenate([stage[k, pl.ds(0, half, 2), :], stage[k, pl.ds(1, half, 2), :]], 0)
        )
    return jnp.concatenate(parts, 1)


def rolled(x, down, right):
    return pltpu.roll(pltpu.roll(x, down, 0), right, 1)


def masks(down, right):
    sub = lax.broadcasted_iota(jnp.int32, (ROWS, LANES), 0) >= down
    lane = lax.broadcasted_iota(jnp.int32, (1, LANES), 1) >= right
    return sub, lane


def window(ref, channel, row, tile, down, right, width):
    sub, lane = masks(down, right)
    parts = []
    for k in range(3):
        at = ref[channel, tile + k, pl.ds(row, width), :]
        after = ref[channel, tile + k, pl.ds(row + width, ROWS), :]
        parts.append(jnp.concatenate([jnp.where(sub, at[:ROWS], after), at[ROWS:]], 0))
    return jnp.concatenate([jnp.where(lane, parts[0], parts[2]), parts[1]], 1)


def accumulate(ref, channel, row, tile, down, right, value):
    width = value.shape[0]
    sub, lane = masks(down, right)
    first = value[:, :LANES]
    for k, part in enumerate(
        (jnp.where(lane, first, 0.0), value[:, LANES:], jnp.where(lane, 0.0, first))
    ):
        head = part[:ROWS]
        ref[channel, tile + k, pl.ds(row, ROWS), :] += jnp.where(sub, head, 0.0)
        ref[channel, tile + k, pl.ds(row + ROWS, width - ROWS), :] += part[ROWS:]
        ref[channel, tile + k, pl.ds(row + width, ROWS), :] += jnp.where(sub, 0.0, head)


def fold_pair(a, b, low_first):
    lane = lax.broadcasted_iota(jnp.int32, (1, LANES), 1) < HALO
    if low_first:
        return jnp.where(lane, a, pltpu.roll(b, HALO, 1))
    return jnp.where(lane, pltpu.roll(a, HALO, 1), b)


def pack_body(place, left, right, outer, inner, ze, zo, de, do, ro):
    tile = left.shape[1]
    half = ze.shape[1]
    corner = HALO // 2
    even = place[1] == 0
    for ch in range(left.shape[0]):
        strips, corners = [], []
        for ref, lanes, low in (
            (left, slice(0, LANES), True),
            (right, slice(tile - LANES, tile), False),
        ):
            below = jnp.concatenate([ref[ch, half:], inner[ch, :, lanes]], 0)
            strips.append(fold_pair(ref[ch, :half], below, low))
            corners.append(
                fold_pair(outer[ch, :corner, lanes], outer[ch, corner:, lanes], low)
            )
        ze[ch] = jnp.where(even, strips[1], strips[0])
        zo[ch] = jnp.where(even, strips[0], strips[1])
        de[ch] = jnp.where(even, corners[1], corners[0])
        do[ch] = jnp.where(even, corners[0], corners[1])
        ro[ch] = outer[ch]


def pack(place, objects, inner):
    channels, tile = objects.shape[:2]
    half = (tile + HALO) // 2
    last = tile // LANES - 1
    strip = jax.ShapeDtypeStruct((channels, half, LANES), jnp.float32)
    corner = jax.ShapeDtypeStruct((channels, HALO // 2, LANES), jnp.float32)
    whole = pl.BlockSpec(memory_space=pltpu.VMEM)
    return pl.pallas_call(
        pack_body,
        out_shape=(strip, strip, corner, corner, jax.ShapeDtypeStruct(inner.shape, jnp.float32)),
        grid_spec=pltpu.PrefetchScalarGridSpec(
            num_scalar_prefetch=1,
            grid=(1,),
            in_specs=[
                pl.BlockSpec((channels, tile, LANES), lambda i, _: (0, 0, 0)),
                pl.BlockSpec((channels, tile, LANES), lambda i, _: (0, 0, last)),
                pl.BlockSpec(
                    (channels, HALO, tile),
                    lambda i, place: (0, place[0] * (tile // HALO - 1), 0),
                ),
                whole,
            ],
            out_specs=[whole] * 5,
        ),
        compiler_params=pltpu.CompilerParams(vmem_limit_bytes=48 * 1024 * 1024),
        name="pack",
    )(place, objects, objects, objects, inner)


def assemble(place, padded, ze, zo, de, do, re, ro):
    tile = re.shape[2]
    tiles = tile // LANES
    half = ze.shape[1]
    corner = HALO // 2
    even = place[1] == 0
    outer = pl.multiple_of(place[0] * (tile + HALO), HALO)
    inner = pl.multiple_of((1 - place[0]) * (tile + HALO), HALO)
    for ch in range(re.shape[0]):
        for side, at in ((0, 0), (1, tiles + 1)):
            strip = jnp.where(even, (zo, ze)[side][ch], (ze, zo)[side][ch])
            piece = jnp.where(even, (do, de)[side][ch], (de, do)[side][ch])
            turned, turned_piece = pltpu.roll(strip, HALO, 1), pltpu.roll(piece, HALO, 1)
            first, second = (turned, strip) if side == 0 else (strip, turned)
            near, far = (turned_piece, piece) if side == 0 else (piece, turned_piece)
            padded[ch, at, HALO : HALO + half] = first
            padded[ch, at, HALO + half : HALO + tile] = second[: tile - half]
            padded[ch, at, pl.ds(inner, HALO)] = second[tile - half :]
            padded[ch, at, pl.ds(outer, corner)] = near
            padded[ch, at, pl.ds(outer + corner, corner)] = far
        for k in range(tiles):
            padded[ch, k + 1, pl.ds(inner, HALO)] = re[ch, :, k * LANES : (k + 1) * LANES]
            padded[ch, k + 1, pl.ds(outer, HALO)] = ro[ch, :, k * LANES : (k + 1) * LANES]


def finish(place, padded, gradient, updated, ze, zo, de, do, re, ro):
    tile = re.shape[2]
    tiles = tile // LANES
    half = ze.shape[1]
    corner = HALO // 2
    even = place[1] == 0
    outer = pl.multiple_of(place[0] * (tile + HALO), HALO)
    inner = pl.multiple_of((1 - place[0]) * (tile + HALO), HALO)
    for ch in range(re.shape[0]):
        strips, corners = [], []
        for at, low in ((0, False), (tiles + 1, True)):
            first = gradient[ch, at, HALO : HALO + half]
            second = jnp.concatenate(
                [gradient[ch, at, HALO + half : HALO + tile], gradient[ch, at, pl.ds(inner, HALO)]],
                0,
            )
            strips.append(-RATE * fold_pair(first, second, low))
            near = gradient[ch, at, pl.ds(outer, corner)]
            far = gradient[ch, at, pl.ds(outer + corner, corner)]
            corners.append(-RATE * fold_pair(near, far, low))
        ze[ch] = jnp.where(even, strips[1], strips[0])
        zo[ch] = jnp.where(even, strips[0], strips[1])
        de[ch] = jnp.where(even, corners[1], corners[0])
        do[ch] = jnp.where(even, corners[0], corners[1])
        for k in range(tiles):
            lanes = slice(k * LANES, (k + 1) * LANES)
            re[ch, :, lanes] = -RATE * gradient[ch, k + 1, pl.ds(inner, HALO)]
            ro[ch, :, lanes] = -RATE * gradient[ch, k + 1, pl.ds(outer, HALO)]
            updated[ch, :, lanes] = (
                padded[ch, k + 1, HALO : HALO + tile]
                - RATE * gradient[ch, k + 1, HALO : HALO + tile]
            )


def body(
    offsets,
    place,
    objects,
    ze,
    zo,
    de,
    do,
    re,
    ro,
    probe,
    kernel,
    measured,
    tables,
    updated,
    gze,
    gzo,
    gde,
    gdo,
    gre,
    gro,
    padded,
    gradient,
    spectrum,
    stage,
    sems,
):
    width = probe.shape[1]
    tile = re.shape[2]
    position = pl.program_id(0)

    @pl.when(position == 0)
    def _():
        copies = [
            pltpu.make_async_copy(
                objects.at[:, :, pl.ds(k * LANES, LANES)],
                padded.at[:, k + 1, pl.ds(HALO, tile), :],
                sems.at[k],
            )
            for k in range(tile // LANES)
        ]
        for copy in copies:
            copy.start()
        gradient[...] = jnp.zeros_like(gradient)
        for part in range(2):
            spectrum[part] = reorder(kernel[part], tables[4], stage)
        assemble(place, padded, ze, zo, de, do, re, ro)
        for copy in copies:
            copy.wait()

    top = offsets[position, 0] + HALO
    left = offsets[position, 1] + LANES
    down, right = top % ROWS, left % LANES
    row, column = pl.multiple_of(top - down, ROWS), left // LANES
    spot = (row, column, down, right)

    pr, pim = rolled(probe[0], down, right), rolled(probe[1], down, right)
    kr, kim = spectrum[0], spectrum[1]
    o1r = window(padded, 0, *spot, width)
    o1i = window(padded, 1, *spot, width)
    fr, fi = forward(pr * o1r - pim * o1i, pr * o1i + pim * o1r, tables)
    sr, si = inverse(kr * fr - kim * fi, kr * fi + kim * fr, tables)
    o2r = window(padded, 2, *spot, width)
    o2i = window(padded, 3, *spot, width)
    zr, zi = forward(sr * o2r - si * o2i, sr * o2i + si * o2r, tables)
    amplitude = reorder(measured[0], tables[4], stage)
    factor = 1.0 - amplitude * lax.rsqrt(zr * zr + zi * zi + 1.0)
    gr, gi = inverse(zr * factor, zi * factor, tables)
    accumulate(gradient, 2, *spot, sr * gr + si * gi)
    accumulate(gradient, 3, *spot, sr * gi - si * gr)
    ur, ui = forward(o2r * gr + o2i * gi, o2r * gi - o2i * gr, tables)
    wr, wi = inverse(kr * ur + kim * ui, kr * ui - kim * ur, tables)
    accumulate(gradient, 0, *spot, pr * wr + pim * wi)
    accumulate(gradient, 1, *spot, pr * wi - pim * wr)

    @pl.when(position == pl.num_programs(0) - 1)
    def _():
        finish(place, padded, gradient, updated, gze, gzo, gde, gdo, gre, gro)


def step(offsets, place, objects, halo, probe, kernel, measured, tables):
    count, width = measured.shape[0], measured.shape[1]
    channels, tile = objects.shape[:2]
    whole = pl.BlockSpec(memory_space=pltpu.VMEM)
    shapes = [jax.ShapeDtypeStruct(x.shape, jnp.float32) for x in (objects,) + halo]
    extended = (channels, tile // LANES + 2, tile + 2 * HALO + ROWS, LANES)
    return pl.pallas_call(
        body,
        out_shape=shapes,
        grid_spec=pltpu.PrefetchScalarGridSpec(
            num_scalar_prefetch=2,
            grid=(count,),
            in_specs=[pl.BlockSpec(memory_space=pl.ANY)]
            + [whole] * 8
            + [pl.BlockSpec((1, width, width), lambda i, *_: (i, 0, 0)), whole],
            out_specs=[whole] * 7,
            scratch_shapes=[
                pltpu.VMEM(extended, jnp.float32),
                pltpu.VMEM(extended, jnp.float32),
                pltpu.VMEM((2, width, width), jnp.float32),
                pltpu.VMEM((2, width, LANES), jnp.float32),
                pltpu.SemaphoreType.DMA((tile // LANES,)),
            ],
        ),
        compiler_params=pltpu.CompilerParams(vmem_limit_bytes=56 * 1024 * 1024),
        name="positions",
    )(offsets, place, objects, *halo, probe, kernel, measured, tables)


def relay_body(place, re, ze, zo, out):
    tile = re.shape[2]
    even = place[1] == 0
    lane = lax.broadcasted_iota(jnp.int32, (1, LANES), 1) < HALO
    for ch in range(re.shape[0]):
        low = jnp.where(even, zo[ch, -HALO:], ze[ch, -HALO:])
        high = jnp.where(even, ze[ch, -HALO:], zo[ch, -HALO:])
        out[ch, :, :LANES] = re[ch, :, :LANES] + jnp.where(lane, pltpu.roll(low, HALO, 1), 0.0)
        out[ch, :, LANES : tile - LANES] = re[ch, :, LANES : tile - LANES]
        out[ch, :, tile - LANES :] = re[ch, :, tile - LANES :] + jnp.where(lane, 0.0, high)


def relay(place, re, ze, zo):
    whole = pl.BlockSpec(memory_space=pltpu.VMEM)
    return pl.pallas_call(
        relay_body,
        out_shape=jax.ShapeDtypeStruct(re.shape, jnp.float32),
        in_specs=[pl.BlockSpec(memory_space=pltpu.SMEM)] + [whole] * 3,
        out_specs=whole,
        name="relay",
    )(place, re, ze, zo)


def settle_body(place, updated, ze, zo, de, do, re, ro, out):
    tile = re.shape[2]
    half = ze.shape[1]
    corner = HALO // 2
    even = place[1] == 0
    outer = pl.multiple_of(place[0] * (tile - HALO), HALO)
    inner = pl.multiple_of((1 - place[0]) * (tile - HALO), HALO)
    lane = lax.broadcasted_iota(jnp.int32, (1, LANES), 1) < HALO
    out[...] = updated[...]
    out[0, pl.ds(inner, HALO)] += re[0]
    out[0, pl.ds(outer, HALO)] += ro[0]
    for side in range(2):
        lanes = slice(0, LANES) if side == 0 else slice(tile - LANES, tile)
        mask = lane if side == 0 else jnp.logical_not(lane)
        strip = jnp.where(even, (zo, ze)[side][0], (ze, zo)[side][0])
        piece = jnp.where(even, (do, de)[side][0], (de, do)[side][0])
        turned, turned_piece = pltpu.roll(strip, HALO, 1), pltpu.roll(piece, HALO, 1)
        first, second = (strip, turned) if side == 0 else (turned, strip)
        near, far = (piece, turned_piece) if side == 0 else (turned_piece, piece)
        out[0, :half, lanes] += jnp.where(mask, first, 0.0)
        out[0, half:, lanes] += jnp.where(mask, second[: tile - half], 0.0)
        out[0, pl.ds(outer, corner), lanes] += jnp.where(mask, near, 0.0)
        out[0, pl.ds(outer + corner, corner), lanes] += jnp.where(mask, far, 0.0)


def settle(place, updated, shares):
    channels = updated.shape[0]

    def spec(x):
        return pl.BlockSpec((1,) + x.shape[1:], lambda i, _: (i, 0, 0))

    return pl.pallas_call(
        settle_body,
        out_shape=jax.ShapeDtypeStruct(updated.shape, jnp.float32),
        grid_spec=pltpu.PrefetchScalarGridSpec(
            num_scalar_prefetch=1,
            grid=(channels,),
            in_specs=[spec(updated)] + [spec(x) for x in shares],
            out_specs=spec(updated),
        ),
        name="settle",
    )(place, updated, *shares)


def swap(x, row, col):
    rows, cols = lax.axis_size("row"), lax.axis_size("col")

    def partner(i, kind):
        return i + kind * (1 - 2 * (i % 2))

    pairs = [
        (r * cols + c, partner(r, row) * cols + partner(c, col))
        for r in range(rows)
        for c in range(cols)
        if 0 <= partner(r, row) < rows and 0 <= partner(c, col) < cols
    ]
    return lax.ppermute(x, ("row", "col"), pairs)


def exchange(ze, zo, de, do):
    return swap(ze, 0, 1), swap(zo, 0, -1), swap(de, -1, 1), swap(do, -1, -1)


def per_device(objects, probe, kernel, measured, offsets):
    tile = objects.shape[1]
    tables = jnp.asarray(make_tables(probe.shape[1]))
    place = jnp.stack([lax.axis_index("row") % 2, lax.axis_index("col") % 2]).astype(jnp.int32)
    rows = lax.dynamic_slice_in_dim(objects, (1 - place[0]) * (tile - HALO), HALO, axis=1)
    re = swap(rows, 1, 0)
    *sides, ro = pack(place, objects, re)
    halo = (*exchange(*sides), re, swap(ro, -1, 0))
    updated, *sides, gre, gro = step(
        offsets[0, 0], place, objects, halo, probe, kernel, measured[0, 0], tables
    )
    ze, zo, de, do = exchange(*sides)
    ro = swap(gro, -1, 0)
    re = swap(relay(place, gre, ze, zo), 1, 0)
    return settle(place, updated, (ze, zo, de, do, re, ro))


def solution(mesh):
    return jax.shard_map(
        per_device,
        mesh=mesh,
        in_specs=(
            P(None, "row", "col"),
            P(),
            P(),
            P("row", "col", None, None, None),
            P("row", "col", None, None),
        ),
        out_specs=P(None, "row", "col"),
        check_vma=False,
    )
```

```python
import itertools
import jax
import jax.numpy as jnp
import numpy as np
from jax import lax
from jax.experimental import pallas as pl
from jax.experimental.pallas import tpu as pltpu
from jax.sharding import PartitionSpec as P

HALO = 64
RATE = 0.5
LANES = 128
ROWS = 8
GROUPS = (3, 2, 1)
VMEM = 24 * 1024 * 1024


def make_tables(width):
    half = width // 2
    index = np.arange(width)
    angle = 2.0 * np.pi / width * (index[:, None] * index[None, :] % width)
    cosine = np.cos(angle) / np.sqrt(width)
    sine = np.sin(angle) / np.sqrt(width)

    def block(parity):
        c, s = cosine[parity::2, :half], sine[parity::2, :half]
        return np.block([[c, s], [-s, c]])

    even, odd = block(0), block(1)
    order = np.zeros((width, width))
    order[index[0::2], np.arange(half)] = 1.0
    order[index[1::2], half + np.arange(half)] = 1.0
    return np.stack([even, odd, even.T, odd.T, order, RATE * order]).astype(jnp.bfloat16)


def dot(a, b):
    return jnp.dot(a, b, preferred_element_type=jnp.float32)


def forward(xr, xi, tables):
    half = xr.shape[0] // 2
    le, lo, re, ro = tables[0], tables[1], tables[2], tables[3]
    u = jnp.concatenate([xr[:half] + xr[half:], xi[:half] + xi[half:]], 0)
    v = jnp.concatenate([xr[:half] - xr[half:], xi[:half] - xi[half:]], 0)
    e = dot(le, u.astype(jnp.bfloat16))
    o = dot(lo, v.astype(jnp.bfloat16))
    yield

    def fold(parts):
        fr, fi = parts[:half], parts[half:]
        p = jnp.concatenate([fr[:, :half] + fr[:, half:], fi[:, :half] + fi[:, half:]], 1)
        m = jnp.concatenate([fr[:, :half] - fr[:, half:], fi[:, :half] - fi[:, half:]], 1)
        return p.astype(jnp.bfloat16), m.astype(jnp.bfloat16)

    pe, me = fold(e)
    po, mo = fold(o)
    y = dot(jnp.concatenate([pe, po], 0), re)
    z = dot(jnp.concatenate([me, mo], 0), ro)
    yield
    return (
        jnp.concatenate([y[:, :half], z[:, :half]], 1),
        jnp.concatenate([y[:, half:], z[:, half:]], 1),
    )


def inverse(xr, xi, tables):
    half = xr.shape[0] // 2
    le, lo, re, ro = tables[2], tables[3], tables[0], tables[1]
    e = dot(le, jnp.concatenate([xr[:half], xi[:half]], 0).astype(jnp.bfloat16))
    o = dot(lo, jnp.concatenate([xr[half:], xi[half:]], 0).astype(jnp.bfloat16))
    yield
    p = (e + o).astype(jnp.bfloat16)
    m = (e - o).astype(jnp.bfloat16)

    def pick(cols):
        return jnp.concatenate(
            [
                jnp.concatenate([p[:half, cols], p[half:, cols]], 1),
                jnp.concatenate([m[:half, cols], m[half:, cols]], 1),
            ],
            0,
        )

    y = dot(pick(slice(0, half)), re)
    z = dot(pick(slice(half, 2 * half)), ro)
    yield
    s, d = y + z, y - z
    return (
        jnp.concatenate([s[:, :half], d[:, :half]], 1),
        jnp.concatenate([s[:, half:], d[:, half:]], 1),
    )


def reorder(x, order, stage):
    half = x.shape[0] // 2
    high = x.astype(jnp.bfloat16)
    low = (x - high.astype(jnp.float32)).astype(jnp.bfloat16)
    columns = dot(high, order) + dot(low, order)
    parts = []
    for k in range(2):
        stage[k] = columns[:, k * LANES : (k + 1) * LANES]
        parts.append(
            jnp.concatenate([stage[k, pl.ds(0, half, 2), :], stage[k, pl.ds(1, half, 2), :]], 0)
        )
    return jnp.concatenate(parts, 1)


def rolled(x, down, right):
    return pltpu.roll(pltpu.roll(x, down, 0), right, 1)


def masks(down, right):
    sub = lax.broadcasted_iota(jnp.int32, (ROWS, LANES), 0) >= down
    lane = lax.broadcasted_iota(jnp.int32, (1, LANES), 1) >= right
    return sub, lane


def window(ref, channel, row, tile, down, right, width):
    sub, lane = masks(down, right)
    parts = []
    for k in range(3):
        at = ref[channel, tile + k, pl.ds(row, width), :]
        after = ref[channel, tile + k, pl.ds(row + width, ROWS), :]
        parts.append(jnp.concatenate([jnp.where(sub, at[:ROWS], after), at[ROWS:]], 0))
    return jnp.concatenate([jnp.where(lane, parts[0], parts[2]), parts[1]], 1)


def accumulate(ref, channel, row, tile, down, right, value):
    width = value.shape[0]
    sub, lane = masks(down, right)
    first = value[:, :LANES]
    for k, part in enumerate(
        (jnp.where(lane, first, 0.0), value[:, LANES:], jnp.where(lane, 0.0, first))
    ):
        head = part[:ROWS]
        ref[channel, tile + k, pl.ds(row, ROWS), :] += jnp.where(sub, head, 0.0)
        ref[channel, tile + k, pl.ds(row + ROWS, width - ROWS), :] += part[ROWS:]
        ref[channel, tile + k, pl.ds(row + width, ROWS), :] += jnp.where(sub, 0.0, head)


def fold_pair(a, b, low_first):
    lane = lax.broadcasted_iota(jnp.int32, (1, LANES), 1) < HALO
    if low_first:
        return jnp.where(lane, a, pltpu.roll(b, HALO, 1))
    return jnp.where(lane, pltpu.roll(a, HALO, 1), b)


def pack_body(place, left, right, outer, inner, ze, zo, de, do):
    tile = left.shape[1]
    half = ze.shape[1]
    corner = HALO // 2
    even = place[1] == 0
    for ch in range(left.shape[0]):
        strips, corners = [], []
        for ref, lanes, low in (
            (left, slice(0, LANES), True),
            (right, slice(tile - LANES, tile), False),
        ):
            below = jnp.concatenate([ref[ch, half:], inner[ch, :, lanes]], 0)
            strips.append(fold_pair(ref[ch, :half], below, low))
            corners.append(
                fold_pair(outer[ch, :corner, lanes], outer[ch, corner:, lanes], low)
            )
        ze[ch] = jnp.where(even, strips[1], strips[0])
        zo[ch] = jnp.where(even, strips[0], strips[1])
        de[ch] = jnp.where(even, corners[1], corners[0])
        do[ch] = jnp.where(even, corners[0], corners[1])


def pack(place, objects, inner):
    channels, tile = objects.shape[:2]
    half = (tile + HALO) // 2
    last = tile // LANES - 1
    strip = jax.ShapeDtypeStruct((channels, half, LANES), jnp.float32)
    corner = jax.ShapeDtypeStruct((channels, HALO // 2, LANES), jnp.float32)
    whole = pl.BlockSpec(memory_space=pltpu.VMEM)
    return pl.pallas_call(
        pack_body,
        out_shape=(strip, strip, corner, corner),
        grid_spec=pltpu.PrefetchScalarGridSpec(
            num_scalar_prefetch=1,
            grid=(1,),
            in_specs=[
                pl.BlockSpec((channels, tile, LANES), lambda i, _: (0, 0, 0)),
                pl.BlockSpec((channels, tile, LANES), lambda i, _: (0, 0, last)),
                pl.BlockSpec(
                    (channels, HALO, tile),
                    lambda i, place: (0, place[0] * (tile // HALO - 1), 0),
                ),
                whole,
            ],
            out_specs=[whole] * 4,
        ),
        compiler_params=pltpu.CompilerParams(vmem_limit_bytes=VMEM),
        name="pack",
    )(place, objects, objects, objects, inner)


def chain(top, left, padded, probe, spectrum, measured, tables, gradient, stage):
    width = probe.shape[1]
    down, right = top % ROWS, left % LANES
    row, column = pl.multiple_of(top - down, ROWS), left // LANES
    spot = (row, column, down, right)
    pr, pim = rolled(probe[0], down, right), rolled(probe[1], down, right)
    kr, kim = spectrum[0], spectrum[1]
    o1r = window(padded, 0, *spot, width)
    o1i = window(padded, 1, *spot, width)
    fr, fi = yield from forward(pr * o1r - pim * o1i, pr * o1i + pim * o1r, tables)
    sr, si = yield from inverse(kr * fr - kim * fi, kr * fi + kim * fr, tables)
    o2r = window(padded, 2, *spot, width)
    o2i = window(padded, 3, *spot, width)
    zr, zi = yield from forward(sr * o2r - si * o2i, sr * o2i + si * o2r, tables)
    amplitude = reorder(measured[...], tables[5], stage)
    factor = amplitude * lax.rsqrt(zr * zr + zi * zi + 1.0) - RATE
    gr, gi = yield from inverse(zr * factor, zi * factor, tables)
    accumulate(gradient, 2, *spot, sr * gr + si * gi)
    accumulate(gradient, 3, *spot, sr * gi - si * gr)
    ur, ui = yield from forward(o2r * gr + o2i * gi, o2r * gi - o2i * gr, tables)
    wr, wi = yield from inverse(kr * ur + kim * ui, kr * ui - kim * ur, tables)
    accumulate(gradient, 0, *spot, pr * wr + pim * wi)
    accumulate(gradient, 1, *spot, pr * wi - pim * wr)


def rows_of(place, tile):
    outer = pl.multiple_of(place[0] * (tile + HALO), HALO)
    inner = pl.multiple_of((1 - place[0]) * (tile + HALO), HALO)
    return outer, inner


def assemble(place, padded, ze, zo, de, do, tile):
    half = ze.shape[1]
    corner = HALO // 2
    even = place[1] == 0
    outer, inner = rows_of(place, tile)
    for ch in range(ze.shape[0]):
        for side, at in ((0, 0), (1, padded.shape[1] - 1)):
            strip = jnp.where(even, (zo, ze)[side][ch], (ze, zo)[side][ch])
            piece = jnp.where(even, (do, de)[side][ch], (de, do)[side][ch])
            turned, turned_piece = pltpu.roll(strip, HALO, 1), pltpu.roll(piece, HALO, 1)
            first, second = (turned, strip) if side == 0 else (strip, turned)
            near, far = (turned_piece, piece) if side == 0 else (piece, turned_piece)
            padded[ch, at, HALO : HALO + half] = first
            padded[ch, at, HALO + half : HALO + tile] = second[: tile - half]
            padded[ch, at, pl.ds(inner, HALO)] = second[tile - half :]
            padded[ch, at, pl.ds(outer, corner)] = near
            padded[ch, at, pl.ds(outer + corner, corner)] = far


def harvest(place, gradient, ze, zo, de, do, re, ro):
    tile = re.shape[2]
    tiles = tile // LANES
    half = ze.shape[1]
    corner = HALO // 2
    even = place[1] == 0
    outer, inner = rows_of(place, tile)
    for ch in range(re.shape[0]):
        strips, corners = [], []
        for at, low in ((0, False), (tiles + 1, True)):
            first = gradient[ch, at, HALO : HALO + half]
            second = jnp.concatenate(
                [gradient[ch, at, HALO + half : HALO + tile], gradient[ch, at, pl.ds(inner, HALO)]],
                0,
            )
            strips.append(fold_pair(first, second, low))
            near = gradient[ch, at, pl.ds(outer, corner)]
            far = gradient[ch, at, pl.ds(outer + corner, corner)]
            corners.append(fold_pair(near, far, low))
        ze[ch] = jnp.where(even, strips[1], strips[0])
        zo[ch] = jnp.where(even, strips[0], strips[1])
        de[ch] = jnp.where(even, corners[1], corners[0])
        do[ch] = jnp.where(even, corners[0], corners[1])
        for k in range(tiles):
            lanes = slice(k * LANES, (k + 1) * LANES)
            re[ch, :, lanes] = gradient[ch, k + 1, pl.ds(inner, HALO)]
            ro[ch, :, lanes] = gradient[ch, k + 1, pl.ds(outer, HALO)]


def sort_positions(offsets, order, inside):
    count = offsets.shape[0]
    needs = [(offsets[i, 1] >= 0) & (offsets[i, 1] <= inside) for i in range(count)]
    at = jnp.int32(0)
    for i in range(count):
        order[at] = i
        at += needs[i].astype(jnp.int32)
    first = at
    for i in range(count):
        order[at] = i
        at += 1 - needs[i].astype(jnp.int32)
    return first


def run_groups(begin, end, group, offsets, order, padded, probe, spectrum, measured, tables, gradient, stage):
    def one(g, carry):
        chains = []
        for k in range(group):
            which = order[g * group + k]
            chains.append(
                chain(
                    offsets[which, 0] + HALO,
                    offsets[which, 1] + LANES,
                    padded,
                    probe,
                    spectrum,
                    measured.at[which],
                    tables,
                    gradient,
                    stage.at[k],
                )
            )
        for _ in itertools.zip_longest(*chains):
            pass
        return carry

    lax.fori_loop(begin, end, one, 0)


def early_body(
    offsets, place, objects, re, ro, probe, kernel, measured, tables,
    padded, gradient, spectrum, order, stage, sems,
):
    tile, width = re.shape[2], probe.shape[1]
    tiles = tile // LANES
    outer, inner = rows_of(place, tile)
    copies = [
        pltpu.make_async_copy(
            objects.at[:, :, pl.ds(k * LANES, LANES)],
            target.at[:, k + 1, pl.ds(HALO, tile), :],
            sems.at[n, k],
        )
        for n, target in enumerate((padded, gradient))
        for k in range(tiles)
    ]
    for copy in copies:
        copy.start()
    first = sort_positions(offsets, order, tile - width)
    for part in range(2):
        spectrum[part] = reorder(kernel[part], tables[4], stage.at[0])
    bottom = gradient.shape[2] - HALO - tile
    for ch in range(gradient.shape[0]):
        for at in (0, tiles + 1):
            gradient[ch, at] = jnp.zeros(gradient.shape[2:], jnp.float32)
        for k in range(tiles):
            gradient[ch, k + 1, :HALO] = jnp.zeros((HALO, LANES), jnp.float32)
            gradient[ch, k + 1, HALO + tile :] = jnp.zeros((bottom, LANES), jnp.float32)
            lanes = slice(k * LANES, (k + 1) * LANES)
            padded[ch, k + 1, pl.ds(inner, HALO)] = re[ch, :, lanes]
            padded[ch, k + 1, pl.ds(outer, HALO)] = ro[ch, :, lanes]
    for copy in copies:
        copy.wait()
    group = stage.shape[0]
    run_groups(
        0, first // group, group, offsets, order,
        padded, probe, spectrum, measured, tables, gradient, stage,
    )


def late_body(
    offsets, place, padded_in, gradient_in, ze, zo, de, do, probe, spectrum, measured, tables,
    padded, gradient, gze, gzo, gde, gdo, gre, gro, order, stage,
):
    tile, width = gre.shape[2], probe.shape[1]
    first = sort_positions(offsets, order, tile - width)
    assemble(place, padded, ze, zo, de, do, tile)
    group = stage.shape[0]
    run_groups(
        first // group, offsets.shape[0] // group, group, offsets, order,
        padded, probe, spectrum, measured, tables, gradient, stage,
    )
    harvest(place, gradient, gze, gzo, gde, gdo, gre, gro)


WHOLE = pl.BlockSpec(memory_space=pltpu.VMEM)
SCALARS = pl.BlockSpec(memory_space=pltpu.SMEM)


def scratch(count, width):
    group = next(k for k in GROUPS if count % k == 0)
    return [
        pltpu.SMEM((count + 1,), jnp.int32),
        pltpu.VMEM((group, 2, width, LANES), jnp.float32),
    ]


def cost(positions, width):
    return pl.CostEstimate(
        flops=positions * 6 * 8 * width**3, bytes_accessed=positions * 4 * width * width, transcendentals=0
    )


def early(offsets, place, objects, re, ro, probe, kernel, measured, tables):
    count, width = measured.shape[0], measured.shape[1]
    channels, tile = objects.shape[:2]
    extended = (channels, tile // LANES + 2, tile + 2 * HALO + ROWS, LANES)
    return pl.pallas_call(
        early_body,
        out_shape=[
            jax.ShapeDtypeStruct(extended, jnp.float32),
            jax.ShapeDtypeStruct(extended, jnp.float32),
            jax.ShapeDtypeStruct(kernel.shape, jnp.float32),
        ],
        in_specs=[SCALARS, SCALARS, pl.BlockSpec(memory_space=pl.ANY)] + [WHOLE] * 6,
        out_specs=[WHOLE] * 3,
        scratch_shapes=scratch(count, width) + [pltpu.SemaphoreType.DMA((2, tile // LANES))],
        compiler_params=pltpu.CompilerParams(vmem_limit_bytes=VMEM),
        cost_estimate=cost(count, width),
        name="early",
    )(offsets, place, objects, re, ro, probe, kernel, measured, tables)


def late(offsets, place, padded, gradient, sides, rows, probe, spectrum, measured, tables):
    count, width = measured.shape[0], measured.shape[1]
    shapes = (padded, gradient) + tuple(sides) + (rows, rows)
    return pl.pallas_call(
        late_body,
        out_shape=[jax.ShapeDtypeStruct(x.shape, jnp.float32) for x in shapes],
        in_specs=[SCALARS, SCALARS] + [WHOLE] * 10,
        out_specs=[WHOLE] * 8,
        scratch_shapes=scratch(count, width),
        input_output_aliases={2: 0, 3: 1},
        compiler_params=pltpu.CompilerParams(vmem_limit_bytes=VMEM),
        cost_estimate=cost(count, width),
        name="late",
    )(offsets, place, padded, gradient, *sides, probe, spectrum, measured, tables)


def relay_body(place, ze, zo, out):
    even = place[1] == 0
    lane = lax.broadcasted_iota(jnp.int32, (1, LANES), 1) < HALO
    for ch in range(out.shape[0]):
        low = jnp.where(even, zo[ch, -HALO:], ze[ch, -HALO:])
        high = jnp.where(even, ze[ch, -HALO:], zo[ch, -HALO:])
        out[ch] = jnp.where(lane, pltpu.roll(low, HALO, 1), high)


def relay(place, ze, zo):
    channels, half = ze.shape[:2]
    return pl.pallas_call(
        relay_body,
        out_shape=jax.ShapeDtypeStruct((channels, HALO, LANES), jnp.float32),
        in_specs=[SCALARS, WHOLE, WHOLE],
        out_specs=WHOLE,
        name="relay",
    )(place, ze, zo)


def settle_body(place, gradient_in, ze, zo, de, do, re, ro, ce, gradient, out, sems):
    tile = re.shape[2]
    tiles = tile // LANES
    half = ze.shape[1]
    corner = HALO // 2
    even = place[1] == 0
    outer = pl.multiple_of(HALO + place[0] * (tile - HALO), HALO)
    inner = pl.multiple_of(HALO + (1 - place[0]) * (tile - HALO), HALO)
    lane = lax.broadcasted_iota(jnp.int32, (1, LANES), 1) < HALO

    def copy(k):
        return pltpu.make_async_copy(
            gradient.at[:, k + 1, pl.ds(HALO, tile), :],
            out.at[:, :, pl.ds(k * LANES, LANES)],
            sems.at[k],
        )

    for k in list(range(1, tiles - 1)) + [0, tiles - 1]:
        for ch in range(re.shape[0]):
            lanes = slice(k * LANES, (k + 1) * LANES)
            gradient[ch, k + 1, pl.ds(inner, HALO)] += re[ch, :, lanes]
            gradient[ch, k + 1, pl.ds(outer, HALO)] += ro[ch, :, lanes]
        for side in range(2):
            if k != (0, tiles - 1)[side]:
                continue
            mask = lane if side == 0 else jnp.logical_not(lane)
            for ch in range(re.shape[0]):
                strip = jnp.where(even, (zo, ze)[side][ch], (ze, zo)[side][ch])
                piece = jnp.where(even, (do, de)[side][ch], (de, do)[side][ch])
                turned, turned_piece = pltpu.roll(strip, HALO, 1), pltpu.roll(piece, HALO, 1)
                first, second = (strip, turned) if side == 0 else (turned, strip)
                near, far = (piece, turned_piece) if side == 0 else (turned_piece, piece)
                gradient[ch, k + 1, HALO : HALO + half] += jnp.where(mask, first, 0.0)
                gradient[ch, k + 1, HALO + half : HALO + tile] += jnp.where(
                    mask, second[: tile - half], 0.0
                )
                gradient[ch, k + 1, pl.ds(outer, corner)] += jnp.where(mask, near, 0.0)
                gradient[ch, k + 1, pl.ds(outer + corner, corner)] += jnp.where(mask, far, 0.0)
                gradient[ch, k + 1, pl.ds(inner, HALO)] += jnp.where(mask, ce[ch], 0.0)
        copy(k).start()
    for k in range(tiles):
        copy(k).wait()


def settle(place, gradient, shares, tile):
    channels = gradient.shape[0]
    return pl.pallas_call(
        settle_body,
        out_shape=[
            jax.ShapeDtypeStruct(gradient.shape, jnp.float32),
            jax.ShapeDtypeStruct((channels, tile, tile), jnp.float32),
        ],
        in_specs=[SCALARS] + [WHOLE] * 8,
        out_specs=[WHOLE, pl.BlockSpec(memory_space=pl.ANY)],
        input_output_aliases={1: 0},
        scratch_shapes=[pltpu.SemaphoreType.DMA((tile // LANES,))],
        compiler_params=pltpu.CompilerParams(vmem_limit_bytes=VMEM),
        name="settle",
    )(place, gradient, *shares)[1]


def swap(x, row, col):
    rows, cols = lax.axis_size("row"), lax.axis_size("col")

    def partner(i, kind):
        return i + kind * (1 - 2 * (i % 2))

    pairs = [
        (r * cols + c, partner(r, row) * cols + partner(c, col))
        for r in range(rows)
        for c in range(cols)
        if 0 <= partner(r, row) < rows and 0 <= partner(c, col) < cols
    ]
    return lax.ppermute(x, ("row", "col"), pairs)


def exchange(ze, zo, de, do):
    return swap(ze, 0, 1), swap(zo, 0, -1), swap(de, -1, 1), swap(do, -1, -1)


def per_device(objects, probe, kernel, measured, offsets):
    tile = objects.shape[1]
    tables = jnp.asarray(make_tables(probe.shape[1]))
    place = jnp.stack([lax.axis_index("row") % 2, lax.axis_index("col") % 2]).astype(jnp.int32)
    offsets, measured = offsets[0, 0], measured[0, 0]
    rows = [
        lax.dynamic_slice_in_dim(objects, at * (tile - HALO), HALO, axis=1)
        for at in (place[0], 1 - place[0])
    ]
    ro = swap(rows[0], -1, 0)
    re = swap(rows[1], 1, 0)
    sides = exchange(*pack(place, objects, re))
    padded, gradient, spectrum = early(
        offsets, place, objects, re, ro, probe, kernel, measured, tables
    )
    _, gradient, *sides, gre, gro = late(
        offsets, place, padded, gradient, sides, re, probe, spectrum, measured, tables
    )
    re, ro = swap(gre, 1, 0), swap(gro, -1, 0)
    ze, zo, de, do = exchange(*sides)
    ze, zo, de, do, re, ro = lax.optimization_barrier((ze, zo, de, do, re, ro))
    ce = swap(relay(place, ze, zo), 1, 0)
    return settle(place, gradient, (ze, zo, de, do, re, ro, ce), tile)


def solution(mesh):
    return jax.shard_map(
        per_device,
        mesh=mesh,
        in_specs=(
            P(None, "row", "col"),
            P(),
            P(),
            P("row", "col", None, None, None),
            P("row", "col", None, None),
        ),
        out_specs=P(None, "row", "col"),
        check_vma=False,
    )
```

```python
import itertools
import jax
import jax.numpy as jnp
import numpy as np
from jax import lax
from jax.experimental import pallas as pl
from jax.experimental.pallas import tpu as pltpu
from jax.sharding import PartitionSpec as P

HALO = 64
RATE = 0.5
LANES = 128
ROWS = 8
GROUPS = (3, 2, 1)
VMEM = 24 * 1024 * 1024
SMALL = 12 * 1024 * 1024
LARGE = 58 * 1024 * 1024
WHOLE = pl.BlockSpec(memory_space=pltpu.VMEM)
SCALARS = pl.BlockSpec(memory_space=pltpu.SMEM)


def make_tables(width):
    half = width // 2
    index = np.arange(width)
    angle = 2.0 * np.pi / width * (index[:, None] * index[None, :] % width)
    cosine = np.cos(angle) / np.sqrt(width)
    sine = np.sin(angle) / np.sqrt(width)

    def block(parity):
        c, s = cosine[parity::2, :half], sine[parity::2, :half]
        return np.block([[c, s], [-s, c]])

    even, odd = block(0), block(1)
    order = np.zeros((width, width))
    order[index[0::2], np.arange(half)] = 1.0
    order[index[1::2], half + np.arange(half)] = 1.0
    return np.stack([even, odd, even.T, odd.T, order, RATE * order]).astype(jnp.bfloat16)


def dot(a, b):
    return jnp.dot(a, b, preferred_element_type=jnp.float32)


def forward(xr, xi, tables):
    half = xr.shape[0] // 2
    le, lo, re, ro = tables[0], tables[1], tables[2], tables[3]
    u = jnp.concatenate([xr[:half] + xr[half:], xi[:half] + xi[half:]], 0)
    v = jnp.concatenate([xr[:half] - xr[half:], xi[:half] - xi[half:]], 0)
    e = dot(le, u.astype(jnp.bfloat16))
    o = dot(lo, v.astype(jnp.bfloat16))
    yield

    def fold(parts):
        fr, fi = parts[:half], parts[half:]
        p = jnp.concatenate([fr[:, :half] + fr[:, half:], fi[:, :half] + fi[:, half:]], 1)
        m = jnp.concatenate([fr[:, :half] - fr[:, half:], fi[:, :half] - fi[:, half:]], 1)
        return p.astype(jnp.bfloat16), m.astype(jnp.bfloat16)

    pe, me = fold(e)
    po, mo = fold(o)
    y = dot(jnp.concatenate([pe, po], 0), re)
    z = dot(jnp.concatenate([me, mo], 0), ro)
    yield
    return (
        jnp.concatenate([y[:, :half], z[:, :half]], 1),
        jnp.concatenate([y[:, half:], z[:, half:]], 1),
    )


def inverse(xr, xi, tables):
    half = xr.shape[0] // 2
    le, lo, re, ro = tables[2], tables[3], tables[0], tables[1]
    e = dot(le, jnp.concatenate([xr[:half], xi[:half]], 0).astype(jnp.bfloat16))
    o = dot(lo, jnp.concatenate([xr[half:], xi[half:]], 0).astype(jnp.bfloat16))
    yield
    p = (e + o).astype(jnp.bfloat16)
    m = (e - o).astype(jnp.bfloat16)

    def pick(cols):
        return jnp.concatenate(
            [
                jnp.concatenate([p[:half, cols], p[half:, cols]], 1),
                jnp.concatenate([m[:half, cols], m[half:, cols]], 1),
            ],
            0,
        )

    y = dot(pick(slice(0, half)), re)
    z = dot(pick(slice(half, 2 * half)), ro)
    yield
    s, d = y + z, y - z
    return (
        jnp.concatenate([s[:, :half], d[:, :half]], 1),
        jnp.concatenate([s[:, half:], d[:, half:]], 1),
    )


def reorder(x, order, stage):
    half = x.shape[0] // 2
    high = x.astype(jnp.bfloat16)
    low = (x - high.astype(jnp.float32)).astype(jnp.bfloat16)
    columns = dot(high, order) + dot(low, order)
    parts = []
    for k in range(2):
        stage[k] = columns[:, k * LANES : (k + 1) * LANES]
        parts.append(
            jnp.concatenate([stage[k, pl.ds(0, half, 2), :], stage[k, pl.ds(1, half, 2), :]], 0)
        )
    return jnp.concatenate(parts, 1)


def rolled(x, down, right):
    return pltpu.roll(pltpu.roll(x, down, 0), right, 1)


def masks(down, right):
    sub = lax.broadcasted_iota(jnp.int32, (ROWS, LANES), 0) >= down
    lane = lax.broadcasted_iota(jnp.int32, (1, LANES), 1) >= right
    return sub, lane


def window(ref, channel, row, tile, down, right, width):
    sub, lane = masks(down, right)
    parts = []
    for k in range(3):
        at = ref[channel, tile + k, pl.ds(row, width), :]
        after = ref[channel, tile + k, pl.ds(row + width, ROWS), :]
        parts.append(jnp.concatenate([jnp.where(sub, at[:ROWS], after), at[ROWS:]], 0))
    return jnp.concatenate([jnp.where(lane, parts[0], parts[2]), parts[1]], 1)


def accumulate(ref, channel, row, tile, down, right, value):
    width = value.shape[0]
    sub, lane = masks(down, right)
    first = value[:, :LANES]
    for k, part in enumerate(
        (jnp.where(lane, first, 0.0), value[:, LANES:], jnp.where(lane, 0.0, first))
    ):
        head = part[:ROWS]
        ref[channel, tile + k, pl.ds(row, ROWS), :] += jnp.where(sub, head, 0.0)
        ref[channel, tile + k, pl.ds(row + ROWS, width - ROWS), :] += part[ROWS:]
        ref[channel, tile + k, pl.ds(row + width, ROWS), :] += jnp.where(sub, 0.0, head)


def fold_pair(a, b, low_first):
    lane = lax.broadcasted_iota(jnp.int32, (1, LANES), 1) < HALO
    if low_first:
        return jnp.where(lane, a, pltpu.roll(b, HALO, 1))
    return jnp.where(lane, pltpu.roll(a, HALO, 1), b)


def pack_body(place, objects, ze, zo, re, ro, left, right, sems):
    tile = objects.shape[2]
    half = ze.shape[1]
    even = place[1] == 0
    outer = pl.multiple_of(place[0] * (tile - HALO), HALO)
    inner = pl.multiple_of((1 - place[0]) * (tile - HALO), HALO)
    copies = [
        pltpu.make_async_copy(source, target, sems.at[n])
        for n, (source, target) in enumerate(
            (
                (objects.at[:, :, pl.ds(0, LANES)], left),
                (objects.at[:, :, pl.ds(tile - LANES, LANES)], right),
                (objects.at[:, pl.ds(outer, HALO), :], ro),
                (objects.at[:, pl.ds(inner, HALO), :], re),
            )
        )
    ]
    for copy in copies:
        copy.start()
    for copy in copies[:2]:
        copy.wait()
    for ch in range(left.shape[0]):
        low = fold_pair(left[ch, :half], left[ch, half:], True)
        high = fold_pair(right[ch, :half], right[ch, half:], False)
        ze[ch] = jnp.where(even, high, low)
        zo[ch] = jnp.where(even, low, high)
    for copy in copies[2:]:
        copy.wait()


def pack(place, objects):
    channels, tile = objects.shape[:2]
    strip = jax.ShapeDtypeStruct((channels, tile // 2, LANES), jnp.float32)
    rows = jax.ShapeDtypeStruct((channels, HALO, tile), jnp.float32)
    return pl.pallas_call(
        pack_body,
        out_shape=(strip, strip, rows, rows),
        in_specs=[SCALARS, pl.BlockSpec(memory_space=pltpu.HBM)],
        out_specs=[WHOLE] * 4,
        scratch_shapes=[
            pltpu.VMEM((channels, tile, LANES), jnp.float32),
            pltpu.VMEM((channels, tile, LANES), jnp.float32),
            pltpu.SemaphoreType.DMA((4,)),
        ],
        compiler_params=pltpu.CompilerParams(vmem_limit_bytes=LARGE),
        name="pack",
    )(place, objects)


def corners_body(place, ze, zo, ce, co):
    below, even = place[0] == 0, place[1] == 0
    lane = lax.broadcasted_iota(jnp.int32, (1, LANES), 1) < HALO
    for ch in range(ze.shape[0]):
        left = jnp.where(even, zo[ch, :HALO], ze[ch, :HALO])
        right = jnp.where(even, ze[ch, :HALO], zo[ch, :HALO])
        top = jnp.where(lane, right, pltpu.roll(left, HALO, 1))
        left = jnp.where(even, zo[ch, -HALO:], ze[ch, -HALO:])
        right = jnp.where(even, ze[ch, -HALO:], zo[ch, -HALO:])
        bottom = jnp.where(lane, pltpu.roll(right, HALO, 1), left)
        ce[ch] = jnp.where(below, bottom, top)
        co[ch] = jnp.where(below, top, bottom)


def shares_body(place, ze, zo, ce, co):
    even = place[1] == 0
    lane = lax.broadcasted_iota(jnp.int32, (1, LANES), 1) < HALO
    for out, rows in ((ce, slice(-2 * HALO, -HALO)), (co, slice(-HALO, None))):
        for ch in range(out.shape[0]):
            low = jnp.where(even, zo[ch, rows], ze[ch, rows])
            high = jnp.where(even, ze[ch, rows], zo[ch, rows])
            out[ch] = jnp.where(lane, pltpu.roll(low, HALO, 1), high)


def relay(place, ze, zo, relay_body):
    shape = jax.ShapeDtypeStruct((ze.shape[0], HALO, LANES), jnp.float32)
    ce, co = pl.pallas_call(
        relay_body,
        out_shape=(shape, shape),
        in_specs=[SCALARS, WHOLE, WHOLE],
        out_specs=[WHOLE] * 2,
        compiler_params=pltpu.CompilerParams(vmem_limit_bytes=SMALL),
        name=relay_body.__name__[:-5],
    )(place, ze, zo)
    return swap(ce, 1, 0), swap(co, -1, 0)


def chain(top, left, padded, probe, spectrum, measured, tables, gradient, stage):
    width = probe.shape[1]
    down, right = top % ROWS, left % LANES
    row, column = pl.multiple_of(top - down, ROWS), left // LANES
    spot = (row, column, down, right)
    pr, pim = rolled(probe[0], down, right), rolled(probe[1], down, right)
    kr, kim = spectrum[0], spectrum[1]
    o1r = window(padded, 0, *spot, width)
    o1i = window(padded, 1, *spot, width)
    fr, fi = yield from forward(pr * o1r - pim * o1i, pr * o1i + pim * o1r, tables)
    sr, si = yield from inverse(kr * fr - kim * fi, kr * fi + kim * fr, tables)
    o2r = window(padded, 2, *spot, width)
    o2i = window(padded, 3, *spot, width)
    zr, zi = yield from forward(sr * o2r - si * o2i, sr * o2i + si * o2r, tables)
    amplitude = reorder(measured[...], tables[5], stage)
    factor = amplitude * lax.rsqrt(zr * zr + zi * zi + 1.0) - RATE
    gr, gi = yield from inverse(zr * factor, zi * factor, tables)
    accumulate(gradient, 2, *spot, sr * gr + si * gi)
    accumulate(gradient, 3, *spot, sr * gi - si * gr)
    ur, ui = yield from forward(o2r * gr + o2i * gi, o2r * gi - o2i * gr, tables)
    wr, wi = yield from inverse(kr * ur + kim * ui, kr * ui - kim * ur, tables)
    accumulate(gradient, 0, *spot, pr * wr + pim * wi)
    accumulate(gradient, 1, *spot, pr * wi - pim * wr)


def rows_of(place, tile):
    outer = pl.multiple_of(place[0] * (tile + HALO), HALO)
    inner = pl.multiple_of((1 - place[0]) * (tile + HALO), HALO)
    return outer, inner


def assemble(place, padded, ze, zo, ce, co, tile):
    half = ze.shape[1]
    even = place[1] == 0
    outer, inner = rows_of(place, tile)
    for ch in range(ze.shape[0]):
        for side, at in ((0, 0), (1, padded.shape[1] - 1)):
            strip = jnp.where(even, (zo, ze)[side][ch], (ze, zo)[side][ch])
            turned = pltpu.roll(strip, HALO, 1)
            first, second = (turned, strip) if side == 0 else (strip, turned)
            padded[ch, at, HALO : HALO + half] = first
            padded[ch, at, HALO + half : HALO + tile] = second
            padded[ch, at, pl.ds(inner, HALO)] = ce[ch]
            padded[ch, at, pl.ds(outer, HALO)] = co[ch]


def harvest(place, gradient, ze, zo, re, ro):
    tile = re.shape[2]
    tiles = tile // LANES
    half = ze.shape[1]
    even = place[1] == 0
    outer, inner = rows_of(place, tile)
    for ch in range(re.shape[0]):
        strips = []
        for at, low in ((0, False), (tiles + 1, True)):
            second = jnp.concatenate(
                [
                    gradient[ch, at, HALO + half : HALO + tile],
                    gradient[ch, at, pl.ds(inner, HALO)],
                    gradient[ch, at, pl.ds(outer, HALO)],
                ],
                0,
            )
            strips.append(fold_pair(gradient[ch, at, HALO : HALO + half], second, low))
        ze[ch] = jnp.where(even, strips[1], strips[0])
        zo[ch] = jnp.where(even, strips[0], strips[1])
        for k in range(tiles):
            lanes = slice(k * LANES, (k + 1) * LANES)
            re[ch, :, lanes] = gradient[ch, k + 1, pl.ds(inner, HALO)]
            ro[ch, :, lanes] = gradient[ch, k + 1, pl.ds(outer, HALO)]


def sort_positions(offsets, order, inside):
    count = offsets.shape[0]
    needs = [(offsets[i, 1] >= 0) & (offsets[i, 1] <= inside) for i in range(count)]
    at = jnp.int32(0)
    for i in range(count):
        order[at] = i
        at += needs[i].astype(jnp.int32)
    first = at
    for i in range(count):
        order[at] = i
        at += 1 - needs[i].astype(jnp.int32)
    return first


def run_groups(begin, end, group, offsets, order, padded, probe, spectrum, measured, tables, gradient, stage):
    def one(g, carry):
        chains = []
        for k in range(group):
            which = order[g * group + k]
            chains.append(
                chain(
                    offsets[which, 0] + HALO,
                    offsets[which, 1] + LANES,
                    padded,
                    probe,
                    spectrum,
                    measured.at[which],
                    tables,
                    gradient,
                    stage.at[k],
                )
            )
        for _ in itertools.zip_longest(*chains):
            pass
        return carry

    lax.fori_loop(begin, end, one, 0)


def early_body(
    offsets, place, objects, re, ro, probe, kernel, measured, tables,
    padded, gradient, spectrum, order, stage, sems,
):
    tile, width = re.shape[2], probe.shape[1]
    tiles = tile // LANES
    outer, inner = rows_of(place, tile)
    copies = [
        pltpu.make_async_copy(
            objects.at[:, :, pl.ds(k * LANES, LANES)],
            target.at[:, k + 1, pl.ds(HALO, tile), :],
            sems.at[n, k],
        )
        for n, target in enumerate((padded, gradient))
        for k in range(tiles)
    ]
    for copy in copies:
        copy.start()
    first = sort_positions(offsets, order, tile - width)
    for part in range(2):
        spectrum[part] = reorder(kernel[part], tables[4], stage.at[0])
    bottom = gradient.shape[2] - HALO - tile
    for ch in range(gradient.shape[0]):
        for at in (0, tiles + 1):
            gradient[ch, at] = jnp.zeros(gradient.shape[2:], jnp.float32)
        for k in range(tiles):
            gradient[ch, k + 1, :HALO] = jnp.zeros((HALO, LANES), jnp.float32)
            gradient[ch, k + 1, HALO + tile :] = jnp.zeros((bottom, LANES), jnp.float32)
            lanes = slice(k * LANES, (k + 1) * LANES)
            padded[ch, k + 1, pl.ds(inner, HALO)] = re[ch, :, lanes]
            padded[ch, k + 1, pl.ds(outer, HALO)] = ro[ch, :, lanes]
    for copy in copies:
        copy.wait()
    group = stage.shape[0]
    run_groups(
        0, first // group, group, offsets, order,
        padded, probe, spectrum, measured, tables, gradient, stage,
    )


def late_body(
    offsets, place, padded_in, gradient_in, ze, zo, ce, co, probe, spectrum, measured, tables,
    padded, gradient, gze, gzo, gre, gro, order, stage,
):
    tile, width = gre.shape[2], probe.shape[1]
    first = sort_positions(offsets, order, tile - width)
    assemble(place, padded, ze, zo, ce, co, tile)
    group = stage.shape[0]
    run_groups(
        first // group, offsets.shape[0] // group, group, offsets, order,
        padded, probe, spectrum, measured, tables, gradient, stage,
    )
    harvest(place, gradient, gze, gzo, gre, gro)


def scratch(count, width):
    group = next(k for k in GROUPS if count % k == 0)
    return [
        pltpu.SMEM((count + 1,), jnp.int32),
        pltpu.VMEM((group, 2, width, LANES), jnp.float32),
    ]


def cost(positions, width):
    return pl.CostEstimate(
        flops=positions * 6 * 8 * width**3, bytes_accessed=positions * 4 * width * width, transcendentals=0
    )


def early(offsets, place, objects, re, ro, probe, kernel, measured, tables):
    count, width = measured.shape[0], measured.shape[1]
    channels, tile = objects.shape[:2]
    extended = (channels, tile // LANES + 2, tile + 2 * HALO + ROWS, LANES)
    return pl.pallas_call(
        early_body,
        out_shape=[
            jax.ShapeDtypeStruct(extended, jnp.float32),
            jax.ShapeDtypeStruct(extended, jnp.float32),
            jax.ShapeDtypeStruct(kernel.shape, jnp.float32),
        ],
        in_specs=[SCALARS, SCALARS, pl.BlockSpec(memory_space=pl.ANY)] + [WHOLE] * 6,
        out_specs=[WHOLE] * 3,
        scratch_shapes=scratch(count, width) + [pltpu.SemaphoreType.DMA((2, tile // LANES))],
        compiler_params=pltpu.CompilerParams(vmem_limit_bytes=VMEM),
        cost_estimate=cost(count, width),
        name="early",
    )(offsets, place, objects, re, ro, probe, kernel, measured, tables)


def late(offsets, place, padded, gradient, sides, probe, spectrum, measured, tables):
    count, width = measured.shape[0], measured.shape[1]
    channels, half = sides[0].shape[:2]
    strip, rows = (channels, half + HALO, LANES), (channels, HALO, 2 * half)
    shapes = (padded.shape, gradient.shape, strip, strip, rows, rows)
    return pl.pallas_call(
        late_body,
        out_shape=[jax.ShapeDtypeStruct(x, jnp.float32) for x in shapes],
        in_specs=[SCALARS, SCALARS] + [WHOLE] * 10,
        out_specs=[WHOLE] * 6,
        scratch_shapes=scratch(count, width),
        input_output_aliases={2: 0, 3: 1},
        compiler_params=pltpu.CompilerParams(vmem_limit_bytes=VMEM),
        cost_estimate=cost(count, width),
        name="late",
    )(offsets, place, padded, gradient, *sides, probe, spectrum, measured, tables)


def settle_body(place, gradient_in, ze, zo, re, ro, ce, co, gradient, out, sems):
    tile = re.shape[2]
    tiles = tile // LANES
    half = ze.shape[1]
    even = place[1] == 0
    outer = pl.multiple_of(HALO + place[0] * (tile - HALO), HALO)
    inner = pl.multiple_of(HALO + (1 - place[0]) * (tile - HALO), HALO)
    lane = lax.broadcasted_iota(jnp.int32, (1, LANES), 1) < HALO

    def copy(k):
        return pltpu.make_async_copy(
            gradient.at[:, k + 1, pl.ds(HALO, tile), :],
            out.at[:, :, pl.ds(k * LANES, LANES)],
            sems.at[k],
        )

    for k in list(range(1, tiles - 1)) + [0, tiles - 1]:
        for ch in range(re.shape[0]):
            lanes = slice(k * LANES, (k + 1) * LANES)
            gradient[ch, k + 1, pl.ds(inner, HALO)] += re[ch, :, lanes]
            gradient[ch, k + 1, pl.ds(outer, HALO)] += ro[ch, :, lanes]
        for side in range(2):
            if k != (0, tiles - 1)[side]:
                continue
            mask = lane if side == 0 else jnp.logical_not(lane)
            for ch in range(re.shape[0]):
                strip = jnp.where(even, (zo, ze)[side][ch], (ze, zo)[side][ch])
                turned = pltpu.roll(strip, HALO, 1)
                first, second = (strip, turned) if side == 0 else (turned, strip)
                gradient[ch, k + 1, HALO : HALO + half] += jnp.where(mask, first, 0.0)
                gradient[ch, k + 1, HALO + half : HALO + tile] += jnp.where(
                    mask, second[: tile - half], 0.0
                )
                gradient[ch, k + 1, pl.ds(inner, HALO)] += jnp.where(mask, ce[ch], 0.0)
                gradient[ch, k + 1, pl.ds(outer, HALO)] += jnp.where(mask, co[ch], 0.0)
        copy(k).start()
    for k in range(tiles):
        copy(k).wait()


def settle(place, gradient, shares, tile):
    channels = gradient.shape[0]
    return pl.pallas_call(
        settle_body,
        out_shape=[
            jax.ShapeDtypeStruct(gradient.shape, jnp.float32),
            jax.ShapeDtypeStruct((channels, tile, tile), jnp.float32),
        ],
        in_specs=[SCALARS] + [WHOLE] * 7,
        out_specs=[WHOLE, pl.BlockSpec(memory_space=pl.ANY)],
        input_output_aliases={1: 0},
        scratch_shapes=[pltpu.SemaphoreType.DMA((tile // LANES,))],
        compiler_params=pltpu.CompilerParams(vmem_limit_bytes=VMEM),
        name="settle",
    )(place, gradient, *shares)[1]


def swap(x, row, col):
    rows, cols = lax.axis_size("row"), lax.axis_size("col")

    def partner(i, kind):
        return i + kind * (1 - 2 * (i % 2))

    pairs = [
        (r * cols + c, partner(r, row) * cols + partner(c, col))
        for r in range(rows)
        for c in range(cols)
        if 0 <= partner(r, row) < rows and 0 <= partner(c, col) < cols
    ]
    return lax.ppermute(x, ("row", "col"), pairs)


def per_device(objects, probe, kernel, measured, offsets):
    tile = objects.shape[1]
    tables = jnp.asarray(make_tables(probe.shape[1]))
    place = jnp.stack([lax.axis_index("row") % 2, lax.axis_index("col") % 2]).astype(jnp.int32)
    offsets, measured = offsets[0, 0], measured[0, 0]
    ze, zo, re, ro = pack(place, objects)
    ze, zo, re, ro = swap(ze, 0, 1), swap(zo, 0, -1), swap(re, 1, 0), swap(ro, -1, 0)
    padded, gradient, spectrum = early(
        offsets, place, objects, re, ro, probe, kernel, measured, tables
    )
    ze, zo, spectrum = lax.optimization_barrier((ze, zo, spectrum))
    sides = (ze, zo, *relay(place, ze, zo, corners_body))
    _, gradient, ze, zo, re, ro = late(
        offsets, place, padded, gradient, sides, probe, spectrum, measured, tables
    )
    ze, zo, re, ro = swap(ze, 0, 1), swap(zo, 0, -1), swap(re, 1, 0), swap(ro, -1, 0)
    shares = (ze, zo, re, ro, *relay(place, ze, zo, shares_body))
    return settle(place, gradient, shares, tile)


def solution(mesh):
    return jax.shard_map(
        per_device,
        mesh=mesh,
        in_specs=(
            P(None, "row", "col"),
            P(),
            P(),
            P("row", "col", None, None, None),
            P("row", "col", None, None),
        ),
        out_specs=P(None, "row", "col"),
        check_vma=False,
    )
```

```python
import itertools
import jax
import jax.numpy as jnp
import numpy as np
from jax import lax
from jax.experimental import pallas as pl
from jax.experimental.pallas import tpu as pltpu
from jax.sharding import PartitionSpec as P

HALO = 64
RATE = 0.5
LANES = 128
ROWS = 8
GROUPS = (3, 2, 1)
VMEM = 24 * 1024 * 1024
SMALL = 12 * 1024 * 1024
LARGE = 24 * 1024 * 1024
WHOLE = pl.BlockSpec(memory_space=pltpu.VMEM)
SCALARS = pl.BlockSpec(memory_space=pltpu.SMEM)


def make_tables(width):
    half = width // 2
    index = np.arange(width)
    angle = 2.0 * np.pi / width * (index[:, None] * index[None, :] % width)
    cosine = np.cos(angle) / np.sqrt(width)
    sine = np.sin(angle) / np.sqrt(width)

    def block(parity):
        c, s = cosine[parity::2, :half], sine[parity::2, :half]
        return np.block([[c, s], [-s, c]])

    even, odd = block(0), block(1)
    order = np.zeros((width, width))
    order[index[0::2], np.arange(half)] = 1.0
    order[index[1::2], half + np.arange(half)] = 1.0
    return np.stack([even, odd, even.T, odd.T, order, RATE * order]).astype(jnp.bfloat16)


def dot(a, b):
    return jnp.dot(a, b, preferred_element_type=jnp.float32)


def forward(xr, xi, tables):
    half = xr.shape[0] // 2
    le, lo, re, ro = tables[0], tables[1], tables[2], tables[3]
    u = jnp.concatenate([xr[:half] + xr[half:], xi[:half] + xi[half:]], 0)
    v = jnp.concatenate([xr[:half] - xr[half:], xi[:half] - xi[half:]], 0)
    e = dot(le, u.astype(jnp.bfloat16))
    o = dot(lo, v.astype(jnp.bfloat16))
    yield

    def fold(parts):
        fr, fi = parts[:half], parts[half:]
        p = jnp.concatenate([fr[:, :half] + fr[:, half:], fi[:, :half] + fi[:, half:]], 1)
        m = jnp.concatenate([fr[:, :half] - fr[:, half:], fi[:, :half] - fi[:, half:]], 1)
        return p.astype(jnp.bfloat16), m.astype(jnp.bfloat16)

    pe, me = fold(e)
    po, mo = fold(o)
    y = dot(jnp.concatenate([pe, po], 0), re)
    z = dot(jnp.concatenate([me, mo], 0), ro)
    yield
    return (
        jnp.concatenate([y[:, :half], z[:, :half]], 1),
        jnp.concatenate([y[:, half:], z[:, half:]], 1),
    )


def inverse(xr, xi, tables):
    half = xr.shape[0] // 2
    le, lo, re, ro = tables[2], tables[3], tables[0], tables[1]
    e = dot(le, jnp.concatenate([xr[:half], xi[:half]], 0).astype(jnp.bfloat16))
    o = dot(lo, jnp.concatenate([xr[half:], xi[half:]], 0).astype(jnp.bfloat16))
    yield
    p = (e + o).astype(jnp.bfloat16)
    m = (e - o).astype(jnp.bfloat16)

    def pick(cols):
        return jnp.concatenate(
            [
                jnp.concatenate([p[:half, cols], p[half:, cols]], 1),
                jnp.concatenate([m[:half, cols], m[half:, cols]], 1),
            ],
            0,
        )

    y = dot(pick(slice(0, half)), re)
    z = dot(pick(slice(half, 2 * half)), ro)
    yield
    s, d = y + z, y - z
    return (
        jnp.concatenate([s[:, :half], d[:, :half]], 1),
        jnp.concatenate([s[:, half:], d[:, half:]], 1),
    )


def reorder(x, order, stage):
    half = x.shape[0] // 2
    high = x.astype(jnp.bfloat16)
    low = (x - high.astype(jnp.float32)).astype(jnp.bfloat16)
    columns = dot(high, order) + dot(low, order)
    parts = []
    for k in range(2):
        stage[k] = columns[:, k * LANES : (k + 1) * LANES]
        parts.append(
            jnp.concatenate([stage[k, pl.ds(0, half, 2), :], stage[k, pl.ds(1, half, 2), :]], 0)
        )
    return jnp.concatenate(parts, 1)


def rolled(x, down, right):
    return pltpu.roll(pltpu.roll(x, down, 0), right, 1)


def masks(down, right):
    sub = lax.broadcasted_iota(jnp.int32, (ROWS, LANES), 0) >= down
    lane = lax.broadcasted_iota(jnp.int32, (1, LANES), 1) >= right
    return sub, lane


def window(ref, channel, row, tile, down, right, width):
    sub, lane = masks(down, right)
    parts = []
    for k in range(3):
        at = ref[channel, tile + k, pl.ds(row, width), :]
        after = ref[channel, tile + k, pl.ds(row + width, ROWS), :]
        parts.append(jnp.concatenate([jnp.where(sub, at[:ROWS], after), at[ROWS:]], 0))
    return jnp.concatenate([jnp.where(lane, parts[0], parts[2]), parts[1]], 1)


def accumulate(ref, channel, row, tile, down, right, value):
    width = value.shape[0]
    sub, lane = masks(down, right)
    first = value[:, :LANES]
    for k, part in enumerate(
        (jnp.where(lane, first, 0.0), value[:, LANES:], jnp.where(lane, 0.0, first))
    ):
        head = part[:ROWS]
        ref[channel, tile + k, pl.ds(row, ROWS), :] += jnp.where(sub, head, 0.0)
        ref[channel, tile + k, pl.ds(row + ROWS, width - ROWS), :] += part[ROWS:]
        ref[channel, tile + k, pl.ds(row + width, ROWS), :] += jnp.where(sub, 0.0, head)


def fold_pair(a, b, low_first):
    lane = lax.broadcasted_iota(jnp.int32, (1, LANES), 1) < HALO
    if low_first:
        return jnp.where(lane, a, pltpu.roll(b, HALO, 1))
    return jnp.where(lane, pltpu.roll(a, HALO, 1), b)


def here():
    return lax.axis_index("row") % 2, lax.axis_index("col") % 2


def low_lanes():
    return lax.broadcasted_iota(jnp.int32, (1, LANES), 1) < HALO


def pack_body(objects, padded, ze, zo, re, ro, co, sems):
    tile = objects.shape[2]
    tiles = tile // LANES
    half = ze.shape[1]
    row, col = here()
    even = col == 0
    outer = pl.multiple_of(HALO + row * (tile - HALO), HALO)
    inner = pl.multiple_of(HALO + (1 - row) * (tile - HALO), HALO)
    lane = low_lanes()
    copies = [
        pltpu.make_async_copy(
            objects.at[:, :, pl.ds(k * LANES, LANES)],
            padded.at[:, k + 1, pl.ds(HALO, tile), :],
            sems.at[k],
        )
        for k in range(tiles)
    ]
    edges = (0, tiles - 1)
    between = range(1, tiles - 1)
    for k in (*edges, *between):
        copies[k].start()
    for k in edges:
        copies[k].wait()
    for ch in range(ze.shape[0]):
        low, high = (
            fold_pair(
                padded[ch, k + 1, HALO : HALO + half],
                padded[ch, k + 1, HALO + half : HALO + tile],
                k == 0,
            )
            for k in edges
        )
        zo[ch], ze[ch] = jnp.where(even, low, high), jnp.where(even, high, low)
        first, last = (padded[ch, k + 1, pl.ds(outer, HALO)] for k in edges)
        co[ch] = jnp.where(lane, first, last)
    for k in between:
        copies[k].wait()
    for ch in range(ze.shape[0]):
        for k in range(tiles):
            lanes = slice(k * LANES, (k + 1) * LANES)
            re[ch, :, lanes] = padded[ch, k + 1, pl.ds(inner, HALO)]
            ro[ch, :, lanes] = padded[ch, k + 1, pl.ds(outer, HALO)]


def floats(*shape):
    return jax.ShapeDtypeStruct(shape, jnp.float32)


def pack(objects):
    channels, tile = objects.shape[:2]
    strip, rows = floats(channels, tile // 2, LANES), floats(channels, HALO, tile)
    extended = pltpu.VMEM(
        (channels, tile // LANES + 2, tile + 2 * HALO + ROWS, LANES), jnp.float32
    )
    return pl.pallas_call(
        pack_body,
        out_shape=(extended, strip, strip, rows, rows, floats(channels, HALO, LANES)),
        in_specs=[pl.BlockSpec(memory_space=pltpu.HBM)],
        out_specs=[WHOLE] * 6,
        scratch_shapes=[pltpu.SemaphoreType.DMA((tile // LANES,))],
        compiler_params=pltpu.CompilerParams(vmem_limit_bytes=LARGE),
        name="pack",
    )(objects)


def extend_body(ze_in, zo_in, re, co, ze, zo):
    even = here()[1] == 0
    half, last = ze_in.shape[1], re.shape[2] - LANES
    lane = low_lanes()
    for ch in range(ze.shape[0]):
        ze[ch, :half] = ze_in[ch]
        zo[ch, :half] = zo_in[ch]
        rows = jnp.where(lane, re[ch, :, :LANES], re[ch, :, last:])
        low = jnp.where(lane, rows, pltpu.roll(co[ch], HALO, 1))
        high = jnp.where(lane, pltpu.roll(rows, HALO, 1), co[ch])
        zo[ch, half:] = jnp.where(even, low, high)
        ze[ch, half:] = jnp.where(even, high, low)


def extend(ze, zo, re, co):
    strip = floats(ze.shape[0], ze.shape[1] + HALO, LANES)
    return pl.pallas_call(
        extend_body,
        out_shape=(strip, strip),
        in_specs=[WHOLE] * 4,
        out_specs=[WHOLE] * 2,
        compiler_params=pltpu.CompilerParams(vmem_limit_bytes=SMALL),
        name="extend",
    )(ze, zo, re, co)


def gather_body(ze_in, zo_in, ce, co, ze, zo):
    row, col = here()
    below, even = row == 0, col == 0
    lane = low_lanes()
    half = ze.shape[1]
    first, last = slice(0, HALO), slice(half - HALO, half)
    for ch in range(ze.shape[0]):
        top = jnp.where(below, co[ch], ce[ch])
        bottom = jnp.where(below, ce[ch], co[ch])
        left = (jnp.where(lane, pltpu.roll(top, HALO, 1), 0.0), jnp.where(lane, 0.0, bottom))
        right = (jnp.where(lane, top, 0.0), jnp.where(lane, 0.0, pltpu.roll(bottom, HALO, 1)))
        for rows, low, high in zip((first, last), left, right):
            zo[ch, rows] += jnp.where(even, low, high)
            ze[ch, rows] += jnp.where(even, high, low)


def gather(ze, zo, ce, co):
    strip = floats(*ze.shape)
    return pl.pallas_call(
        gather_body,
        out_shape=(strip, strip),
        in_specs=[WHOLE] * 4,
        out_specs=[WHOLE] * 2,
        input_output_aliases={0: 0, 1: 1},
        compiler_params=pltpu.CompilerParams(vmem_limit_bytes=SMALL),
        name="gather",
    )(ze, zo, ce, co)


def chain(top, left, padded, probe, spectrum, measured, tables, gradient):
    width = probe.shape[1]
    down, right = top % ROWS, left % LANES
    row, column = pl.multiple_of(top - down, ROWS), left // LANES
    spot = (row, column, down, right)
    pr, pim = rolled(probe[0], down, right), rolled(probe[1], down, right)
    kr, kim = spectrum[0], spectrum[1]
    o1r = window(padded, 0, *spot, width)
    o1i = window(padded, 1, *spot, width)
    fr, fi = yield from forward(pr * o1r - pim * o1i, pr * o1i + pim * o1r, tables)
    sr, si = yield from inverse(kr * fr - kim * fi, kr * fi + kim * fr, tables)
    o2r = window(padded, 2, *spot, width)
    o2i = window(padded, 3, *spot, width)
    zr, zi = yield from forward(sr * o2r - si * o2i, sr * o2i + si * o2r, tables)
    factor = measured[...] * lax.rsqrt(zr * zr + zi * zi + 1.0) - RATE
    gr, gi = yield from inverse(zr * factor, zi * factor, tables)
    accumulate(gradient, 2, *spot, sr * gr + si * gi)
    accumulate(gradient, 3, *spot, sr * gi - si * gr)
    ur, ui = yield from forward(o2r * gr + o2i * gi, o2r * gi - o2i * gr, tables)
    wr, wi = yield from inverse(kr * ur + kim * ui, kr * ui - kim * ur, tables)
    accumulate(gradient, 0, *spot, pr * wr + pim * wi)
    accumulate(gradient, 1, *spot, pr * wi - pim * wr)


def rows_of(row, tile):
    outer = pl.multiple_of(row * (tile + HALO), HALO)
    inner = pl.multiple_of((1 - row) * (tile + HALO), HALO)
    return outer, inner


def assemble(padded, ze, zo, tile):
    row, col = here()
    even = col == 0
    half = tile // 2
    outer, inner = rows_of(row, tile)
    for ch in range(ze.shape[0]):
        for side, at in ((0, 0), (1, padded.shape[1] - 1)):
            strip = jnp.where(even, (zo, ze)[side][ch], (ze, zo)[side][ch])
            turned = pltpu.roll(strip, HALO, 1)
            first, second = (turned, strip) if side == 0 else (strip, turned)
            padded[ch, at, HALO : HALO + half] = first[:half]
            padded[ch, at, HALO + half : HALO + tile] = second[:half]
            padded[ch, at, pl.ds(inner, HALO)] = first[half:]
            padded[ch, at, pl.ds(outer, HALO)] = second[half:]


def harvest(gradient, ze, zo, re, ro, ce, co):
    tile = re.shape[2]
    tiles = tile // LANES
    half = ze.shape[1]
    row, col = here()
    even = col == 0
    lane = low_lanes()
    outer, inner = rows_of(row, tile)
    for ch in range(re.shape[0]):
        for out, rows in ((ce, inner), (co, outer)):
            out[ch] = jnp.where(
                lane, gradient[ch, tiles + 1, pl.ds(rows, HALO)], gradient[ch, 0, pl.ds(rows, HALO)]
            )
        left, right = (
            fold_pair(
                gradient[ch, at, HALO : HALO + half],
                gradient[ch, at, HALO + half : HALO + tile],
                at > 0,
            )
            for at in (0, tiles + 1)
        )
        ze[ch] = jnp.where(even, right, left)
        zo[ch] = jnp.where(even, left, right)
        for k in range(tiles):
            lanes = slice(k * LANES, (k + 1) * LANES)
            re[ch, :, lanes] = gradient[ch, k + 1, pl.ds(inner, HALO)]
            ro[ch, :, lanes] = gradient[ch, k + 1, pl.ds(outer, HALO)]


def sort_positions(offsets, order, inside):
    count = offsets.shape[1]
    needs = [(offsets[1, i] >= 0) & (offsets[1, i] <= inside) for i in range(count)]
    at = jnp.int32(0)
    for i in range(count):
        order[at] = i
        at += needs[i].astype(jnp.int32)
    first = at
    for i in range(count):
        order[at] = i
        at += 1 - needs[i].astype(jnp.int32)
    return first


def run_groups(begin, end, offsets, order, padded, probe, spectrum, measured, tables, gradient):
    group = group_of(offsets.shape[1])

    def one(g, carry):
        chains = []
        for k in range(group):
            which = order[g * group + k]
            chains.append(
                chain(
                    offsets[0, which] + HALO,
                    offsets[1, which] + LANES,
                    padded,
                    probe,
                    spectrum,
                    measured.at[which],
                    tables,
                    gradient,
                )
            )
        for _ in itertools.zip_longest(*chains):
            pass
        return carry

    lax.fori_loop(begin, end, one, 0)


def prepare_body(
    padded, probe_in, kernel, measured, tables_in,
    gradient, probe, tables, spectrum, amplitudes, held, patterns, stage, sems,
):
    tile = gradient.shape[2] - 2 * HALO - ROWS
    tiles = gradient.shape[1] - 2
    loads = [
        pltpu.make_async_copy(source, target, sems.at[n])
        for n, (source, target) in enumerate(
            ((tables_in, tables), (kernel, held), (probe_in, probe), (measured, patterns))
        )
    ]
    rows = pl.ds(HALO, tile)
    copies = [
        pltpu.make_async_copy(
            padded.at[:, k + 1, rows, :], gradient.at[:, k + 1, rows, :], sems.at[len(loads) + k]
        )
        for k in range(tiles)
    ]
    for copy in loads + copies:
        copy.start()
    bottom = gradient.shape[2] - HALO - tile
    for ch in range(gradient.shape[0]):
        for at in (0, tiles + 1):
            gradient[ch, at] = jnp.zeros(gradient.shape[2:], jnp.float32)
        for k in range(tiles):
            gradient[ch, k + 1, :HALO] = jnp.zeros((HALO, LANES), jnp.float32)
            gradient[ch, k + 1, HALO + tile :] = jnp.zeros((bottom, LANES), jnp.float32)
    for copy in loads:
        copy.wait()
    for part in range(2):
        spectrum[part] = reorder(held[part], tables[4], stage.at[part])
    for which in range(patterns.shape[0]):
        amplitudes[which] = reorder(patterns[which], tables[5], stage.at[which % 2])
    for copy in copies:
        copy.wait()


def early_body(
    offsets, padded_in, gradient_in, re, ro, probe, spectrum, amplitudes, tables,
    padded, gradient, order,
):
    tile, width = re.shape[2], probe.shape[1]
    outer, inner = rows_of(here()[0], tile)
    first = sort_positions(offsets, order, tile - width)
    for ch in range(gradient.shape[0]):
        for k in range(tile // LANES):
            lanes = slice(k * LANES, (k + 1) * LANES)
            padded[ch, k + 1, pl.ds(inner, HALO)] = re[ch, :, lanes]
            padded[ch, k + 1, pl.ds(outer, HALO)] = ro[ch, :, lanes]
    run_groups(
        0, first // group_of(offsets.shape[1]), offsets, order,
        padded, probe, spectrum, amplitudes, tables, gradient,
    )


def late_body(
    offsets, padded_in, gradient_in, ze, zo, probe, spectrum, amplitudes, tables,
    padded, gradient, gze, gzo, gre, gro, gce, gco, order,
):
    tile, width = gre.shape[2], probe.shape[1]
    first = sort_positions(offsets, order, tile - width)
    assemble(padded, ze, zo, tile)
    group = group_of(offsets.shape[1])
    run_groups(
        first // group, offsets.shape[1] // group, offsets, order,
        padded, probe, spectrum, amplitudes, tables, gradient,
    )
    harvest(gradient, gze, gzo, gre, gro, gce, gco)


def group_of(count):
    return next(k for k in GROUPS if count % k == 0)


def cost(positions, width):
    return pl.CostEstimate(
        flops=positions * 6 * 8 * width**3, bytes_accessed=positions * 4 * width * width, transcendentals=0
    )


def prepare(padded, probe, kernel, measured, tables):
    width = probe.shape[1]
    far = pl.BlockSpec(memory_space=pltpu.HBM)
    anywhere = pl.BlockSpec(memory_space=pl.ANY)
    return pl.pallas_call(
        prepare_body,
        out_shape=[
            floats(*padded.shape),
            floats(*probe.shape),
            jax.ShapeDtypeStruct(tables.shape, tables.dtype),
            floats(*kernel.shape),
            floats(*measured.shape),
        ],
        in_specs=[WHOLE] + [far] * 3 + [anywhere],
        out_specs=[WHOLE] * 5,
        scratch_shapes=[
            pltpu.VMEM(kernel.shape, jnp.float32),
            pltpu.VMEM(measured.shape, jnp.float32),
            pltpu.VMEM((2, 2, width, LANES), jnp.float32),
            pltpu.SemaphoreType.DMA((4 + padded.shape[1] - 2,)),
        ],
        compiler_params=pltpu.CompilerParams(vmem_limit_bytes=VMEM),
        cost_estimate=cost(2, width),
        name="prepare",
    )(padded, probe, kernel, measured, tables)


def early(offsets, padded, gradient, re, ro, fixed):
    count, width = fixed[2].shape[:2]
    return pl.pallas_call(
        early_body,
        out_shape=[floats(*padded.shape), floats(*gradient.shape)],
        in_specs=[SCALARS] + [WHOLE] * 8,
        out_specs=[WHOLE] * 2,
        scratch_shapes=[pltpu.SMEM((count + 1,), jnp.int32)],
        input_output_aliases={1: 0, 2: 1},
        compiler_params=pltpu.CompilerParams(vmem_limit_bytes=VMEM),
        cost_estimate=cost(count, width),
        name="early",
    )(offsets, padded, gradient, re, ro, *fixed)


def late(offsets, padded, gradient, ze, zo, fixed):
    count, width = fixed[2].shape[:2]
    channels, half = ze.shape[0], ze.shape[1] - HALO
    strip, rows = floats(channels, half, LANES), floats(channels, HALO, 2 * half)
    corner = floats(channels, HALO, LANES)
    return pl.pallas_call(
        late_body,
        out_shape=[
            floats(*padded.shape), floats(*gradient.shape), strip, strip, rows, rows, corner, corner
        ],
        in_specs=[SCALARS] + [WHOLE] * 8,
        out_specs=[WHOLE] * 8,
        scratch_shapes=[pltpu.SMEM((count + 1,), jnp.int32)],
        input_output_aliases={1: 0, 2: 1},
        compiler_params=pltpu.CompilerParams(vmem_limit_bytes=VMEM),
        cost_estimate=cost(count, width),
        name="late",
    )(offsets, padded, gradient, ze, zo, *fixed)


def settle_body(gradient_in, ze, zo, re, ro, gradient, out, sems):
    tile = re.shape[2]
    tiles = tile // LANES
    half = ze.shape[1]
    row, col = here()
    even = col == 0
    outer = pl.multiple_of(HALO + row * (tile - HALO), HALO)
    inner = pl.multiple_of(HALO + (1 - row) * (tile - HALO), HALO)
    lane = low_lanes()

    def copy(k):
        return pltpu.make_async_copy(
            gradient.at[:, k + 1, pl.ds(HALO, tile), :],
            out.at[:, :, pl.ds(k * LANES, LANES)],
            sems.at[k],
        )

    for k in list(range(1, tiles - 1)) + [0, tiles - 1]:
        for ch in range(re.shape[0]):
            lanes = slice(k * LANES, (k + 1) * LANES)
            gradient[ch, k + 1, pl.ds(inner, HALO)] += re[ch, :, lanes]
            gradient[ch, k + 1, pl.ds(outer, HALO)] += ro[ch, :, lanes]
        for side in range(2):
            if k != (0, tiles - 1)[side]:
                continue
            mask = lane if side == 0 else jnp.logical_not(lane)
            for ch in range(re.shape[0]):
                strip = jnp.where(even, (zo, ze)[side][ch], (ze, zo)[side][ch])
                turned = pltpu.roll(strip, HALO, 1)
                first, second = (strip, turned) if side == 0 else (turned, strip)
                gradient[ch, k + 1, HALO : HALO + half] += jnp.where(mask, first, 0.0)
                gradient[ch, k + 1, HALO + half : HALO + tile] += jnp.where(
                    mask, second[: tile - half], 0.0
                )
        copy(k).start()
    for k in range(tiles):
        copy(k).wait()


def settle(gradient, shares, tile):
    channels = gradient.shape[0]
    return pl.pallas_call(
        settle_body,
        out_shape=[
            jax.ShapeDtypeStruct(gradient.shape, jnp.float32),
            jax.ShapeDtypeStruct((channels, tile, tile), jnp.float32),
        ],
        in_specs=[WHOLE] * 5,
        out_specs=[WHOLE, pl.BlockSpec(memory_space=pl.ANY)],
        input_output_aliases={0: 0},
        scratch_shapes=[pltpu.SemaphoreType.DMA((tile // LANES,))],
        compiler_params=pltpu.CompilerParams(vmem_limit_bytes=VMEM),
        name="settle",
    )(gradient, *shares)[1]


def swap(x, row, col):
    rows, cols = lax.axis_size("row"), lax.axis_size("col")

    def partner(i, kind):
        return i + kind * (1 - 2 * (i % 2))

    pairs = [
        (r * cols + c, partner(r, row) * cols + partner(c, col))
        for r in range(rows)
        for c in range(cols)
        if 0 <= partner(r, row) < rows and 0 <= partner(c, col) < cols
    ]
    return lax.ppermute(x, ("row", "col"), pairs)


def per_device(objects, probe, kernel, measured, offsets):
    tile = objects.shape[1]
    tables = jnp.asarray(make_tables(probe.shape[1]))
    offsets, measured = offsets[0, 0].T, measured[0, 0]
    objects, probe, kernel, measured = (
        pltpu.with_memory_space_constraint(x, pltpu.HBM) for x in (objects, probe, kernel, measured)
    )
    padded, ze, zo, re, ro, co = pack(objects)
    re, co = swap(re, 1, 0), swap(co, -1, 0)
    re, ro = lax.optimization_barrier((re, ro))
    ro = swap(ro, -1, 0)
    ze, zo = extend(ze, zo, re, co)
    ze, zo, padded = lax.optimization_barrier((ze, zo, padded))
    ze, zo = swap(ze, 0, 1), swap(zo, 0, -1)
    gradient, *fixed = prepare(padded, probe, kernel, measured, tables)
    probe, tables, spectrum, amplitudes = fixed
    fixed = (probe, spectrum, amplitudes, tables)
    padded, gradient = early(offsets, padded, gradient, re, ro, fixed)
    _, gradient, ze, zo, re, ro, ce, co = late(offsets, padded, gradient, ze, zo, fixed)
    ce, co, re, ro = swap(ce, 1, 0), swap(co, -1, 0), swap(re, 1, 0), swap(ro, -1, 0)
    ze, zo = gather(ze, zo, ce, co)
    ze, zo = swap(ze, 0, 1), swap(zo, 0, -1)
    return settle(gradient, (ze, zo, re, ro), tile)


def solution(mesh):
    return jax.shard_map(
        per_device,
        mesh=mesh,
        in_specs=(
            P(None, "row", "col"),
            P(),
            P(),
            P("row", "col", None, None, None),
            P("row", "col", None, None),
        ),
        out_specs=P(None, "row", "col"),
        check_vma=False,
    )
```

```python
import itertools
import jax
import jax.numpy as jnp
import numpy as np
from jax import lax
from jax.experimental import pallas as pl
from jax.experimental.pallas import tpu as pltpu
from jax.sharding import PartitionSpec as P

HALO = 64
RATE = 0.5
LANES = 128
ROWS = 8
GROUPS = (3, 2, 1)
VMEM = 24 * 1024 * 1024
SMALL = 12 * 1024 * 1024
LARGE = 24 * 1024 * 1024
WHOLE = pl.BlockSpec(memory_space=pltpu.VMEM)
SCALARS = pl.BlockSpec(memory_space=pltpu.SMEM)


def make_tables(width):
    half = width // 2
    index = np.arange(width)
    angle = 2.0 * np.pi / width * (index[:, None] * index[None, :] % width)
    cosine = np.cos(angle) / np.sqrt(width)
    sine = np.sin(angle) / np.sqrt(width)

    def block(parity):
        c, s = cosine[parity::2, :half], sine[parity::2, :half]
        return np.block([[c, s], [-s, c]])

    even, odd = block(0), block(1)
    order = np.zeros((width, width))
    order[index[0::2], np.arange(half)] = 1.0
    order[index[1::2], half + np.arange(half)] = 1.0
    return np.stack([even, odd, even.T, odd.T, order, RATE * order]).astype(jnp.bfloat16)


def dot(a, b):
    return jnp.dot(a, b, preferred_element_type=jnp.float32)


def forward(xr, xi, tables):
    half = xr.shape[0] // 2
    le, lo, re, ro = tables[0], tables[1], tables[2], tables[3]
    u = jnp.concatenate([xr[:half] + xr[half:], xi[:half] + xi[half:]], 0)
    v = jnp.concatenate([xr[:half] - xr[half:], xi[:half] - xi[half:]], 0)
    e = dot(le, u.astype(jnp.bfloat16))
    o = dot(lo, v.astype(jnp.bfloat16))
    yield

    def fold(parts):
        fr, fi = parts[:half], parts[half:]
        p = jnp.concatenate([fr[:, :half] + fr[:, half:], fi[:, :half] + fi[:, half:]], 1)
        m = jnp.concatenate([fr[:, :half] - fr[:, half:], fi[:, :half] - fi[:, half:]], 1)
        return p.astype(jnp.bfloat16), m.astype(jnp.bfloat16)

    pe, me = fold(e)
    po, mo = fold(o)
    y = dot(jnp.concatenate([pe, po], 0), re)
    z = dot(jnp.concatenate([me, mo], 0), ro)
    yield
    return (
        jnp.concatenate([y[:, :half], z[:, :half]], 1),
        jnp.concatenate([y[:, half:], z[:, half:]], 1),
    )


def inverse(xr, xi, tables):
    half = xr.shape[0] // 2
    le, lo, re, ro = tables[2], tables[3], tables[0], tables[1]
    e = dot(le, jnp.concatenate([xr[:half], xi[:half]], 0).astype(jnp.bfloat16))
    o = dot(lo, jnp.concatenate([xr[half:], xi[half:]], 0).astype(jnp.bfloat16))
    yield
    p = (e + o).astype(jnp.bfloat16)
    m = (e - o).astype(jnp.bfloat16)

    def pick(cols):
        return jnp.concatenate(
            [
                jnp.concatenate([p[:half, cols], p[half:, cols]], 1),
                jnp.concatenate([m[:half, cols], m[half:, cols]], 1),
            ],
            0,
        )

    y = dot(pick(slice(0, half)), re)
    z = dot(pick(slice(half, 2 * half)), ro)
    yield
    s, d = y + z, y - z
    return (
        jnp.concatenate([s[:, :half], d[:, :half]], 1),
        jnp.concatenate([s[:, half:], d[:, half:]], 1),
    )


def reorder(x, order, stage):
    half = x.shape[0] // 2
    high = x.astype(jnp.bfloat16)
    low = (x - high.astype(jnp.float32)).astype(jnp.bfloat16)
    columns = dot(high, order) + dot(low, order)
    parts = []
    for k in range(2):
        stage[k] = columns[:, k * LANES : (k + 1) * LANES]
        parts.append(
            jnp.concatenate([stage[k, pl.ds(0, half, 2), :], stage[k, pl.ds(1, half, 2), :]], 0)
        )
    return jnp.concatenate(parts, 1)


def rolled(x, down, right):
    return pltpu.roll(pltpu.roll(x, down, 0), right, 1)


def masks(down, right):
    sub = lax.broadcasted_iota(jnp.int32, (ROWS, LANES), 0) >= down
    lane = lax.broadcasted_iota(jnp.int32, (1, LANES), 1) >= right
    return sub, lane


def window(ref, channel, row, tile, down, right, width):
    sub, lane = masks(down, right)
    parts = []
    for k in range(3):
        at = ref[channel, tile + k, pl.ds(row, width), :]
        after = ref[channel, tile + k, pl.ds(row + width, ROWS), :]
        parts.append(jnp.concatenate([jnp.where(sub, at[:ROWS], after), at[ROWS:]], 0))
    return jnp.concatenate([jnp.where(lane, parts[0], parts[2]), parts[1]], 1)


def accumulate(ref, channel, row, tile, down, right, value):
    width = value.shape[0]
    sub, lane = masks(down, right)
    first = value[:, :LANES]
    for k, part in enumerate(
        (jnp.where(lane, first, 0.0), value[:, LANES:], jnp.where(lane, 0.0, first))
    ):
        head = part[:ROWS]
        ref[channel, tile + k, pl.ds(row, ROWS), :] += jnp.where(sub, head, 0.0)
        ref[channel, tile + k, pl.ds(row + ROWS, width - ROWS), :] += part[ROWS:]
        ref[channel, tile + k, pl.ds(row + width, ROWS), :] += jnp.where(sub, 0.0, head)


def fold_pair(a, b, low_first):
    lane = lax.broadcasted_iota(jnp.int32, (1, LANES), 1) < HALO
    if low_first:
        return jnp.where(lane, a, pltpu.roll(b, HALO, 1))
    return jnp.where(lane, pltpu.roll(a, HALO, 1), b)


def here():
    return lax.axis_index("row") % 2, lax.axis_index("col") % 2


def low_lanes():
    return lax.broadcasted_iota(jnp.int32, (1, LANES), 1) < HALO


def pack_body(objects, padded, ze, zo, re, ro, co, sems):
    tile = objects.shape[2]
    tiles = tile // LANES
    half = ze.shape[1]
    row, col = here()
    even = col == 0
    outer = pl.multiple_of(HALO + row * (tile - HALO), HALO)
    inner = pl.multiple_of(HALO + (1 - row) * (tile - HALO), HALO)
    lane = low_lanes()
    copies = [
        pltpu.make_async_copy(
            objects.at[:, :, pl.ds(k * LANES, LANES)],
            padded.at[:, k + 1, pl.ds(HALO, tile), :],
            sems.at[k],
        )
        for k in range(tiles)
    ]
    edges = (0, tiles - 1)
    between = range(1, tiles - 1)
    for k in (*edges, *between):
        copies[k].start()
    for k in edges:
        copies[k].wait()
    for ch in range(ze.shape[0]):
        low, high = (
            fold_pair(
                padded[ch, k + 1, HALO : HALO + half],
                padded[ch, k + 1, HALO + half : HALO + tile],
                k == 0,
            )
            for k in edges
        )
        zo[ch], ze[ch] = jnp.where(even, low, high), jnp.where(even, high, low)
        first, last = (padded[ch, k + 1, pl.ds(outer, HALO)] for k in edges)
        co[ch] = jnp.where(lane, first, last)
    for k in between:
        copies[k].wait()
    for ch in range(ze.shape[0]):
        for k in range(tiles):
            lanes = slice(k * LANES, (k + 1) * LANES)
            re[ch, :, lanes] = padded[ch, k + 1, pl.ds(inner, HALO)]
            ro[ch, :, lanes] = padded[ch, k + 1, pl.ds(outer, HALO)]


def floats(*shape):
    return jax.ShapeDtypeStruct(shape, jnp.float32)


def pack(objects):
    channels, tile = objects.shape[:2]
    strip, rows = floats(channels, tile // 2, LANES), floats(channels, HALO, tile)
    extended = pltpu.VMEM(
        (channels, tile // LANES + 2, tile + 2 * HALO + ROWS, LANES), jnp.float32
    )
    return pl.pallas_call(
        pack_body,
        out_shape=(extended, strip, strip, rows, rows, floats(channels, HALO, LANES)),
        in_specs=[pl.BlockSpec(memory_space=pltpu.HBM)],
        out_specs=[WHOLE] * 6,
        scratch_shapes=[pltpu.SemaphoreType.DMA((tile // LANES,))],
        compiler_params=pltpu.CompilerParams(vmem_limit_bytes=LARGE),
        name="pack",
    )(objects)


def extend_body(ze_in, zo_in, re, co, ze, zo):
    even = here()[1] == 0
    half, last = ze_in.shape[1], re.shape[2] - LANES
    lane = low_lanes()
    for ch in range(ze.shape[0]):
        ze[ch, :half] = ze_in[ch]
        zo[ch, :half] = zo_in[ch]
        rows = jnp.where(lane, re[ch, :, :LANES], re[ch, :, last:])
        low = jnp.where(lane, rows, pltpu.roll(co[ch], HALO, 1))
        high = jnp.where(lane, pltpu.roll(rows, HALO, 1), co[ch])
        zo[ch, half:] = jnp.where(even, low, high)
        ze[ch, half:] = jnp.where(even, high, low)


def extend(ze, zo, re, co):
    strip = floats(ze.shape[0], ze.shape[1] + HALO, LANES)
    return pl.pallas_call(
        extend_body,
        out_shape=(strip, strip),
        in_specs=[WHOLE] * 4,
        out_specs=[WHOLE] * 2,
        compiler_params=pltpu.CompilerParams(vmem_limit_bytes=SMALL),
        cost_estimate=cost(6, 2 * LANES),
        name="extend",
    )(ze, zo, re, co)


def gather_body(ze_in, zo_in, re, co, ze, zo):
    row, col = here()
    below, even = row == 0, col == 0
    lane = low_lanes()
    half = ze.shape[1]
    first, last = slice(0, HALO), slice(half - HALO, half)
    for ch in range(ze.shape[0]):
        ce = re[ch, :, re.shape[2] - LANES :]
        top = jnp.where(below, co[ch], ce)
        bottom = jnp.where(below, ce, co[ch])
        left = (jnp.where(lane, pltpu.roll(top, HALO, 1), 0.0), jnp.where(lane, 0.0, bottom))
        right = (jnp.where(lane, top, 0.0), jnp.where(lane, 0.0, pltpu.roll(bottom, HALO, 1)))
        for rows, low, high in zip((first, last), left, right):
            zo[ch, rows] += jnp.where(even, low, high)
            ze[ch, rows] += jnp.where(even, high, low)


def gather(ze, zo, re, co):
    strip = floats(*ze.shape)
    return pl.pallas_call(
        gather_body,
        out_shape=(strip, strip),
        in_specs=[WHOLE] * 4,
        out_specs=[WHOLE] * 2,
        input_output_aliases={0: 0, 1: 1},
        compiler_params=pltpu.CompilerParams(vmem_limit_bytes=SMALL),
        cost_estimate=cost(6, 2 * LANES),
        name="gather",
    )(ze, zo, re, co)


def chain(top, left, padded, probe, spectrum, measured, tables, gradient):
    width = probe.shape[1]
    down, right = top % ROWS, left % LANES
    row, column = pl.multiple_of(top - down, ROWS), left // LANES
    spot = (row, column, down, right)
    pr, pim = rolled(probe[0], down, right), rolled(probe[1], down, right)
    kr, kim = spectrum[0], spectrum[1]
    o1r = window(padded, 0, *spot, width)
    o1i = window(padded, 1, *spot, width)
    fr, fi = yield from forward(pr * o1r - pim * o1i, pr * o1i + pim * o1r, tables)
    sr, si = yield from inverse(kr * fr - kim * fi, kr * fi + kim * fr, tables)
    o2r = window(padded, 2, *spot, width)
    o2i = window(padded, 3, *spot, width)
    zr, zi = yield from forward(sr * o2r - si * o2i, sr * o2i + si * o2r, tables)
    factor = measured[...] * lax.rsqrt(zr * zr + zi * zi + 1.0) - RATE
    gr, gi = yield from inverse(zr * factor, zi * factor, tables)
    accumulate(gradient, 2, *spot, sr * gr + si * gi)
    accumulate(gradient, 3, *spot, sr * gi - si * gr)
    ur, ui = yield from forward(o2r * gr + o2i * gi, o2r * gi - o2i * gr, tables)
    wr, wi = yield from inverse(kr * ur + kim * ui, kr * ui - kim * ur, tables)
    accumulate(gradient, 0, *spot, pr * wr + pim * wi)
    accumulate(gradient, 1, *spot, pr * wi - pim * wr)


def rows_of(row, tile):
    outer = pl.multiple_of(row * (tile + HALO), HALO)
    inner = pl.multiple_of((1 - row) * (tile + HALO), HALO)
    return outer, inner


def assemble(padded, ze, zo, tile):
    row, col = here()
    even = col == 0
    half = tile // 2
    outer, inner = rows_of(row, tile)
    for ch in range(ze.shape[0]):
        for side, at in ((0, 0), (1, padded.shape[1] - 1)):
            strip = jnp.where(even, (zo, ze)[side][ch], (ze, zo)[side][ch])
            turned = pltpu.roll(strip, HALO, 1)
            first, second = (turned, strip) if side == 0 else (strip, turned)
            padded[ch, at, HALO : HALO + half] = first[:half]
            padded[ch, at, HALO + half : HALO + tile] = second[:half]
            padded[ch, at, pl.ds(inner, HALO)] = first[half:]
            padded[ch, at, pl.ds(outer, HALO)] = second[half:]


def harvest(gradient, ze, zo, re, ro, co):
    tile = ro.shape[2]
    tiles = tile // LANES
    half = ze.shape[1]
    row, col = here()
    even = col == 0
    lane = low_lanes()
    outer, inner = rows_of(row, tile)
    for ch in range(re.shape[0]):
        re[ch, :, tile:], co[ch] = (
            jnp.where(
                lane, gradient[ch, tiles + 1, pl.ds(rows, HALO)], gradient[ch, 0, pl.ds(rows, HALO)]
            )
            for rows in (inner, outer)
        )
        left, right = (
            fold_pair(
                gradient[ch, at, HALO : HALO + half],
                gradient[ch, at, HALO + half : HALO + tile],
                at > 0,
            )
            for at in (0, tiles + 1)
        )
        ze[ch] = jnp.where(even, right, left)
        zo[ch] = jnp.where(even, left, right)
        for k in range(tiles):
            lanes = slice(k * LANES, (k + 1) * LANES)
            re[ch, :, lanes] = gradient[ch, k + 1, pl.ds(inner, HALO)]
            ro[ch, :, lanes] = gradient[ch, k + 1, pl.ds(outer, HALO)]


def sort_positions(offsets, order, inside):
    count = offsets.shape[1]
    needs = [(offsets[1, i] >= 0) & (offsets[1, i] <= inside) for i in range(count)]
    at = jnp.int32(0)
    for i in range(count):
        order[at] = i
        at += needs[i].astype(jnp.int32)
    first = at
    for i in range(count):
        order[at] = i
        at += 1 - needs[i].astype(jnp.int32)
    return first


def run_groups(begin, end, offsets, order, padded, probe, spectrum, measured, tables, gradient):
    group = group_of(offsets.shape[1])

    def one(g, carry):
        chains = []
        for k in range(group):
            which = order[g * group + k]
            chains.append(
                chain(
                    offsets[0, which] + HALO,
                    offsets[1, which] + LANES,
                    padded,
                    probe,
                    spectrum,
                    measured.at[which],
                    tables,
                    gradient,
                )
            )
        for _ in itertools.zip_longest(*chains):
            pass
        return carry

    lax.fori_loop(begin, end, one, 0)


def prepare_body(
    padded, probe_in, kernel, measured, tables_in,
    gradient, probe, tables, spectrum, amplitudes, held, patterns, stage, sems,
):
    tile = gradient.shape[2] - 2 * HALO - ROWS
    tiles = gradient.shape[1] - 2
    loads = [
        pltpu.make_async_copy(source, target, sems.at[n])
        for n, (source, target) in enumerate(
            ((tables_in, tables), (kernel, held), (probe_in, probe), (measured, patterns))
        )
    ]
    rows = pl.ds(HALO, tile)
    copies = [
        pltpu.make_async_copy(
            padded.at[:, k + 1, rows, :], gradient.at[:, k + 1, rows, :], sems.at[len(loads) + k]
        )
        for k in range(tiles)
    ]
    for copy in loads + copies:
        copy.start()
    bottom = gradient.shape[2] - HALO - tile
    for ch in range(gradient.shape[0]):
        for at in (0, tiles + 1):
            gradient[ch, at] = jnp.zeros(gradient.shape[2:], jnp.float32)
        for k in range(tiles):
            gradient[ch, k + 1, :HALO] = jnp.zeros((HALO, LANES), jnp.float32)
            gradient[ch, k + 1, HALO + tile :] = jnp.zeros((bottom, LANES), jnp.float32)
    for copy in loads:
        copy.wait()
    for part in range(2):
        spectrum[part] = reorder(held[part], tables[4], stage.at[part])
    for which in range(patterns.shape[0]):
        amplitudes[which] = reorder(patterns[which], tables[5], stage.at[which % 2])
    for copy in copies:
        copy.wait()


def early_body(
    offsets, padded_in, gradient_in, re, ro, probe, spectrum, amplitudes, tables,
    padded, gradient, order,
):
    tile, width = re.shape[2], probe.shape[1]
    outer, inner = rows_of(here()[0], tile)
    first = sort_positions(offsets, order, tile - width)
    for ch in range(gradient.shape[0]):
        for k in range(tile // LANES):
            lanes = slice(k * LANES, (k + 1) * LANES)
            padded[ch, k + 1, pl.ds(inner, HALO)] = re[ch, :, lanes]
            padded[ch, k + 1, pl.ds(outer, HALO)] = ro[ch, :, lanes]
    run_groups(
        0, first // group_of(offsets.shape[1]), offsets, order,
        padded, probe, spectrum, amplitudes, tables, gradient,
    )


def late_body(
    offsets, padded_in, gradient_in, ze, zo, probe, spectrum, amplitudes, tables,
    padded, gradient, gze, gzo, gre, gro, gco, order,
):
    tile, width = gro.shape[2], probe.shape[1]
    first = sort_positions(offsets, order, tile - width)
    assemble(padded, ze, zo, tile)
    group = group_of(offsets.shape[1])
    run_groups(
        first // group, offsets.shape[1] // group, offsets, order,
        padded, probe, spectrum, amplitudes, tables, gradient,
    )
    harvest(gradient, gze, gzo, gre, gro, gco)


def group_of(count):
    return next(k for k in GROUPS if count % k == 0)


def cost(positions, width):
    return pl.CostEstimate(
        flops=positions * 6 * 8 * width**3, bytes_accessed=positions * 4 * width * width, transcendentals=0
    )


def prepare(padded, probe, kernel, measured, tables):
    width = probe.shape[1]
    far = pl.BlockSpec(memory_space=pltpu.HBM)
    return pl.pallas_call(
        prepare_body,
        out_shape=[
            floats(*padded.shape),
            floats(*probe.shape),
            jax.ShapeDtypeStruct(tables.shape, tables.dtype),
            floats(*kernel.shape),
            floats(*measured.shape),
        ],
        in_specs=[WHOLE] + [far] * 4,
        out_specs=[WHOLE] * 5,
        scratch_shapes=[
            pltpu.VMEM(kernel.shape, jnp.float32),
            pltpu.VMEM(measured.shape, jnp.float32),
            pltpu.VMEM((2, 2, width, LANES), jnp.float32),
            pltpu.SemaphoreType.DMA((4 + padded.shape[1] - 2,)),
        ],
        compiler_params=pltpu.CompilerParams(vmem_limit_bytes=VMEM),
        cost_estimate=cost(2, width),
        name="prepare",
    )(padded, probe, kernel, measured, tables)


def early(offsets, padded, gradient, re, ro, fixed):
    count, width = fixed[2].shape[:2]
    return pl.pallas_call(
        early_body,
        out_shape=[floats(*padded.shape), floats(*gradient.shape)],
        in_specs=[SCALARS] + [WHOLE] * 8,
        out_specs=[WHOLE] * 2,
        scratch_shapes=[pltpu.SMEM((count + 1,), jnp.int32)],
        input_output_aliases={1: 0, 2: 1},
        compiler_params=pltpu.CompilerParams(vmem_limit_bytes=VMEM),
        cost_estimate=cost(3, width),
        name="early",
    )(offsets, padded, gradient, re, ro, *fixed)


def late(offsets, padded, gradient, ze, zo, fixed):
    count, width = fixed[2].shape[:2]
    channels, half = ze.shape[0], ze.shape[1] - HALO
    strip, rows = floats(channels, half, LANES), floats(channels, HALO, 2 * half)
    wide, corner = floats(channels, HALO, 2 * half + LANES), floats(channels, HALO, LANES)
    return pl.pallas_call(
        late_body,
        out_shape=[
            floats(*padded.shape), floats(*gradient.shape), strip, strip, wide, rows, corner
        ],
        in_specs=[SCALARS] + [WHOLE] * 8,
        out_specs=[WHOLE] * 7,
        scratch_shapes=[pltpu.SMEM((count + 1,), jnp.int32)],
        input_output_aliases={1: 0, 2: 1},
        compiler_params=pltpu.CompilerParams(vmem_limit_bytes=VMEM),
        cost_estimate=cost(count, width),
        name="late",
    )(offsets, padded, gradient, ze, zo, *fixed)


def settle_body(gradient_in, ze, zo, re, ro, gradient, out, sems):
    tile = ro.shape[2]
    tiles = tile // LANES
    half = ze.shape[1]
    row, col = here()
    even = col == 0
    outer = pl.multiple_of(HALO + row * (tile - HALO), HALO)
    inner = pl.multiple_of(HALO + (1 - row) * (tile - HALO), HALO)
    lane = low_lanes()

    def copy(k):
        return pltpu.make_async_copy(
            gradient.at[:, k + 1, pl.ds(HALO, tile), :],
            out.at[:, :, pl.ds(k * LANES, LANES)],
            sems.at[k],
        )

    for k in list(range(1, tiles - 1)) + [0, tiles - 1]:
        for ch in range(re.shape[0]):
            lanes = slice(k * LANES, (k + 1) * LANES)
            gradient[ch, k + 1, pl.ds(inner, HALO)] += re[ch, :, lanes]
            gradient[ch, k + 1, pl.ds(outer, HALO)] += ro[ch, :, lanes]
        for side in range(2):
            if k != (0, tiles - 1)[side]:
                continue
            mask = lane if side == 0 else jnp.logical_not(lane)
            for ch in range(re.shape[0]):
                strip = jnp.where(even, (zo, ze)[side][ch], (ze, zo)[side][ch])
                turned = pltpu.roll(strip, HALO, 1)
                first, second = (strip, turned) if side == 0 else (turned, strip)
                gradient[ch, k + 1, HALO : HALO + half] += jnp.where(mask, first, 0.0)
                gradient[ch, k + 1, HALO + half : HALO + tile] += jnp.where(
                    mask, second[: tile - half], 0.0
                )
        copy(k).start()
    for k in range(tiles):
        copy(k).wait()


def settle(gradient, shares, tile):
    channels = gradient.shape[0]
    return pl.pallas_call(
        settle_body,
        out_shape=[
            jax.ShapeDtypeStruct(gradient.shape, jnp.float32),
            jax.ShapeDtypeStruct((channels, tile, tile), jnp.float32),
        ],
        in_specs=[WHOLE] * 5,
        out_specs=[WHOLE, pl.BlockSpec(memory_space=pl.ANY)],
        input_output_aliases={0: 0},
        scratch_shapes=[pltpu.SemaphoreType.DMA((tile // LANES,))],
        compiler_params=pltpu.CompilerParams(vmem_limit_bytes=VMEM),
        name="settle",
    )(gradient, *shares)[1]


def swap(x, row, col):
    rows, cols = lax.axis_size("row"), lax.axis_size("col")

    def partner(i, kind):
        return i + kind * (1 - 2 * (i % 2))

    pairs = [
        (r * cols + c, partner(r, row) * cols + partner(c, col))
        for r in range(rows)
        for c in range(cols)
        if 0 <= partner(r, row) < rows and 0 <= partner(c, col) < cols
    ]
    return lax.ppermute(x, ("row", "col"), pairs)


def per_device(objects, probe, kernel, measured, offsets):
    tile = objects.shape[1]
    tables = jnp.asarray(make_tables(probe.shape[1]))
    offsets, measured = offsets[0, 0].T, measured[0, 0]
    objects, probe, kernel, measured = (
        pltpu.with_memory_space_constraint(x, pltpu.HBM) for x in (objects, probe, kernel, measured)
    )
    tables = pltpu.with_memory_space_constraint(tables, pltpu.HBM)
    padded, ze, zo, re, ro, co = pack(objects)
    re, co = swap(re, 1, 0), swap(co, -1, 0)
    ro = swap(ro, -1, 0)
    ze, zo = extend(ze, zo, re, co)
    ze, zo, padded = lax.optimization_barrier((ze, zo, padded))
    ze, zo = swap(ze, 0, 1), swap(zo, 0, -1)
    gradient, *fixed = prepare(padded, probe, kernel, measured, tables)
    probe, tables, spectrum, amplitudes = fixed
    fixed = (probe, spectrum, amplitudes, tables)
    padded, gradient = early(offsets, padded, gradient, re, ro, fixed)
    _, gradient, ze, zo, re, ro, co = late(offsets, padded, gradient, ze, zo, fixed)
    re, co, ro = swap(re, 1, 0), swap(co, -1, 0), swap(ro, -1, 0)
    ze, zo = gather(ze, zo, re, co)
    ze, zo = swap(ze, 0, 1), swap(zo, 0, -1)
    return settle(gradient, (ze, zo, re, ro), tile)


def solution(mesh):
    return jax.shard_map(
        per_device,
        mesh=mesh,
        in_specs=(
            P(None, "row", "col"),
            P(),
            P(),
            P("row", "col", None, None, None),
            P("row", "col", None, None),
        ),
        out_specs=P(None, "row", "col"),
        check_vma=False,
    )
```

```python
import itertools
import jax
import jax.numpy as jnp
import numpy as np
from jax import lax
from jax.experimental import pallas as pl
from jax.experimental.pallas import tpu as pltpu
from jax.sharding import PartitionSpec as P

HALO = 64
RATE = 0.5
LANES = 128
ROWS = 8
GROUPS = (3, 2, 1)
VMEM = 24 * 1024 * 1024
SMALL = 12 * 1024 * 1024
LARGE = 24 * 1024 * 1024
WHOLE = pl.BlockSpec(memory_space=pltpu.VMEM)
SCALARS = pl.BlockSpec(memory_space=pltpu.SMEM)


def make_tables(width):
    half = width // 2
    index = np.arange(width)
    angle = 2.0 * np.pi / width * (index[:, None] * index[None, :] % width)
    cosine = np.cos(angle) / np.sqrt(width)
    sine = np.sin(angle) / np.sqrt(width)

    def block(parity):
        c, s = cosine[parity::2, :half], sine[parity::2, :half]
        return np.block([[c, s], [-s, c]])

    even, odd = block(0), block(1)
    order = np.zeros((width, width))
    order[index[0::2], np.arange(half)] = 1.0
    order[index[1::2], half + np.arange(half)] = 1.0
    return np.stack([even, odd, even.T, odd.T, order, RATE * order]).astype(jnp.bfloat16)


def dot(a, b):
    return jnp.dot(a, b, preferred_element_type=jnp.float32)


def forward(xr, xi, tables):
    half = xr.shape[0] // 2
    le, lo, re, ro = tables[0], tables[1], tables[2], tables[3]
    u = jnp.concatenate([xr[:half] + xr[half:], xi[:half] + xi[half:]], 0)
    v = jnp.concatenate([xr[:half] - xr[half:], xi[:half] - xi[half:]], 0)
    e = dot(le, u.astype(jnp.bfloat16))
    o = dot(lo, v.astype(jnp.bfloat16))
    yield

    def fold(parts):
        fr, fi = parts[:half], parts[half:]
        p = jnp.concatenate([fr[:, :half] + fr[:, half:], fi[:, :half] + fi[:, half:]], 1)
        m = jnp.concatenate([fr[:, :half] - fr[:, half:], fi[:, :half] - fi[:, half:]], 1)
        return p.astype(jnp.bfloat16), m.astype(jnp.bfloat16)

    pe, me = fold(e)
    po, mo = fold(o)
    y = dot(jnp.concatenate([pe, po], 0), re)
    z = dot(jnp.concatenate([me, mo], 0), ro)
    yield
    return (
        jnp.concatenate([y[:, :half], z[:, :half]], 1),
        jnp.concatenate([y[:, half:], z[:, half:]], 1),
    )


def inverse(xr, xi, tables):
    half = xr.shape[0] // 2
    le, lo, re, ro = tables[2], tables[3], tables[0], tables[1]
    e = dot(le, jnp.concatenate([xr[:half], xi[:half]], 0).astype(jnp.bfloat16))
    o = dot(lo, jnp.concatenate([xr[half:], xi[half:]], 0).astype(jnp.bfloat16))
    yield
    p = (e + o).astype(jnp.bfloat16)
    m = (e - o).astype(jnp.bfloat16)

    def pick(cols):
        return jnp.concatenate(
            [
                jnp.concatenate([p[:half, cols], p[half:, cols]], 1),
                jnp.concatenate([m[:half, cols], m[half:, cols]], 1),
            ],
            0,
        )

    y = dot(pick(slice(0, half)), re)
    z = dot(pick(slice(half, 2 * half)), ro)
    yield
    s, d = y + z, y - z
    return (
        jnp.concatenate([s[:, :half], d[:, :half]], 1),
        jnp.concatenate([s[:, half:], d[:, half:]], 1),
    )


def reorder(x, order, stage):
    half = x.shape[0] // 2
    high = x.astype(jnp.bfloat16)
    low = (x - high.astype(jnp.float32)).astype(jnp.bfloat16)
    columns = dot(high, order) + dot(low, order)
    parts = []
    for k in range(2):
        stage[k] = columns[:, k * LANES : (k + 1) * LANES]
        parts.append(
            jnp.concatenate([stage[k, pl.ds(0, half, 2), :], stage[k, pl.ds(1, half, 2), :]], 0)
        )
    return jnp.concatenate(parts, 1)


def rolled(x, down, right):
    return pltpu.roll(pltpu.roll(x, down, 0), right, 1)


def masks(down, right):
    sub = lax.broadcasted_iota(jnp.int32, (ROWS, LANES), 0) >= down
    lane = lax.broadcasted_iota(jnp.int32, (1, LANES), 1) >= right
    return sub, lane


def window(ref, channel, row, tile, down, right, width):
    sub, lane = masks(down, right)
    parts = []
    for k in range(3):
        at = ref[channel, tile + k, pl.ds(row, width), :]
        after = ref[channel, tile + k, pl.ds(row + width, ROWS), :]
        parts.append(jnp.concatenate([jnp.where(sub, at[:ROWS], after), at[ROWS:]], 0))
    return jnp.concatenate([jnp.where(lane, parts[0], parts[2]), parts[1]], 1)


def accumulate(ref, channel, row, tile, down, right, value):
    width = value.shape[0]
    sub, lane = masks(down, right)
    first = value[:, :LANES]
    for k, part in enumerate(
        (jnp.where(lane, first, 0.0), value[:, LANES:], jnp.where(lane, 0.0, first))
    ):
        head = part[:ROWS]
        ref[channel, tile + k, pl.ds(row, ROWS), :] += jnp.where(sub, head, 0.0)
        ref[channel, tile + k, pl.ds(row + ROWS, width - ROWS), :] += part[ROWS:]
        ref[channel, tile + k, pl.ds(row + width, ROWS), :] += jnp.where(sub, 0.0, head)


def fold_pair(a, b, low_first):
    lane = lax.broadcasted_iota(jnp.int32, (1, LANES), 1) < HALO
    if low_first:
        return jnp.where(lane, a, pltpu.roll(b, HALO, 1))
    return jnp.where(lane, pltpu.roll(a, HALO, 1), b)


def here():
    return lax.axis_index("row") % 2, lax.axis_index("col") % 2


def low_lanes():
    return lax.broadcasted_iota(jnp.int32, (1, LANES), 1) < HALO


def pack_body(objects, padded, ze, zo, re, ro, co, sems):
    tile = objects.shape[2]
    tiles = tile // LANES
    half = ze.shape[1]
    row, col = here()
    even = col == 0
    outer = pl.multiple_of(HALO + row * (tile - HALO), HALO)
    inner = pl.multiple_of(HALO + (1 - row) * (tile - HALO), HALO)
    lane = low_lanes()
    copies = [
        pltpu.make_async_copy(
            objects.at[:, :, pl.ds(k * LANES, LANES)],
            padded.at[:, k + 1, pl.ds(HALO, tile), :],
            sems.at[k],
        )
        for k in range(tiles)
    ]
    edges = (0, tiles - 1)
    between = range(1, tiles - 1)
    for k in (*edges, *between):
        copies[k].start()
    for k in edges:
        copies[k].wait()
    for ch in range(ze.shape[0]):
        low, high = (
            fold_pair(
                padded[ch, k + 1, HALO : HALO + half],
                padded[ch, k + 1, HALO + half : HALO + tile],
                k == 0,
            )
            for k in edges
        )
        zo[ch], ze[ch] = jnp.where(even, low, high), jnp.where(even, high, low)
        first, last = (padded[ch, k + 1, pl.ds(outer, HALO)] for k in edges)
        co[ch] = jnp.where(lane, first, last)
    for k in between:
        copies[k].wait()
    for ch in range(ze.shape[0]):
        for k in range(tiles):
            lanes = slice(k * LANES, (k + 1) * LANES)
            re[ch, :, lanes] = padded[ch, k + 1, pl.ds(inner, HALO)]
            ro[ch, :, lanes] = padded[ch, k + 1, pl.ds(outer, HALO)]


def floats(*shape):
    return jax.ShapeDtypeStruct(shape, jnp.float32)


def pack(objects):
    channels, tile = objects.shape[:2]
    strip, rows = floats(channels, tile // 2, LANES), floats(channels, HALO, tile)
    extended = pltpu.VMEM(
        (channels, tile // LANES + 2, tile + 2 * HALO + ROWS, LANES), jnp.float32
    )
    return pl.pallas_call(
        pack_body,
        out_shape=(extended, strip, strip, rows, rows, floats(channels, HALO, LANES)),
        in_specs=[pl.BlockSpec(memory_space=pltpu.HBM)],
        out_specs=[WHOLE] * 6,
        scratch_shapes=[pltpu.SemaphoreType.DMA((tile // LANES,))],
        compiler_params=pltpu.CompilerParams(vmem_limit_bytes=LARGE),
        name="pack",
    )(objects)


def extend_body(re, co, ze, zo):
    even = here()[1] == 0
    last = re.shape[2] - LANES
    lane = low_lanes()
    for ch in range(ze.shape[0]):
        rows = jnp.where(lane, re[ch, :, :LANES], re[ch, :, last:])
        low = jnp.where(lane, rows, pltpu.roll(co[ch], HALO, 1))
        high = jnp.where(lane, pltpu.roll(rows, HALO, 1), co[ch])
        zo[ch] = jnp.where(even, low, high)
        ze[ch] = jnp.where(even, high, low)


def extend(re, co):
    corner = floats(*co.shape)
    return pl.pallas_call(
        extend_body,
        out_shape=(corner, corner),
        in_specs=[WHOLE] * 2,
        out_specs=[WHOLE] * 2,
        compiler_params=pltpu.CompilerParams(vmem_limit_bytes=SMALL),
        cost_estimate=cost(6, 2 * LANES),
        name="extend",
    )(re, co)


def gather_body(ze_in, zo_in, re, co, ze, zo):
    row, col = here()
    below, even = row == 0, col == 0
    lane = low_lanes()
    half = ze.shape[1]
    first, last = slice(0, HALO), slice(half - HALO, half)
    for ch in range(ze.shape[0]):
        ce = re[ch, :, re.shape[2] - LANES :]
        top = jnp.where(below, co[ch], ce)
        bottom = jnp.where(below, ce, co[ch])
        left = (jnp.where(lane, pltpu.roll(top, HALO, 1), 0.0), jnp.where(lane, 0.0, bottom))
        right = (jnp.where(lane, top, 0.0), jnp.where(lane, 0.0, pltpu.roll(bottom, HALO, 1)))
        for rows, low, high in zip((first, last), left, right):
            zo[ch, rows] += jnp.where(even, low, high)
            ze[ch, rows] += jnp.where(even, high, low)


def gather(ze, zo, re, co):
    strip = floats(*ze.shape)
    return pl.pallas_call(
        gather_body,
        out_shape=(strip, strip),
        in_specs=[WHOLE] * 4,
        out_specs=[WHOLE] * 2,
        input_output_aliases={0: 0, 1: 1},
        compiler_params=pltpu.CompilerParams(vmem_limit_bytes=SMALL),
        cost_estimate=cost(6, 2 * LANES),
        name="gather",
    )(ze, zo, re, co)


def chain(top, left, padded, probe, spectrum, measured, tables, gradient):
    width = probe.shape[1]
    down, right = top % ROWS, left % LANES
    row, column = pl.multiple_of(top - down, ROWS), left // LANES
    spot = (row, column, down, right)
    pr, pim = rolled(probe[0], down, right), rolled(probe[1], down, right)
    kr, kim = spectrum[0], spectrum[1]
    o1r = window(padded, 0, *spot, width)
    o1i = window(padded, 1, *spot, width)
    fr, fi = yield from forward(pr * o1r - pim * o1i, pr * o1i + pim * o1r, tables)
    sr, si = yield from inverse(kr * fr - kim * fi, kr * fi + kim * fr, tables)
    o2r = window(padded, 2, *spot, width)
    o2i = window(padded, 3, *spot, width)
    zr, zi = yield from forward(sr * o2r - si * o2i, sr * o2i + si * o2r, tables)
    factor = measured[...] * lax.rsqrt(zr * zr + zi * zi + 1.0) - RATE
    gr, gi = yield from inverse(zr * factor, zi * factor, tables)
    accumulate(gradient, 2, *spot, sr * gr + si * gi)
    accumulate(gradient, 3, *spot, sr * gi - si * gr)
    ur, ui = yield from forward(o2r * gr + o2i * gi, o2r * gi - o2i * gr, tables)
    wr, wi = yield from inverse(kr * ur + kim * ui, kr * ui - kim * ur, tables)
    accumulate(gradient, 0, *spot, pr * wr + pim * wi)
    accumulate(gradient, 1, *spot, pr * wi - pim * wr)


def rows_of(row, tile):
    outer = pl.multiple_of(row * (tile + HALO), HALO)
    inner = pl.multiple_of((1 - row) * (tile + HALO), HALO)
    return outer, inner


def assemble(padded, ze, zo, ke, ko, tile):
    row, col = here()
    even = col == 0
    half = tile // 2
    outer, inner = rows_of(row, tile)
    for ch in range(ze.shape[0]):
        for side, at in ((0, 0), (1, padded.shape[1] - 1)):
            strip = jnp.where(even, (zo, ze)[side][ch], (ze, zo)[side][ch])
            turned = pltpu.roll(strip, HALO, 1)
            first, second = (turned, strip) if side == 0 else (strip, turned)
            padded[ch, at, HALO : HALO + half] = first
            padded[ch, at, HALO + half : HALO + tile] = second
            corner = jnp.where(even, (ko, ke)[side][ch], (ke, ko)[side][ch])
            turned = pltpu.roll(corner, HALO, 1)
            near, far = (turned, corner) if side == 0 else (corner, turned)
            padded[ch, at, pl.ds(inner, HALO)] = near
            padded[ch, at, pl.ds(outer, HALO)] = far


def harvest(gradient, ze, zo, re, ro, co):
    tile = ro.shape[2]
    tiles = tile // LANES
    half = ze.shape[1]
    row, col = here()
    even = col == 0
    lane = low_lanes()
    outer, inner = rows_of(row, tile)
    for ch in range(re.shape[0]):
        re[ch, :, tile:], co[ch] = (
            jnp.where(
                lane, gradient[ch, tiles + 1, pl.ds(rows, HALO)], gradient[ch, 0, pl.ds(rows, HALO)]
            )
            for rows in (inner, outer)
        )
        left, right = (
            fold_pair(
                gradient[ch, at, HALO : HALO + half],
                gradient[ch, at, HALO + half : HALO + tile],
                at > 0,
            )
            for at in (0, tiles + 1)
        )
        ze[ch] = jnp.where(even, right, left)
        zo[ch] = jnp.where(even, left, right)
        for k in range(tiles):
            lanes = slice(k * LANES, (k + 1) * LANES)
            re[ch, :, lanes] = gradient[ch, k + 1, pl.ds(inner, HALO)]
            ro[ch, :, lanes] = gradient[ch, k + 1, pl.ds(outer, HALO)]


def sort_positions(offsets, order, inside):
    count = offsets.shape[1]
    needs = [(offsets[1, i] >= 0) & (offsets[1, i] <= inside) for i in range(count)]
    at = jnp.int32(0)
    for i in range(count):
        order[at] = i
        at += needs[i].astype(jnp.int32)
    first = at
    for i in range(count):
        order[at] = i
        at += 1 - needs[i].astype(jnp.int32)
    return first


def run_groups(begin, end, offsets, order, padded, probe, spectrum, measured, tables, gradient):
    group = group_of(offsets.shape[1])

    def one(g, carry):
        chains = []
        for k in range(group):
            which = order[g * group + k]
            chains.append(
                chain(
                    offsets[0, which] + HALO,
                    offsets[1, which] + LANES,
                    padded,
                    probe,
                    spectrum,
                    measured.at[which],
                    tables,
                    gradient,
                )
            )
        for _ in itertools.zip_longest(*chains):
            pass
        return carry

    lax.fori_loop(begin, end, one, 0)


def prepare_body(
    padded, probe_in, kernel, measured, tables_in,
    gradient, probe, tables, spectrum, amplitudes, held, patterns, stage, sems,
):
    tile = gradient.shape[2] - 2 * HALO - ROWS
    tiles = gradient.shape[1] - 2
    loads = [
        pltpu.make_async_copy(source, target, sems.at[n])
        for n, (source, target) in enumerate(
            ((tables_in, tables), (kernel, held), (probe_in, probe), (measured, patterns))
        )
    ]
    rows = pl.ds(HALO, tile)
    copies = [
        pltpu.make_async_copy(
            padded.at[:, k + 1, rows, :], gradient.at[:, k + 1, rows, :], sems.at[len(loads) + k]
        )
        for k in range(tiles)
    ]
    for copy in loads + copies:
        copy.start()
    bottom = gradient.shape[2] - HALO - tile
    for ch in range(gradient.shape[0]):
        for at in (0, tiles + 1):
            gradient[ch, at] = jnp.zeros(gradient.shape[2:], jnp.float32)
        for k in range(tiles):
            gradient[ch, k + 1, :HALO] = jnp.zeros((HALO, LANES), jnp.float32)
            gradient[ch, k + 1, HALO + tile :] = jnp.zeros((bottom, LANES), jnp.float32)
    for copy in loads:
        copy.wait()
    for part in range(2):
        spectrum[part] = reorder(held[part], tables[4], stage.at[part])
    for which in range(patterns.shape[0]):
        amplitudes[which] = reorder(patterns[which], tables[5], stage.at[which % 2])
    for copy in copies:
        copy.wait()


def early_body(
    offsets, padded_in, gradient_in, re, ro, probe, spectrum, amplitudes, tables,
    padded, gradient, order,
):
    tile, width = re.shape[2], probe.shape[1]
    outer, inner = rows_of(here()[0], tile)
    first = sort_positions(offsets, order, tile - width)
    for ch in range(gradient.shape[0]):
        for k in range(tile // LANES):
            lanes = slice(k * LANES, (k + 1) * LANES)
            padded[ch, k + 1, pl.ds(inner, HALO)] = re[ch, :, lanes]
            padded[ch, k + 1, pl.ds(outer, HALO)] = ro[ch, :, lanes]
    run_groups(
        0, first // group_of(offsets.shape[1]), offsets, order,
        padded, probe, spectrum, amplitudes, tables, gradient,
    )


def late_body(
    offsets, padded_in, gradient_in, ze, zo, ke, ko, probe, spectrum, amplitudes, tables,
    padded, gradient, gze, gzo, gre, gro, gco, order,
):
    tile, width = gro.shape[2], probe.shape[1]
    first = sort_positions(offsets, order, tile - width)
    assemble(padded, ze, zo, ke, ko, tile)
    group = group_of(offsets.shape[1])
    run_groups(
        first // group, offsets.shape[1] // group, offsets, order,
        padded, probe, spectrum, amplitudes, tables, gradient,
    )
    harvest(gradient, gze, gzo, gre, gro, gco)


def group_of(count):
    return next(k for k in GROUPS if count % k == 0)


def cost(positions, width):
    return pl.CostEstimate(
        flops=positions * 6 * 8 * width**3, bytes_accessed=positions * 4 * width * width, transcendentals=0
    )


def prepare(padded, probe, kernel, measured, tables):
    width = probe.shape[1]
    far = pl.BlockSpec(memory_space=pltpu.HBM)
    return pl.pallas_call(
        prepare_body,
        out_shape=[
            floats(*padded.shape),
            floats(*probe.shape),
            jax.ShapeDtypeStruct(tables.shape, tables.dtype),
            floats(*kernel.shape),
            floats(*measured.shape),
        ],
        in_specs=[WHOLE] + [far] * 4,
        out_specs=[WHOLE] * 5,
        scratch_shapes=[
            pltpu.VMEM(kernel.shape, jnp.float32),
            pltpu.VMEM(measured.shape, jnp.float32),
            pltpu.VMEM((2, 2, width, LANES), jnp.float32),
            pltpu.SemaphoreType.DMA((4 + padded.shape[1] - 2,)),
        ],
        compiler_params=pltpu.CompilerParams(vmem_limit_bytes=VMEM),
        cost_estimate=cost(2, width),
        name="prepare",
    )(padded, probe, kernel, measured, tables)


def early(offsets, padded, gradient, re, ro, fixed):
    count, width = fixed[2].shape[:2]
    return pl.pallas_call(
        early_body,
        out_shape=[floats(*padded.shape), floats(*gradient.shape)],
        in_specs=[SCALARS] + [WHOLE] * 8,
        out_specs=[WHOLE] * 2,
        scratch_shapes=[pltpu.SMEM((count + 1,), jnp.int32)],
        input_output_aliases={1: 0, 2: 1},
        compiler_params=pltpu.CompilerParams(vmem_limit_bytes=VMEM),
        cost_estimate=cost(3, width),
        name="early",
    )(offsets, padded, gradient, re, ro, *fixed)


def late(offsets, padded, gradient, sides, fixed):
    count, width = fixed[2].shape[:2]
    channels, half = sides[0].shape[:2]
    strip, rows = floats(channels, half, LANES), floats(channels, HALO, 2 * half)
    wide, corner = floats(channels, HALO, 2 * half + LANES), floats(channels, HALO, LANES)
    return pl.pallas_call(
        late_body,
        out_shape=[
            floats(*padded.shape), floats(*gradient.shape), strip, strip, wide, rows, corner
        ],
        in_specs=[SCALARS] + [WHOLE] * 10,
        out_specs=[WHOLE] * 7,
        scratch_shapes=[pltpu.SMEM((count + 1,), jnp.int32)],
        input_output_aliases={1: 0, 2: 1},
        compiler_params=pltpu.CompilerParams(vmem_limit_bytes=VMEM),
        cost_estimate=cost(count, width),
        name="late",
    )(offsets, padded, gradient, *sides, *fixed)


def settle_body(gradient_in, ze, zo, re, ro, gradient, out, sems):
    tile = ro.shape[2]
    tiles = tile // LANES
    half = ze.shape[1]
    row, col = here()
    even = col == 0
    outer = pl.multiple_of(HALO + row * (tile - HALO), HALO)
    inner = pl.multiple_of(HALO + (1 - row) * (tile - HALO), HALO)
    lane = low_lanes()

    def copy(k):
        return pltpu.make_async_copy(
            gradient.at[:, k + 1, pl.ds(HALO, tile), :],
            out.at[:, :, pl.ds(k * LANES, LANES)],
            sems.at[k],
        )

    for k in list(range(1, tiles - 1)) + [0, tiles - 1]:
        for ch in range(re.shape[0]):
            lanes = slice(k * LANES, (k + 1) * LANES)
            gradient[ch, k + 1, pl.ds(inner, HALO)] += re[ch, :, lanes]
            gradient[ch, k + 1, pl.ds(outer, HALO)] += ro[ch, :, lanes]
        for side in range(2):
            if k != (0, tiles - 1)[side]:
                continue
            mask = lane if side == 0 else jnp.logical_not(lane)
            for ch in range(re.shape[0]):
                strip = jnp.where(even, (zo, ze)[side][ch], (ze, zo)[side][ch])
                turned = pltpu.roll(strip, HALO, 1)
                first, second = (strip, turned) if side == 0 else (turned, strip)
                gradient[ch, k + 1, HALO : HALO + half] += jnp.where(mask, first, 0.0)
                gradient[ch, k + 1, HALO + half : HALO + tile] += jnp.where(
                    mask, second[: tile - half], 0.0
                )
        copy(k).start()
    for k in range(tiles):
        copy(k).wait()


def settle(gradient, shares, tile):
    channels = gradient.shape[0]
    return pl.pallas_call(
        settle_body,
        out_shape=[
            jax.ShapeDtypeStruct(gradient.shape, jnp.float32),
            jax.ShapeDtypeStruct((channels, tile, tile), jnp.float32),
        ],
        in_specs=[WHOLE] * 5,
        out_specs=[WHOLE, pl.BlockSpec(memory_space=pl.ANY)],
        input_output_aliases={0: 0},
        scratch_shapes=[pltpu.SemaphoreType.DMA((tile // LANES,))],
        compiler_params=pltpu.CompilerParams(vmem_limit_bytes=VMEM),
        name="settle",
    )(gradient, *shares)[1]


def swap(x, row, col):
    rows, cols = lax.axis_size("row"), lax.axis_size("col")

    def partner(i, kind):
        return i + kind * (1 - 2 * (i % 2))

    pairs = [
        (r * cols + c, partner(r, row) * cols + partner(c, col))
        for r in range(rows)
        for c in range(cols)
        if 0 <= partner(r, row) < rows and 0 <= partner(c, col) < cols
    ]
    return lax.ppermute(x, ("row", "col"), pairs)


def per_device(objects, probe, kernel, measured, offsets):
    tile = objects.shape[1]
    tables = jnp.asarray(make_tables(probe.shape[1]))
    offsets, measured = offsets[0, 0].T, measured[0, 0]
    objects, probe, kernel, measured = (
        pltpu.with_memory_space_constraint(x, pltpu.HBM) for x in (objects, probe, kernel, measured)
    )
    tables = pltpu.with_memory_space_constraint(tables, pltpu.HBM)
    padded, ze, zo, re, ro, co = pack(objects)
    ze, zo, re, co, ro = swap(ze, 0, 1), swap(zo, 0, -1), swap(re, 1, 0), swap(co, -1, 0), swap(ro, -1, 0)
    ke, ko = extend(re, co)
    ke, ko, padded = lax.optimization_barrier((ke, ko, padded))
    sides = (ze, zo, swap(ke, 0, 1), swap(ko, 0, -1))
    gradient, *fixed = prepare(padded, probe, kernel, measured, tables)
    probe, tables, spectrum, amplitudes = fixed
    fixed = (probe, spectrum, amplitudes, tables)
    padded, gradient = early(offsets, padded, gradient, re, ro, fixed)
    _, gradient, ze, zo, re, ro, co = late(offsets, padded, gradient, sides, fixed)
    re, co, ro = swap(re, 1, 0), swap(co, -1, 0), swap(ro, -1, 0)
    ze, zo = gather(ze, zo, re, co)
    ze, zo = swap(ze, 0, 1), swap(zo, 0, -1)
    return settle(gradient, (ze, zo, re, ro), tile)


def solution(mesh):
    return jax.shard_map(
        per_device,
        mesh=mesh,
        in_specs=(
            P(None, "row", "col"),
            P(),
            P(),
            P("row", "col", None, None, None),
            P("row", "col", None, None),
        ),
        out_specs=P(None, "row", "col"),
        check_vma=False,
    )
```

```python
import itertools
import jax
import jax.numpy as jnp
import numpy as np
from jax import lax
from jax.experimental import pallas as pl
from jax.experimental.pallas import tpu as pltpu
from jax.sharding import PartitionSpec as P

HALO = 64
RATE = 0.5
LANES = 128
ROWS = 8
STEP = 32
GROUPS = (3, 2, 1)
VMEM = 24 * 1024 * 1024
SMALL = 12 * 1024 * 1024
LARGE = 24 * 1024 * 1024
WHOLE = pl.BlockSpec(memory_space=pltpu.VMEM)
SCALARS = pl.BlockSpec(memory_space=pltpu.SMEM)


def make_tables(width):
    half = width // 2
    index = np.arange(width)
    angle = 2.0 * np.pi / width * (index[:, None] * index[None, :] % width)
    cosine = np.cos(angle) / np.sqrt(width)
    sine = np.sin(angle) / np.sqrt(width)

    def block(parity):
        c, s = cosine[parity::2, :half], sine[parity::2, :half]
        return np.block([[c, s], [-s, c]])

    even, odd = block(0), block(1)
    order = np.zeros((width, width))
    order[index[0::2], np.arange(half)] = 1.0
    order[index[1::2], half + np.arange(half)] = 1.0
    return np.stack([even, odd, even.T, odd.T, order, RATE * order]).astype(jnp.bfloat16)


def dot(a, b):
    return jnp.dot(a, b, preferred_element_type=jnp.float32)


def steps(length):
    return range(0, length, STEP)


def rows_at(x, at):
    return x[at : at + STEP]


def narrow(*parts):
    return jnp.concatenate(parts, 1).astype(jnp.bfloat16)


def stack(parts):
    return jnp.concatenate(parts, 0)


def forward(x, half, tables):
    le, lo, re, ro = tables[0], tables[1], tables[2], tables[3]
    ur, ui, vr, vi = [], [], [], []
    for at in steps(half):
        (ar, ai), (br, bi) = x(at), x(half + at)
        for out, value in ((ur, ar + br), (ui, ai + bi), (vr, ar - br), (vi, ai - bi)):
            out.append(value.astype(jnp.bfloat16))
    e = dot(le, stack(ur + ui))
    o = dot(lo, stack(vr + vi))
    yield
    plus, minus = [], []
    for parts in (e, o):
        for at in steps(half):
            fr, fi = rows_at(parts, at), rows_at(parts, half + at)
            plus.append(narrow(fr[:, :half] + fr[:, half:], fi[:, :half] + fi[:, half:]))
            minus.append(narrow(fr[:, :half] - fr[:, half:], fi[:, :half] - fi[:, half:]))
    y = dot(stack(plus), re)
    z = dot(stack(minus), ro)
    yield

    def result(at):
        p, m = rows_at(y, at), rows_at(z, at)
        return (
            jnp.concatenate([p[:, :half], m[:, :half]], 1),
            jnp.concatenate([p[:, half:], m[:, half:]], 1),
        )

    return result


def inverse(x, half, tables):
    le, lo, re, ro = tables[2], tables[3], tables[0], tables[1]
    parities = []
    for first in (0, half):
        xr, xi = [], []
        for at in steps(half):
            r, i = x(first + at)
            xr.append(r.astype(jnp.bfloat16))
            xi.append(i.astype(jnp.bfloat16))
        parities.append(stack(xr + xi))
    e, o = dot(le, parities[0]), dot(lo, parities[1])
    yield
    low, high = [], []
    for sign in (1, -1):
        for at in steps(half):
            er, ei = rows_at(e, at), rows_at(e, half + at)
            fr, fi = rows_at(o, at), rows_at(o, half + at)
            r, i = (er + fr, ei + fi) if sign > 0 else (er - fr, ei - fi)
            low.append(narrow(r[:, :half], i[:, :half]))
            high.append(narrow(r[:, half:], i[:, half:]))
    y = dot(stack(low), re)
    z = dot(stack(high), ro)
    yield

    def result(at):
        p, m = rows_at(y, at), rows_at(z, at)
        s, d = p + m, p - m
        return (
            jnp.concatenate([s[:, :half], d[:, :half]], 1),
            jnp.concatenate([s[:, half:], d[:, half:]], 1),
        )

    return result


def reorder(x, order, stage):
    half = x.shape[0] // 2
    high = x.astype(jnp.bfloat16)
    low = (x - high.astype(jnp.float32)).astype(jnp.bfloat16)
    columns = dot(high, order) + dot(low, order)
    parts = []
    for k in range(2):
        stage[k] = columns[:, k * LANES : (k + 1) * LANES]
        parts.append(
            jnp.concatenate([stage[k, pl.ds(0, half, 2), :], stage[k, pl.ds(1, half, 2), :]], 0)
        )
    return jnp.concatenate(parts, 1)


def rolled(x, down, right):
    return pltpu.roll(pltpu.roll(x, down, 0), right, 1)


def masks(down, right):
    sub = lax.broadcasted_iota(jnp.int32, (ROWS, LANES), 0) >= down
    lane = lax.broadcasted_iota(jnp.int32, (1, LANES), 1) >= right
    return sub, lane


def window(ref, channel, row, tile, down, right, width, at):
    sub, lane = masks(down, right)
    parts = []
    for k in range(3):
        part = ref[channel, tile + k, pl.ds(row + at, STEP), :]
        if at == 0:
            after = ref[channel, tile + k, pl.ds(row + width, ROWS), :]
            part = jnp.concatenate([jnp.where(sub, part[:ROWS], after), part[ROWS:]], 0)
        parts.append(part)
    return jnp.concatenate([jnp.where(lane, parts[0], parts[2]), parts[1]], 1)


def accumulate(ref, channel, row, tile, down, right, width, at, value):
    sub, lane = masks(down, right)
    first = value[:, :LANES]
    for k, part in enumerate(
        (jnp.where(lane, first, 0.0), value[:, LANES:], jnp.where(lane, 0.0, first))
    ):
        if at == 0:
            head = part[:ROWS]
            ref[channel, tile + k, pl.ds(row, ROWS), :] += jnp.where(sub, head, 0.0)
            ref[channel, tile + k, pl.ds(row + ROWS, STEP - ROWS), :] += part[ROWS:]
            ref[channel, tile + k, pl.ds(row + width, ROWS), :] += jnp.where(sub, 0.0, head)
        else:
            ref[channel, tile + k, pl.ds(row + at, STEP), :] += part


def fold_pair(a, b, low_first):
    lane = lax.broadcasted_iota(jnp.int32, (1, LANES), 1) < HALO
    if low_first:
        return jnp.where(lane, a, pltpu.roll(b, HALO, 1))
    return jnp.where(lane, pltpu.roll(a, HALO, 1), b)


def here():
    return lax.axis_index("row") % 2, lax.axis_index("col") % 2


def low_lanes():
    return lax.broadcasted_iota(jnp.int32, (1, LANES), 1) < HALO


def pack_body(objects, padded, ze, zo, re, ro, co, sems):
    tile = objects.shape[2]
    tiles = tile // LANES
    half = ze.shape[1]
    row, col = here()
    even = col == 0
    outer = pl.multiple_of(HALO + row * (tile - HALO), HALO)
    inner = pl.multiple_of(HALO + (1 - row) * (tile - HALO), HALO)
    lane = low_lanes()
    edges = (0, tiles - 1)
    copies = [
        pltpu.make_async_copy(
            objects.at[:, :, pl.ds(k * LANES, LANES)],
            padded.at[:, k + 1, pl.ds(HALO, tile), :],
            sems.at[n],
        )
        for n, k in enumerate(edges)
    ] + [
        pltpu.make_async_copy(objects.at[:, pl.ds(rows - HALO, HALO), :], target, sems.at[2 + n])
        for n, (rows, target) in enumerate(((inner, re), (outer, ro)))
    ]
    for copy in copies:
        copy.start()
    for copy in copies[:2]:
        copy.wait()
    for ch in range(ze.shape[0]):
        low, high = (
            fold_pair(
                padded[ch, k + 1, HALO : HALO + half],
                padded[ch, k + 1, HALO + half : HALO + tile],
                k == 0,
            )
            for k in edges
        )
        zo[ch], ze[ch] = jnp.where(even, low, high), jnp.where(even, high, low)
        first, last = (padded[ch, k + 1, pl.ds(outer, HALO)] for k in edges)
        co[ch] = jnp.where(lane, first, last)
    for copy in copies[2:]:
        copy.wait()


def floats(*shape):
    return jax.ShapeDtypeStruct(shape, jnp.float32)


def pack(objects):
    channels, tile = objects.shape[:2]
    strip, rows = floats(channels, tile // 2, LANES), floats(channels, HALO, tile)
    extended = pltpu.VMEM(
        (channels, tile // LANES + 2, tile + 2 * HALO + ROWS, LANES), jnp.float32
    )
    return pl.pallas_call(
        pack_body,
        out_shape=(extended, strip, strip, rows, rows, floats(channels, HALO, LANES)),
        in_specs=[pl.BlockSpec(memory_space=pltpu.HBM)],
        out_specs=[WHOLE] * 6,
        scratch_shapes=[pltpu.SemaphoreType.DMA((4,))],
        compiler_params=pltpu.CompilerParams(vmem_limit_bytes=LARGE),
        name="pack",
    )(objects)


def extend_body(re, co, ze, zo):
    even = here()[1] == 0
    last = re.shape[2] - LANES
    lane = low_lanes()
    for ch in range(ze.shape[0]):
        rows = jnp.where(lane, re[ch, :, :LANES], re[ch, :, last:])
        low = jnp.where(lane, rows, pltpu.roll(co[ch], HALO, 1))
        high = jnp.where(lane, pltpu.roll(rows, HALO, 1), co[ch])
        zo[ch] = jnp.where(even, low, high)
        ze[ch] = jnp.where(even, high, low)


def extend(re, co):
    corner = floats(*co.shape)
    return pl.pallas_call(
        extend_body,
        out_shape=(corner, corner),
        in_specs=[WHOLE] * 2,
        out_specs=[WHOLE] * 2,
        compiler_params=pltpu.CompilerParams(vmem_limit_bytes=SMALL),
        cost_estimate=cost(1, 2 * LANES),
        name="extend",
    )(re, co)


def gather_body(ze_in, zo_in, re, co, ze, zo):
    row, col = here()
    below, even = row == 0, col == 0
    lane = low_lanes()
    half = ze.shape[1]
    first, last = slice(0, HALO), slice(half - HALO, half)
    for ch in range(ze.shape[0]):
        ce = re[ch, :, re.shape[2] - LANES :]
        top = jnp.where(below, co[ch], ce)
        bottom = jnp.where(below, ce, co[ch])
        left = (jnp.where(lane, pltpu.roll(top, HALO, 1), 0.0), jnp.where(lane, 0.0, bottom))
        right = (jnp.where(lane, top, 0.0), jnp.where(lane, 0.0, pltpu.roll(bottom, HALO, 1)))
        for rows, low, high in zip((first, last), left, right):
            zo[ch, rows] += jnp.where(even, low, high)
            ze[ch, rows] += jnp.where(even, high, low)


def gather(ze, zo, re, co):
    strip = floats(*ze.shape)
    return pl.pallas_call(
        gather_body,
        out_shape=(strip, strip),
        in_specs=[WHOLE] * 4,
        out_specs=[WHOLE] * 2,
        input_output_aliases={0: 0, 1: 1},
        compiler_params=pltpu.CompilerParams(vmem_limit_bytes=SMALL),
        cost_estimate=cost(1, 2 * LANES),
        name="gather",
    )(ze, zo, re, co)


def place_of(offsets, which):
    top = offsets[0, which] + HALO
    left = offsets[1, which] + LANES
    down, right = top % ROWS, left % LANES
    return pl.multiple_of(top - down, ROWS), left // LANES, down, right


def chain(spot, padded, probe, spectrum, measured, tables, gradient):
    width = probe.shape[1]
    half = width // 2
    held = {}

    def fixed(ref, at):
        return ref[0, pl.ds(at, STEP), :], ref[1, pl.ds(at, STEP), :]

    def windows(channel, at):
        return (window(padded, channel + part, *spot, width, at) for part in range(2))

    def illuminated(at):
        (pr, pim), (o1r, o1i) = fixed(probe, at), windows(0, at)
        return pr * o1r - pim * o1i, pr * o1i + pim * o1r

    f = yield from forward(illuminated, half, tables)

    def propagated(at):
        (kr, kim), (fr, fi) = fixed(spectrum, at), f(at)
        return kr * fr - kim * fi, kr * fi + kim * fr

    s = yield from inverse(propagated, half, tables)

    def leaving(at):
        held[at] = s(at)
        (sr, si), (o2r, o2i) = held[at], windows(2, at)
        return sr * o2r - si * o2i, sr * o2i + si * o2r

    z = yield from forward(leaving, half, tables)

    def residual(at):
        zr, zi = z(at)
        factor = measured[pl.ds(at, STEP), :] * lax.rsqrt(zr * zr + zi * zi + 1.0) - RATE
        return zr * factor, zi * factor

    g = yield from inverse(residual, half, tables)

    def back(at):
        (gr, gi), (sr, si), (o2r, o2i) = g(at), held[at], windows(2, at)
        accumulate(gradient, 2, *spot, width, at, sr * gr + si * gi)
        accumulate(gradient, 3, *spot, width, at, sr * gi - si * gr)
        return o2r * gr + o2i * gi, o2r * gi - o2i * gr

    u = yield from forward(back, half, tables)

    def returned(at):
        (kr, kim), (ur, ui) = fixed(spectrum, at), u(at)
        return kr * ur + kim * ui, kr * ui - kim * ur

    w = yield from inverse(returned, half, tables)
    for at in steps(width):
        (pr, pim), (wr, wi) = fixed(probe, at), w(at)
        accumulate(gradient, 0, *spot, width, at, pr * wr + pim * wi)
        accumulate(gradient, 1, *spot, width, at, pr * wi - pim * wr)


def rows_of(row, tile):
    outer = pl.multiple_of(row * (tile + HALO), HALO)
    inner = pl.multiple_of((1 - row) * (tile + HALO), HALO)
    return outer, inner


def write_columns(padded, ze, zo, tile):
    even = here()[1] == 0
    half = tile // 2
    for ch in range(ze.shape[0]):
        for side, at in ((0, 0), (1, padded.shape[1] - 1)):
            strip = jnp.where(even, (zo, ze)[side][ch], (ze, zo)[side][ch])
            turned = pltpu.roll(strip, HALO, 1)
            first, second = (turned, strip) if side == 0 else (strip, turned)
            padded[ch, at, HALO : HALO + half] = first
            padded[ch, at, HALO + half : HALO + tile] = second


def write_rows(padded, ke, ko, re, ro, tile):
    row, col = here()
    even = col == 0
    outer, inner = rows_of(row, tile)
    for ch in range(ke.shape[0]):
        for side, at in ((0, 0), (1, padded.shape[1] - 1)):
            corner = jnp.where(even, (ko, ke)[side][ch], (ke, ko)[side][ch])
            turned = pltpu.roll(corner, HALO, 1)
            near, far = (turned, corner) if side == 0 else (corner, turned)
            padded[ch, at, pl.ds(inner, HALO)] = near
            padded[ch, at, pl.ds(outer, HALO)] = far
        for k in range(tile // LANES):
            lanes = slice(k * LANES, (k + 1) * LANES)
            padded[ch, k + 1, pl.ds(inner, HALO)] = re[ch, :, lanes]
            padded[ch, k + 1, pl.ds(outer, HALO)] = ro[ch, :, lanes]


def harvest(gradient, ze, zo, re, ro, co):
    tile = ro.shape[2]
    tiles = tile // LANES
    half = ze.shape[1]
    row, col = here()
    even = col == 0
    lane = low_lanes()
    outer, inner = rows_of(row, tile)
    for ch in range(re.shape[0]):
        re[ch, :, tile:], co[ch] = (
            jnp.where(
                lane, gradient[ch, tiles + 1, pl.ds(rows, HALO)], gradient[ch, 0, pl.ds(rows, HALO)]
            )
            for rows in (inner, outer)
        )
        left, right = (
            fold_pair(
                gradient[ch, at, HALO : HALO + half],
                gradient[ch, at, HALO + half : HALO + tile],
                at > 0,
            )
            for at in (0, tiles + 1)
        )
        ze[ch] = jnp.where(even, right, left)
        zo[ch] = jnp.where(even, left, right)
        for k in range(tiles):
            lanes = slice(k * LANES, (k + 1) * LANES)
            re[ch, :, lanes] = gradient[ch, k + 1, pl.ds(inner, HALO)]
            ro[ch, :, lanes] = gradient[ch, k + 1, pl.ds(outer, HALO)]


def sort_positions(offsets, order, inside):
    count = offsets.shape[1]
    needs = [(offsets[0, i] >= 0) & (offsets[0, i] <= inside) for i in range(count)]
    at = jnp.int32(0)
    for i in range(count):
        order[at] = i
        at += needs[i].astype(jnp.int32)
    first = at
    for i in range(count):
        order[at] = i
        at += 1 - needs[i].astype(jnp.int32)
    return first


def run_groups(begin, end, offsets, order, padded, probes, spectrum, measured, tables, gradient):
    group = group_of(offsets.shape[1])

    def one(g, carry):
        chains = []
        for k in range(group):
            which = order[g * group + k]
            chains.append(
                chain(
                    place_of(offsets, which),
                    padded,
                    probes.at[which],
                    spectrum,
                    measured.at[which],
                    tables,
                    gradient,
                )
            )
        for _ in itertools.zip_longest(*chains):
            pass
        return carry

    lax.fori_loop(begin, end, one, 0)


def prepare_body(
    offsets, padded_in, objects, probe_in, kernel, measured, tables_in,
    padded, gradient, probes, tables, spectrum, amplitudes, probe, held, patterns, stage, sems,
):
    tile = gradient.shape[2] - 2 * HALO - ROWS
    tiles = gradient.shape[1] - 2
    loads = [
        pltpu.make_async_copy(source, target, sems.at[n])
        for n, (source, target) in enumerate(
            ((tables_in, tables), (kernel, held), (probe_in, probe), (measured, patterns))
        )
    ]
    rows = pl.ds(HALO, tile)
    copies = [
        pltpu.make_async_copy(
            padded.at[:, k + 1, rows, :], gradient.at[:, k + 1, rows, :], sems.at[len(loads) + k]
        )
        for k in (0, tiles - 1)
    ] + [
        pltpu.make_async_copy(
            objects.at[:, :, pl.ds(k * LANES, LANES)],
            target.at[:, k + 1, rows, :],
            sems.at[len(loads) + k + n * tiles],
        )
        for n, target in enumerate((gradient, padded))
        for k in range(1, tiles - 1)
    ]
    for copy in loads + copies:
        copy.start()
    bottom = gradient.shape[2] - HALO - tile
    for ch in range(gradient.shape[0]):
        for at in (0, tiles + 1):
            gradient[ch, at] = jnp.zeros(gradient.shape[2:], jnp.float32)
        for k in range(tiles):
            gradient[ch, k + 1, :HALO] = jnp.zeros((HALO, LANES), jnp.float32)
            gradient[ch, k + 1, HALO + tile :] = jnp.zeros((bottom, LANES), jnp.float32)
    for copy in loads:
        copy.wait()
    for part in range(2):
        spectrum[part] = reorder(held[part], tables[4], stage.at[part])
    for which in range(patterns.shape[0]):
        amplitudes[which] = reorder(patterns[which], tables[5], stage.at[which % 2])
        _, _, down, right = place_of(offsets, which)
        for part in range(2):
            probes[which, part] = rolled(probe[part], down, right)
    for copy in copies:
        copy.wait()


def early_body(
    offsets, padded_in, gradient_in, ze, zo, probes, spectrum, amplitudes, tables,
    padded, gradient, order,
):
    tile, width = 2 * ze.shape[1], probes.shape[2]
    first = sort_positions(offsets, order, tile - width)
    write_columns(padded, ze, zo, tile)
    run_groups(
        0, first // group_of(offsets.shape[1]), offsets, order,
        padded, probes, spectrum, amplitudes, tables, gradient,
    )


def late_body(
    offsets, padded_in, gradient_in, ke, ko, re, ro, probes, spectrum, amplitudes, tables,
    padded, gradient, gze, gzo, gre, gro, gco, order,
):
    tile, width = ro.shape[2], probes.shape[2]
    first = sort_positions(offsets, order, tile - width)
    write_rows(padded, ke, ko, re, ro, tile)
    group = group_of(offsets.shape[1])
    run_groups(
        first // group, offsets.shape[1] // group, offsets, order,
        padded, probes, spectrum, amplitudes, tables, gradient,
    )
    harvest(gradient, gze, gzo, gre, gro, gco)


def group_of(count):
    return next(k for k in GROUPS if count % k == 0)


def cost(positions, width):
    return pl.CostEstimate(
        flops=positions * 6 * 8 * width**3, bytes_accessed=positions * 4 * width * width, transcendentals=0
    )


def prepare(offsets, padded, objects, probe, kernel, measured, tables):
    width = probe.shape[1]
    far = pl.BlockSpec(memory_space=pltpu.HBM)
    return pl.pallas_call(
        prepare_body,
        out_shape=[
            floats(*padded.shape),
            floats(*padded.shape),
            floats(measured.shape[0], *probe.shape),
            jax.ShapeDtypeStruct(tables.shape, tables.dtype),
            floats(*kernel.shape),
            floats(*measured.shape),
        ],
        in_specs=[SCALARS, WHOLE] + [far] * 5,
        out_specs=[WHOLE] * 6,
        input_output_aliases={1: 0},
        scratch_shapes=[
            pltpu.VMEM(probe.shape, jnp.float32),
            pltpu.VMEM(kernel.shape, jnp.float32),
            pltpu.VMEM(measured.shape, jnp.float32),
            pltpu.VMEM((2, 2, width, LANES), jnp.float32),
            pltpu.SemaphoreType.DMA((4 + 2 * (padded.shape[1] - 2),)),
        ],
        compiler_params=pltpu.CompilerParams(vmem_limit_bytes=VMEM),
        cost_estimate=cost(2, width),
        name="prepare",
    )(offsets, padded, objects, probe, kernel, measured, tables)


def early(offsets, padded, gradient, ze, zo, fixed):
    count, width = fixed[2].shape[:2]
    return pl.pallas_call(
        early_body,
        out_shape=[floats(*padded.shape), floats(*gradient.shape)],
        in_specs=[SCALARS] + [WHOLE] * 8,
        out_specs=[WHOLE] * 2,
        scratch_shapes=[pltpu.SMEM((count + 1,), jnp.int32)],
        input_output_aliases={1: 0, 2: 1},
        compiler_params=pltpu.CompilerParams(vmem_limit_bytes=VMEM),
        cost_estimate=cost(3, width),
        name="early",
    )(offsets, padded, gradient, ze, zo, *fixed)


def late(offsets, padded, gradient, sides, fixed):
    count, width = fixed[2].shape[:2]
    channels, half = sides[2].shape[0], sides[2].shape[2] // 2
    strip, rows = floats(channels, half, LANES), floats(channels, HALO, 2 * half)
    wide, corner = floats(channels, HALO, 2 * half + LANES), floats(channels, HALO, LANES)
    return pl.pallas_call(
        late_body,
        out_shape=[
            floats(*padded.shape), floats(*gradient.shape), strip, strip, wide, rows, corner
        ],
        in_specs=[SCALARS] + [WHOLE] * 10,
        out_specs=[WHOLE] * 7,
        scratch_shapes=[pltpu.SMEM((count + 1,), jnp.int32)],
        input_output_aliases={1: 0, 2: 1},
        compiler_params=pltpu.CompilerParams(vmem_limit_bytes=VMEM),
        cost_estimate=cost(count, width),
        name="late",
    )(offsets, padded, gradient, *sides, *fixed)


def tile_copy(gradient, out, sems, k):
    tile = out.shape[2]
    return pltpu.make_async_copy(
        gradient.at[:, k + 1, pl.ds(HALO, tile), :],
        out.at[:, :, pl.ds(k * LANES, LANES)],
        sems.at[k],
    )


def inside_body(gradient_in, re, ro, gradient, out, sems):
    tile = ro.shape[2]
    row = here()[0]
    outer = pl.multiple_of(HALO + row * (tile - HALO), HALO)
    inner = pl.multiple_of(HALO + (1 - row) * (tile - HALO), HALO)
    tiles = tile // LANES
    for k in [*range(1, tiles - 1), 0, tiles - 1]:
        lanes = slice(k * LANES, (k + 1) * LANES)
        for ch in range(ro.shape[0]):
            gradient[ch, k + 1, pl.ds(inner, HALO)] += re[ch, :, lanes]
            gradient[ch, k + 1, pl.ds(outer, HALO)] += ro[ch, :, lanes]
        if 0 < k < tiles - 1:
            tile_copy(gradient, out, sems, k).start()
    for k in range(1, tiles - 1):
        tile_copy(gradient, out, sems, k).wait()


def border_body(gradient_in, out_in, ze, zo, gradient, out, sems):
    tile = out.shape[2]
    tiles = tile // LANES
    half = ze.shape[1]
    even = here()[1] == 0
    lane = low_lanes()
    for side, k in enumerate((0, tiles - 1)):
        mask = lane if side == 0 else jnp.logical_not(lane)
        for ch in range(ze.shape[0]):
            strip = jnp.where(even, (zo, ze)[side][ch], (ze, zo)[side][ch])
            turned = pltpu.roll(strip, HALO, 1)
            first, second = (strip, turned) if side == 0 else (turned, strip)
            gradient[ch, k + 1, HALO : HALO + half] += jnp.where(mask, first, 0.0)
            gradient[ch, k + 1, HALO + half : HALO + tile] += jnp.where(mask, second, 0.0)
        tile_copy(gradient, out, sems, k).start()
    for k in (0, tiles - 1):
        tile_copy(gradient, out, sems, k).wait()


def settle(gradient, ze, zo, re, ro, tile):
    channels = gradient.shape[0]
    far = pl.BlockSpec(memory_space=pltpu.HBM)
    shapes = [floats(*gradient.shape), floats(channels, tile, tile)]
    common = dict(
        out_shape=shapes,
        out_specs=[WHOLE, far],
        scratch_shapes=[pltpu.SemaphoreType.DMA((tile // LANES,))],
        compiler_params=pltpu.CompilerParams(vmem_limit_bytes=VMEM),
    )
    gradient, out = pl.pallas_call(
        inside_body,
        in_specs=[WHOLE] * 3,
        input_output_aliases={0: 0},
        name="inside",
        **common,
    )(gradient, re, ro)
    return pl.pallas_call(
        border_body,
        in_specs=[WHOLE, far, WHOLE, WHOLE],
        input_output_aliases={0: 0, 1: 1},
        name="border",
        **common,
    )(gradient, out, ze, zo)[1]


def swap(x, row, col):
    rows, cols = lax.axis_size("row"), lax.axis_size("col")

    def partner(i, kind):
        return i + kind * (1 - 2 * (i % 2))

    pairs = [
        (r * cols + c, partner(r, row) * cols + partner(c, col))
        for r in range(rows)
        for c in range(cols)
        if 0 <= partner(r, row) < rows and 0 <= partner(c, col) < cols
    ]
    return lax.ppermute(x, ("row", "col"), pairs)


def per_device(objects, probe, kernel, measured, offsets):
    tile = objects.shape[1]
    tables = jnp.asarray(make_tables(probe.shape[1]))
    offsets, measured = offsets[0, 0].T, measured[0, 0]
    objects, probe, kernel, measured = (
        pltpu.with_memory_space_constraint(x, pltpu.HBM) for x in (objects, probe, kernel, measured)
    )
    tables = pltpu.with_memory_space_constraint(tables, pltpu.HBM)
    padded, ze, zo, re, ro, co = pack(objects)
    ze, zo, re, co, ro = swap(ze, 0, 1), swap(zo, 0, -1), swap(re, 1, 0), swap(co, -1, 0), swap(ro, -1, 0)
    ke, ko = extend(re, co)
    ke, ko, padded = lax.optimization_barrier((ke, ko, padded))
    sides = (swap(ke, 0, 1), swap(ko, 0, -1), re, ro)
    padded, gradient, *fixed = prepare(offsets, padded, objects, probe, kernel, measured, tables)
    probe, tables, spectrum, amplitudes = fixed
    fixed = (probe, spectrum, amplitudes, tables)
    padded, gradient = early(offsets, padded, gradient, ze, zo, fixed)
    _, gradient, ze, zo, re, ro, co = late(offsets, padded, gradient, sides, fixed)
    re, co, ro = swap(re, 1, 0), swap(co, -1, 0), swap(ro, -1, 0)
    ze, zo = gather(ze, zo, re, co)
    ze, zo = swap(ze, 0, 1), swap(zo, 0, -1)
    return settle(gradient, ze, zo, re, ro, tile)


def solution(mesh):
    return jax.shard_map(
        per_device,
        mesh=mesh,
        in_specs=(
            P(None, "row", "col"),
            P(),
            P(),
            P("row", "col", None, None, None),
            P("row", "col", None, None),
        ),
        out_specs=P(None, "row", "col"),
        check_vma=False,
    )
```

```python
import itertools
import jax
import jax.numpy as jnp
import numpy as np
from jax import lax
from jax.experimental import pallas as pl
from jax.experimental.pallas import tpu as pltpu
from jax.sharding import PartitionSpec as P

HALO = 64
RATE = 0.5
LANES = 128
ROWS = 8
STEP = 32
GROUPS = (3, 2, 1)
VMEM = 24 * 1024 * 1024
SMALL = 12 * 1024 * 1024
LARGE = 24 * 1024 * 1024
WHOLE = pl.BlockSpec(memory_space=pltpu.VMEM)
SCALARS = pl.BlockSpec(memory_space=pltpu.SMEM)


def make_tables(width):
    half = width // 2
    index = np.arange(width)
    angle = 2.0 * np.pi / width * (index[:, None] * index[None, :] % width)
    cosine = np.cos(angle) / np.sqrt(width)
    sine = np.sin(angle) / np.sqrt(width)

    def block(parity):
        c, s = cosine[parity::2, :half], sine[parity::2, :half]
        return np.block([[c, s], [-s, c]])

    even, odd = block(0), block(1)
    order = np.zeros((width, width))
    order[index[0::2], np.arange(half)] = 1.0
    order[index[1::2], half + np.arange(half)] = 1.0
    return np.stack([even, odd, even.T, odd.T, order, RATE * order]).astype(jnp.bfloat16)


def dot(a, b):
    return jnp.dot(a, b, preferred_element_type=jnp.float32)


def steps(length):
    return range(0, length, STEP)


def rows_at(x, at):
    return x[at : at + STEP]


def narrow(*parts):
    return jnp.concatenate(parts, 1).astype(jnp.bfloat16)


def stack(parts):
    return jnp.concatenate(parts, 0)


def forward(x, half, tables):
    le, lo, re, ro = tables[0], tables[1], tables[2], tables[3]
    ur, ui, vr, vi = [], [], [], []
    for at in steps(half):
        (ar, ai), (br, bi) = x(at), x(half + at)
        for out, value in ((ur, ar + br), (ui, ai + bi), (vr, ar - br), (vi, ai - bi)):
            out.append(value.astype(jnp.bfloat16))
    e = dot(le, stack(ur + ui))
    o = dot(lo, stack(vr + vi))
    yield
    plus, minus = [], []
    for parts in (e, o):
        for at in steps(half):
            fr, fi = rows_at(parts, at), rows_at(parts, half + at)
            plus.append(narrow(fr[:, :half] + fr[:, half:], fi[:, :half] + fi[:, half:]))
            minus.append(narrow(fr[:, :half] - fr[:, half:], fi[:, :half] - fi[:, half:]))
    y = dot(stack(plus), re)
    z = dot(stack(minus), ro)
    yield

    def result(at):
        p, m = rows_at(y, at), rows_at(z, at)
        return (
            jnp.concatenate([p[:, :half], m[:, :half]], 1),
            jnp.concatenate([p[:, half:], m[:, half:]], 1),
        )

    return result


def inverse(x, half, tables):
    le, lo, re, ro = tables[2], tables[3], tables[0], tables[1]
    parities = []
    for first in (0, half):
        xr, xi = [], []
        for at in steps(half):
            r, i = x(first + at)
            xr.append(r.astype(jnp.bfloat16))
            xi.append(i.astype(jnp.bfloat16))
        parities.append(stack(xr + xi))
    e, o = dot(le, parities[0]), dot(lo, parities[1])
    yield
    low, high = [], []
    for sign in (1, -1):
        for at in steps(half):
            er, ei = rows_at(e, at), rows_at(e, half + at)
            fr, fi = rows_at(o, at), rows_at(o, half + at)
            r, i = (er + fr, ei + fi) if sign > 0 else (er - fr, ei - fi)
            low.append(narrow(r[:, :half], i[:, :half]))
            high.append(narrow(r[:, half:], i[:, half:]))
    y = dot(stack(low), re)
    z = dot(stack(high), ro)
    yield

    def result(at):
        p, m = rows_at(y, at), rows_at(z, at)
        s, d = p + m, p - m
        return (
            jnp.concatenate([s[:, :half], d[:, :half]], 1),
            jnp.concatenate([s[:, half:], d[:, half:]], 1),
        )

    return result


def reorder(x, order, stage):
    half = x.shape[0] // 2
    high = x.astype(jnp.bfloat16)
    low = (x - high.astype(jnp.float32)).astype(jnp.bfloat16)
    columns = dot(high, order) + dot(low, order)
    parts = []
    for k in range(2):
        stage[k] = columns[:, k * LANES : (k + 1) * LANES]
        parts.append(
            jnp.concatenate([stage[k, pl.ds(0, half, 2), :], stage[k, pl.ds(1, half, 2), :]], 0)
        )
    return jnp.concatenate(parts, 1)


def rolled(x, down, right):
    return pltpu.roll(pltpu.roll(x, down, 0), right, 1)


def masks(down, right):
    sub = lax.broadcasted_iota(jnp.int32, (ROWS, LANES), 0) >= down
    lane = lax.broadcasted_iota(jnp.int32, (1, LANES), 1) >= right
    return sub, lane


def window(ref, channel, row, tile, down, right, width, at):
    sub, lane = masks(down, right)
    parts = []
    for k in range(3):
        part = ref[channel, tile + k, pl.ds(row + at, STEP), :]
        if at == 0:
            after = ref[channel, tile + k, pl.ds(row + width, ROWS), :]
            part = jnp.concatenate([jnp.where(sub, part[:ROWS], after), part[ROWS:]], 0)
        parts.append(part)
    return jnp.concatenate([jnp.where(lane, parts[0], parts[2]), parts[1]], 1)


def accumulate(ref, channel, row, tile, down, right, width, at, value):
    sub, lane = masks(down, right)
    first = value[:, :LANES]
    for k, part in enumerate(
        (jnp.where(lane, first, 0.0), value[:, LANES:], jnp.where(lane, 0.0, first))
    ):
        if at == 0:
            head = part[:ROWS]
            ref[channel, tile + k, pl.ds(row, ROWS), :] += jnp.where(sub, head, 0.0)
            ref[channel, tile + k, pl.ds(row + ROWS, STEP - ROWS), :] += part[ROWS:]
            ref[channel, tile + k, pl.ds(row + width, ROWS), :] += jnp.where(sub, 0.0, head)
        else:
            ref[channel, tile + k, pl.ds(row + at, STEP), :] += part


def fold_pair(a, b, low_first):
    lane = lax.broadcasted_iota(jnp.int32, (1, LANES), 1) < HALO
    if low_first:
        return jnp.where(lane, a, pltpu.roll(b, HALO, 1))
    return jnp.where(lane, pltpu.roll(a, HALO, 1), b)


def here():
    return lax.axis_index("row") % 2, lax.axis_index("col") % 2


def low_lanes():
    return lax.broadcasted_iota(jnp.int32, (1, LANES), 1) < HALO


def pack_body(objects, padded, ze, zo, re, ro, co, sems):
    tile = objects.shape[2]
    tiles = tile // LANES
    half = ze.shape[1]
    row, col = here()
    even = col == 0
    outer = pl.multiple_of(HALO + row * (tile - HALO), HALO)
    inner = pl.multiple_of(HALO + (1 - row) * (tile - HALO), HALO)
    lane = low_lanes()
    edges = (0, tiles - 1)
    copies = [
        pltpu.make_async_copy(
            objects.at[:, :, pl.ds(k * LANES, LANES)],
            padded.at[:, k + 1, pl.ds(HALO, tile), :],
            sems.at[n],
        )
        for n, k in enumerate(edges)
    ] + [
        pltpu.make_async_copy(objects.at[:, pl.ds(rows - HALO, HALO), :], target, sems.at[2 + n])
        for n, (rows, target) in enumerate(((inner, re), (outer, ro)))
    ]
    for copy in copies:
        copy.start()
    for copy in copies[:2]:
        copy.wait()
    for ch in range(ze.shape[0]):
        low, high = (
            fold_pair(
                padded[ch, k + 1, HALO : HALO + half],
                padded[ch, k + 1, HALO + half : HALO + tile],
                k == 0,
            )
            for k in edges
        )
        zo[ch], ze[ch] = jnp.where(even, low, high), jnp.where(even, high, low)
        first, last = (padded[ch, k + 1, pl.ds(outer, HALO)] for k in edges)
        co[ch] = jnp.where(lane, first, last)
    for copy in copies[2:]:
        copy.wait()


def floats(*shape):
    return jax.ShapeDtypeStruct(shape, jnp.float32)


def pack(objects):
    channels, tile = objects.shape[:2]
    strip, rows = floats(channels, tile // 2, LANES), floats(channels, HALO, tile)
    extended = pltpu.VMEM(
        (channels, tile // LANES + 2, tile + 2 * HALO + ROWS, LANES), jnp.float32
    )
    return pl.pallas_call(
        pack_body,
        out_shape=(extended, strip, strip, rows, rows, floats(channels, HALO, LANES)),
        in_specs=[pl.BlockSpec(memory_space=pltpu.HBM)],
        out_specs=[WHOLE] * 6,
        scratch_shapes=[pltpu.SemaphoreType.DMA((4,))],
        compiler_params=pltpu.CompilerParams(vmem_limit_bytes=LARGE),
        name="pack",
    )(objects)


def extend_body(re, co, ze, zo):
    even = here()[1] == 0
    last = re.shape[2] - LANES
    lane = low_lanes()
    for ch in range(ze.shape[0]):
        rows = jnp.where(lane, re[ch, :, :LANES], re[ch, :, last:])
        low = jnp.where(lane, rows, pltpu.roll(co[ch], HALO, 1))
        high = jnp.where(lane, pltpu.roll(rows, HALO, 1), co[ch])
        zo[ch] = jnp.where(even, low, high)
        ze[ch] = jnp.where(even, high, low)


def extend(re, co):
    corner = floats(*co.shape)
    return pl.pallas_call(
        extend_body,
        out_shape=(corner, corner),
        in_specs=[WHOLE] * 2,
        out_specs=[WHOLE] * 2,
        compiler_params=pltpu.CompilerParams(vmem_limit_bytes=SMALL),
        cost_estimate=cost(1, 2 * LANES),
        name="extend",
    )(re, co)


def gather_body(ze_in, zo_in, re, co, ze, zo):
    row, col = here()
    below, even = row == 0, col == 0
    lane = low_lanes()
    half = ze.shape[1]
    first, last = slice(0, HALO), slice(half - HALO, half)
    for ch in range(ze.shape[0]):
        ce = re[ch, :, re.shape[2] - LANES :]
        top = jnp.where(below, co[ch], ce)
        bottom = jnp.where(below, ce, co[ch])
        left = (jnp.where(lane, pltpu.roll(top, HALO, 1), 0.0), jnp.where(lane, 0.0, bottom))
        right = (jnp.where(lane, top, 0.0), jnp.where(lane, 0.0, pltpu.roll(bottom, HALO, 1)))
        for rows, low, high in zip((first, last), left, right):
            zo[ch, rows] += jnp.where(even, low, high)
            ze[ch, rows] += jnp.where(even, high, low)


def gather(ze, zo, re, co):
    strip = floats(*ze.shape)
    return pl.pallas_call(
        gather_body,
        out_shape=(strip, strip),
        in_specs=[WHOLE] * 4,
        out_specs=[WHOLE] * 2,
        input_output_aliases={0: 0, 1: 1},
        compiler_params=pltpu.CompilerParams(vmem_limit_bytes=SMALL),
        cost_estimate=cost(1, 2 * LANES),
        name="gather",
    )(ze, zo, re, co)


def place_of(offsets, which):
    top = offsets[0, which] + HALO
    left = offsets[1, which] + LANES
    down, right = top % ROWS, left % LANES
    return pl.multiple_of(top - down, ROWS), left // LANES, down, right


def chain(spot, padded, probe, spectrum, measured, tables, gradient):
    width = probe.shape[1]
    half = width // 2
    held = {}

    def fixed(ref, at):
        return ref[0, pl.ds(at, STEP), :], ref[1, pl.ds(at, STEP), :]

    def windows(channel, at):
        return (window(padded, channel + part, *spot, width, at) for part in range(2))

    def illuminated(at):
        (pr, pim), (o1r, o1i) = fixed(probe, at), windows(0, at)
        return pr * o1r - pim * o1i, pr * o1i + pim * o1r

    f = yield from forward(illuminated, half, tables)

    def propagated(at):
        (kr, kim), (fr, fi) = fixed(spectrum, at), f(at)
        return kr * fr - kim * fi, kr * fi + kim * fr

    s = yield from inverse(propagated, half, tables)

    def leaving(at):
        held[at] = s(at)
        (sr, si), (o2r, o2i) = held[at], windows(2, at)
        return sr * o2r - si * o2i, sr * o2i + si * o2r

    z = yield from forward(leaving, half, tables)

    def residual(at):
        zr, zi = z(at)
        factor = measured[pl.ds(at, STEP), :] * lax.rsqrt(zr * zr + zi * zi + 1.0) - RATE
        return zr * factor, zi * factor

    g = yield from inverse(residual, half, tables)

    def back(at):
        (gr, gi), (sr, si), (o2r, o2i) = g(at), held[at], windows(2, at)
        accumulate(gradient, 2, *spot, width, at, sr * gr + si * gi)
        accumulate(gradient, 3, *spot, width, at, sr * gi - si * gr)
        return o2r * gr + o2i * gi, o2r * gi - o2i * gr

    u = yield from forward(back, half, tables)

    def returned(at):
        (kr, kim), (ur, ui) = fixed(spectrum, at), u(at)
        return kr * ur + kim * ui, kr * ui - kim * ur

    w = yield from inverse(returned, half, tables)
    for at in steps(width):
        (pr, pim), (wr, wi) = fixed(probe, at), w(at)
        accumulate(gradient, 0, *spot, width, at, pr * wr + pim * wi)
        accumulate(gradient, 1, *spot, width, at, pr * wi - pim * wr)


def rows_of(row, tile):
    outer = pl.multiple_of(row * (tile + HALO), HALO)
    inner = pl.multiple_of((1 - row) * (tile + HALO), HALO)
    return outer, inner


def write_columns(padded, ze, zo, tile):
    even = here()[1] == 0
    half = tile // 2
    for ch in range(ze.shape[0]):
        for side, at in ((0, 0), (1, padded.shape[1] - 1)):
            strip = jnp.where(even, (zo, ze)[side][ch], (ze, zo)[side][ch])
            turned = pltpu.roll(strip, HALO, 1)
            first, second = (turned, strip) if side == 0 else (strip, turned)
            padded[ch, at, HALO : HALO + half] = first
            padded[ch, at, HALO + half : HALO + tile] = second


def write_rows(padded, ke, ko, re, ro, tile):
    row, col = here()
    even = col == 0
    outer, inner = rows_of(row, tile)
    for ch in range(ke.shape[0]):
        for side, at in ((0, 0), (1, padded.shape[1] - 1)):
            corner = jnp.where(even, (ko, ke)[side][ch], (ke, ko)[side][ch])
            turned = pltpu.roll(corner, HALO, 1)
            near, far = (turned, corner) if side == 0 else (corner, turned)
            padded[ch, at, pl.ds(inner, HALO)] = near
            padded[ch, at, pl.ds(outer, HALO)] = far
        for k in range(tile // LANES):
            lanes = slice(k * LANES, (k + 1) * LANES)
            padded[ch, k + 1, pl.ds(inner, HALO)] = re[ch, :, lanes]
            padded[ch, k + 1, pl.ds(outer, HALO)] = ro[ch, :, lanes]


def harvest(gradient, ze, zo, re, ro, co):
    tile = ro.shape[2]
    tiles = tile // LANES
    half = ze.shape[1]
    row, col = here()
    even = col == 0
    lane = low_lanes()
    outer, inner = rows_of(row, tile)
    for ch in range(re.shape[0]):
        re[ch, :, tile:], co[ch] = (
            jnp.where(
                lane, gradient[ch, tiles + 1, pl.ds(rows, HALO)], gradient[ch, 0, pl.ds(rows, HALO)]
            )
            for rows in (inner, outer)
        )
        left, right = (
            fold_pair(
                gradient[ch, at, HALO : HALO + half],
                gradient[ch, at, HALO + half : HALO + tile],
                at > 0,
            )
            for at in (0, tiles + 1)
        )
        ze[ch] = jnp.where(even, right, left)
        zo[ch] = jnp.where(even, left, right)
        for k in range(tiles):
            lanes = slice(k * LANES, (k + 1) * LANES)
            re[ch, :, lanes] = gradient[ch, k + 1, pl.ds(inner, HALO)]
            ro[ch, :, lanes] = gradient[ch, k + 1, pl.ds(outer, HALO)]


def sort_positions(offsets, order, inside):
    count = offsets.shape[1]
    needs = [(offsets[0, i] >= 0) & (offsets[0, i] <= inside) for i in range(count)]
    at = jnp.int32(0)
    for i in range(count):
        order[at] = i
        at += needs[i].astype(jnp.int32)
    first = at
    for i in range(count):
        order[at] = i
        at += 1 - needs[i].astype(jnp.int32)
    return first


def run_groups(begin, end, offsets, order, padded, probes, spectrum, measured, tables, gradient):
    group = group_of(offsets.shape[1])

    def one(g, carry):
        chains = []
        for k in range(group):
            which = order[g * group + k]
            chains.append(
                chain(
                    place_of(offsets, which),
                    padded,
                    probes.at[which],
                    spectrum,
                    measured.at[which],
                    tables,
                    gradient,
                )
            )
        for _ in itertools.zip_longest(*chains):
            pass
        return carry

    lax.fori_loop(begin, end, one, 0)


def prepare_body(
    offsets, padded_in, objects, probe_in, kernel, measured, tables_in,
    padded, gradient, probes, tables, spectrum, amplitudes, probe, held, patterns, stage, sems,
):
    tile = gradient.shape[2] - 2 * HALO - ROWS
    tiles = gradient.shape[1] - 2
    loads = [
        pltpu.make_async_copy(source, target, sems.at[n])
        for n, (source, target) in enumerate(
            ((tables_in, tables), (kernel, held), (probe_in, probe), (measured, patterns))
        )
    ]
    rows = pl.ds(HALO, tile)
    copies = [
        pltpu.make_async_copy(
            padded.at[:, k + 1, rows, :], gradient.at[:, k + 1, rows, :], sems.at[len(loads) + k]
        )
        for k in (0, tiles - 1)
    ] + [
        pltpu.make_async_copy(
            objects.at[:, :, pl.ds(k * LANES, LANES)],
            target.at[:, k + 1, rows, :],
            sems.at[len(loads) + k + n * tiles],
        )
        for n, target in enumerate((gradient, padded))
        for k in range(1, tiles - 1)
    ]
    for copy in loads + copies:
        copy.start()
    bottom = gradient.shape[2] - HALO - tile
    for ch in range(gradient.shape[0]):
        for at in (0, tiles + 1):
            gradient[ch, at] = jnp.zeros(gradient.shape[2:], jnp.float32)
        for k in range(tiles):
            gradient[ch, k + 1, :HALO] = jnp.zeros((HALO, LANES), jnp.float32)
            gradient[ch, k + 1, HALO + tile :] = jnp.zeros((bottom, LANES), jnp.float32)
    for copy in loads[:3]:
        copy.wait()
    for part in range(2):
        spectrum[part] = reorder(held[part], tables[4], stage.at[part])
    for which in range(patterns.shape[0]):
        _, _, down, right = place_of(offsets, which)
        for part in range(2):
            probes[which, part] = rolled(probe[part], down, right)
    loads[3].wait()
    for which in range(patterns.shape[0]):
        amplitudes[which] = reorder(patterns[which], tables[5], stage.at[which % 2])
    for copy in copies:
        copy.wait()


def early_body(
    offsets, padded_in, gradient_in, ze, zo, probes, spectrum, amplitudes, tables,
    padded, gradient, order,
):
    tile, width = 2 * ze.shape[1], probes.shape[2]
    first = sort_positions(offsets, order, tile - width)
    write_columns(padded, ze, zo, tile)
    run_groups(
        0, first // group_of(offsets.shape[1]), offsets, order,
        padded, probes, spectrum, amplitudes, tables, gradient,
    )


def late_body(
    offsets, padded_in, gradient_in, ke, ko, re, ro, probes, spectrum, amplitudes, tables,
    padded, gradient, gze, gzo, gre, gro, gco, order,
):
    tile, width = ro.shape[2], probes.shape[2]
    first = sort_positions(offsets, order, tile - width)
    write_rows(padded, ke, ko, re, ro, tile)
    group = group_of(offsets.shape[1])
    run_groups(
        first // group, offsets.shape[1] // group, offsets, order,
        padded, probes, spectrum, amplitudes, tables, gradient,
    )
    harvest(gradient, gze, gzo, gre, gro, gco)


def group_of(count):
    return next(k for k in GROUPS if count % k == 0)


def cost(positions, width):
    return pl.CostEstimate(
        flops=positions * 6 * 8 * width**3, bytes_accessed=positions * 4 * width * width, transcendentals=0
    )


def prepare(offsets, padded, objects, probe, kernel, measured, tables):
    width = probe.shape[1]
    far = pl.BlockSpec(memory_space=pltpu.HBM)
    return pl.pallas_call(
        prepare_body,
        out_shape=[
            floats(*padded.shape),
            floats(*padded.shape),
            floats(measured.shape[0], *probe.shape),
            jax.ShapeDtypeStruct(tables.shape, tables.dtype),
            floats(*kernel.shape),
            floats(*measured.shape),
        ],
        in_specs=[SCALARS, WHOLE] + [far] * 5,
        out_specs=[WHOLE] * 6,
        input_output_aliases={1: 0},
        scratch_shapes=[
            pltpu.VMEM(probe.shape, jnp.float32),
            pltpu.VMEM(kernel.shape, jnp.float32),
            pltpu.VMEM(measured.shape, jnp.float32),
            pltpu.VMEM((2, 2, width, LANES), jnp.float32),
            pltpu.SemaphoreType.DMA((4 + 2 * (padded.shape[1] - 2),)),
        ],
        compiler_params=pltpu.CompilerParams(vmem_limit_bytes=VMEM),
        cost_estimate=cost(2, width),
        name="prepare",
    )(offsets, padded, objects, probe, kernel, measured, tables)


def early(offsets, padded, gradient, ze, zo, fixed):
    count, width = fixed[2].shape[:2]
    return pl.pallas_call(
        early_body,
        out_shape=[floats(*padded.shape), floats(*gradient.shape)],
        in_specs=[SCALARS] + [WHOLE] * 8,
        out_specs=[WHOLE] * 2,
        scratch_shapes=[pltpu.SMEM((count + 1,), jnp.int32)],
        input_output_aliases={1: 0, 2: 1},
        compiler_params=pltpu.CompilerParams(vmem_limit_bytes=VMEM),
        cost_estimate=cost(3, width),
        name="early",
    )(offsets, padded, gradient, ze, zo, *fixed)


def late(offsets, padded, gradient, sides, fixed):
    count, width = fixed[2].shape[:2]
    channels, half = sides[2].shape[0], sides[2].shape[2] // 2
    strip, rows = floats(channels, half, LANES), floats(channels, HALO, 2 * half)
    wide, corner = floats(channels, HALO, 2 * half + LANES), floats(channels, HALO, LANES)
    return pl.pallas_call(
        late_body,
        out_shape=[
            floats(*padded.shape), floats(*gradient.shape), strip, strip, wide, rows, corner
        ],
        in_specs=[SCALARS] + [WHOLE] * 10,
        out_specs=[WHOLE] * 7,
        scratch_shapes=[pltpu.SMEM((count + 1,), jnp.int32)],
        input_output_aliases={1: 0, 2: 1},
        compiler_params=pltpu.CompilerParams(vmem_limit_bytes=VMEM),
        cost_estimate=cost(count, width),
        name="late",
    )(offsets, padded, gradient, *sides, *fixed)


def tile_copy(gradient, out, sems, k):
    tile = out.shape[2]
    return pltpu.make_async_copy(
        gradient.at[:, k + 1, pl.ds(HALO, tile), :],
        out.at[:, :, pl.ds(k * LANES, LANES)],
        sems.at[k],
    )


def inside_body(gradient_in, re, ro, gradient, out, sems):
    tile = ro.shape[2]
    row = here()[0]
    outer = pl.multiple_of(HALO + row * (tile - HALO), HALO)
    inner = pl.multiple_of(HALO + (1 - row) * (tile - HALO), HALO)
    tiles = tile // LANES
    for k in [*range(1, tiles - 1), 0, tiles - 1]:
        lanes = slice(k * LANES, (k + 1) * LANES)
        for ch in range(ro.shape[0]):
            gradient[ch, k + 1, pl.ds(inner, HALO)] += re[ch, :, lanes]
            gradient[ch, k + 1, pl.ds(outer, HALO)] += ro[ch, :, lanes]
        if 0 < k < tiles - 1:
            tile_copy(gradient, out, sems, k).start()
    for k in range(1, tiles - 1):
        tile_copy(gradient, out, sems, k).wait()


def border_body(gradient_in, out_in, ze, zo, gradient, out, sems):
    tile = out.shape[2]
    tiles = tile // LANES
    half = ze.shape[1]
    even = here()[1] == 0
    lane = low_lanes()
    for side, k in enumerate((0, tiles - 1)):
        mask = lane if side == 0 else jnp.logical_not(lane)
        for ch in range(ze.shape[0]):
            strip = jnp.where(even, (zo, ze)[side][ch], (ze, zo)[side][ch])
            turned = pltpu.roll(strip, HALO, 1)
            first, second = (strip, turned) if side == 0 else (turned, strip)
            gradient[ch, k + 1, HALO : HALO + half] += jnp.where(mask, first, 0.0)
            gradient[ch, k + 1, HALO + half : HALO + tile] += jnp.where(mask, second, 0.0)
        tile_copy(gradient, out, sems, k).start()
    for k in (0, tiles - 1):
        tile_copy(gradient, out, sems, k).wait()


def settle(gradient, ze, zo, re, ro, tile):
    channels = gradient.shape[0]
    far = pl.BlockSpec(memory_space=pltpu.HBM)
    shapes = [floats(*gradient.shape), floats(channels, tile, tile)]
    common = dict(
        out_shape=shapes,
        out_specs=[WHOLE, far],
        scratch_shapes=[pltpu.SemaphoreType.DMA((tile // LANES,))],
        compiler_params=pltpu.CompilerParams(vmem_limit_bytes=VMEM),
    )
    gradient, out = pl.pallas_call(
        inside_body,
        in_specs=[WHOLE] * 3,
        input_output_aliases={0: 0},
        name="inside",
        **common,
    )(gradient, re, ro)
    return pl.pallas_call(
        border_body,
        in_specs=[WHOLE, far, WHOLE, WHOLE],
        input_output_aliases={0: 0, 1: 1},
        name="border",
        **common,
    )(gradient, out, ze, zo)[1]


def swap(x, row, col):
    rows, cols = lax.axis_size("row"), lax.axis_size("col")

    def partner(i, kind):
        return i + kind * (1 - 2 * (i % 2))

    pairs = [
        (r * cols + c, partner(r, row) * cols + partner(c, col))
        for r in range(rows)
        for c in range(cols)
        if 0 <= partner(r, row) < rows and 0 <= partner(c, col) < cols
    ]
    return lax.ppermute(x, ("row", "col"), pairs)


def per_device(objects, probe, kernel, measured, offsets):
    tile = objects.shape[1]
    tables = jnp.asarray(make_tables(probe.shape[1]))
    offsets, measured = offsets[0, 0].T, measured[0, 0]
    objects, probe, kernel, measured = (
        pltpu.with_memory_space_constraint(x, pltpu.HBM) for x in (objects, probe, kernel, measured)
    )
    tables = pltpu.with_memory_space_constraint(tables, pltpu.HBM)
    padded, ze, zo, re, ro, co = pack(objects)
    ze, zo, re, co, ro = swap(ze, 0, 1), swap(zo, 0, -1), swap(re, 1, 0), swap(co, -1, 0), swap(ro, -1, 0)
    ke, ko = extend(re, co)
    ke, ko, padded = lax.optimization_barrier((ke, ko, padded))
    sides = (swap(ke, 0, 1), swap(ko, 0, -1), re, ro)
    padded, gradient, *fixed = prepare(offsets, padded, objects, probe, kernel, measured, tables)
    probe, tables, spectrum, amplitudes = fixed
    fixed = (probe, spectrum, amplitudes, tables)
    padded, gradient = early(offsets, padded, gradient, ze, zo, fixed)
    _, gradient, ze, zo, re, ro, co = late(offsets, padded, gradient, sides, fixed)
    re, co, ro = swap(re, 1, 0), swap(co, -1, 0), swap(ro, -1, 0)
    ze, zo = gather(ze, zo, re, co)
    ze, zo = swap(ze, 0, 1), swap(zo, 0, -1)
    return settle(gradient, ze, zo, re, ro, tile)


def solution(mesh):
    return jax.shard_map(
        per_device,
        mesh=mesh,
        in_specs=(
            P(None, "row", "col"),
            P(),
            P(),
            P("row", "col", None, None, None),
            P("row", "col", None, None),
        ),
        out_specs=P(None, "row", "col"),
        check_vma=False,
    )
```
